32 devices in a mesh: layer: 4 (over z), dp: 8 (over y, x, core).
Axes of the slice: x: 2, y: 2, z: 4, core: 2. Of those that a mesh axis runs over, the one named last changes fastest.
Arguments:
- pixels: bfloat16 [8, 20, 196, 768], P('dp', 'layer')
- teacher: bfloat16 [4, 8, 20, 196, 768], P('layer', 'dp'), may hold values from -6 to 6
- masked_at: int32 [8, 20, 196], P('dp', 'layer'), may hold values from 0 to 195, each once within a row
- mask_count: int32 [8, 20], P('dp', 'layer'), may hold values from 39 to 136, as said below
- wide_master: float32 [768, 7680], P('dp'), may hold values from -0.21875 to 0.21875
- wide_first: float32 [768, 7680], P('dp'), may hold values from -2.670288e-05 to 2.670288e-05
- wide_second: float32 [768, 7680], P('dp'), may hold values from 2.9681848e-13 to 1.1872739e-12
- tall_master: float32 [3287, 768], P(None, 'dp')
- tall_first: float32 [3287, 768], P(None, 'dp'), may hold values from -2.670288e-05 to 2.670288e-05
- tall_second: float32 [3287, 768], P(None, 'dp'), may hold values from 2.9681848e-13 to 1.1872739e-12
Outputs:
- loss_sum: float32 [], replicated
- mask_total: float32 [], replicated
- grad_norm: float32 [], replicated
- wide_new: float32 [768, 7680], P('dp')
- wide_first_new: float32 [768, 7680], P('dp')
- wide_second_new: float32 [768, 7680], P('dp')
- wide_copy: bfloat16 [768, 7680], P('dp')
- tall_new: float32 [3287, 768], P(None, 'dp')
- tall_first_new: float32 [3287, 768], P(None, 'dp')
- tall_second_new: float32 [3287, 768], P(None, 'dp')
- tall_copy: bfloat16 [3287, 768], P(None, 'dp')
- query_gradient: float32 [768], P('dp')
The draws below stay inside these ranges and needn't reach their ends.
Inputs may be any that keep to these rules, and one draw needn't show every extreme that they name: `masked_at`: each image's row is an order of its 196 patches, the first mask_count of them masked. `mask_count`: the number of masked patches of each image; at most 136, reached in every draw.
All inputs are finite; a program needn't handle non-finite values.
Results may differ from the reference program's by a relative error of at most 0.017.
The reference program's roundings to bfloat16 on the way count: a program that leaves them out, or rounds other values in their place, can miss the bound.
Values may be sent and summed in bfloat16 or wider, within the bound.
No kernel may reach another device: no remote copies, remote signals or barrier semaphores. Data moves between devices by JAX's collectives and lax.ppermute only.
A program may use at most 256 MiB of HBM per device.

```python
import math
import jax
import jax.numpy as jnp
from jax import lax

D = 768
HEADS = 12
HD = 64
FF = 3072
PIX = 768
P_SIZE = 196
IMG_DEV = 5
STEP = 10
NV = 19
WCOLS = 7680
TROWS = 3287
IMAGES_GRP = 20
N_LAYER = 4
N_DP = 8


def draw_pixels(key, part):
    key = jax.random.fold_in(key, 1)
    feature = jnp.arange(PIX, dtype=jnp.float32) / (PIX - 1)
    shape = (N_DP, IMAGES_GRP, P_SIZE, PIX)
    values = jax.random.normal(key, shape, jnp.float32) * (1.0 + 2.0 * feature)
    return values.astype(jnp.bfloat16)


def draw_mask_count(key, part):
    key = jax.random.fold_in(key, 2)
    shape = (N_DP, IMAGES_GRP)
    dp_index = lax.broadcasted_iota(jnp.int32, shape, 0)
    layer_index = lax.broadcasted_iota(jnp.int32, shape, 1) // IMG_DEV
    layer_total = IMAGES_GRP // IMG_DEV
    span = 2 * (N_DP - 1) * (layer_total - 1)
    rising = 2 * P_SIZE // 5 * (dp_index * (layer_total - 1) + layer_index * (N_DP - 1)) // span
    noise = jax.random.randint(key, shape, 0, P_SIZE // 10 + 1)
    noise = noise.at[0, 0].set(0).at[N_DP - 1, IMAGES_GRP - 1].set(P_SIZE // 10)
    return P_SIZE // 5 + rising + noise


def draw_tall_master(key, part):
    key = jax.random.fold_in(key, 3)
    key_down, key_position, key_gain, key_vector = jax.random.split(key, 4)
    column = jnp.arange(D, dtype=jnp.float32) / (D - 1)
    down_part = jax.random.normal(key_down, (FF, D), jnp.float32)
    position_part = jax.random.normal(key_position, (P_SIZE, D), jnp.float32)
    vector_part = jax.random.normal(key_vector, (NV, D), jnp.float32)
    rising = 1.0 + 2.0 * column
    gain_rows = rising * jax.random.uniform(key_gain, (D,), jnp.float32, 0.8, 1.2)
    row_scale = jnp.concatenate([jnp.array([1.0, 0.2, 0.5, 0.5, 0.2, 1.0, 1.0, 0.2, 0.2, 1.0, 1.0, 0.2, 0.3, 0.2, 1.0], jnp.float32), jnp.full((NV - 15,), 0.5, jnp.float32)])
    is_gain = jnp.zeros((NV,), jnp.float32).at[jnp.array([0, 5, 6, 9, 10])].set(1.0)
    vectors = is_gain[:, None] * gain_rows + (1.0 - is_gain[:, None]) * vector_part * row_scale[:, None]
    return jnp.concatenate([down_part * FF ** (-0.5), position_part * 0.5, vectors], axis=0)


def block_levels(own_key, dims, cuts, smallest, top_value):
    level, own = 1.0, jax.random.fold_in(own_key, 6)
    for dim, shards_of in cuts:
        heights = jnp.exp(jax.random.uniform(jax.random.fold_in(own, dim), (shards_of,), jnp.float32, smallest / len(cuts), top_value / len(cuts)))
        level = level * jnp.repeat(heights, dims[dim] // shards_of).reshape([-1 if axis == dim else 1 for axis in range(len(dims))])
    return level


def normal_values(rng, extent, width, most, shards=(), held_as=jnp.bfloat16):
    entries = jax.random.normal(rng, extent, jnp.float32) * width
    if len(shards) > 0:
        entries = block_levels(rng, extent, shards, -0.22, 0.18) * entries
    return jnp.clip(entries, min=-most, max=most).astype(held_as)


def setup_inputs(seed: int = 0) -> dict:
    arg_keys = jax.random.split(jax.random.key(seed), 11)
    return {
        "pixels": draw_pixels(jax.random.fold_in(arg_keys[10], 71), 0),
        "teacher": normal_values(arg_keys[1], (N_LAYER, N_DP, IMAGES_GRP, P_SIZE, D), 1.0, 6.0, ((0, 4), (1, 8))),
        "masked_at": jax.vmap(lambda own: jax.random.permutation(own, P_SIZE))(jax.random.split(arg_keys[2], N_DP * IMAGES_GRP)).reshape((N_DP, IMAGES_GRP, P_SIZE)).astype(jnp.int32),
        "mask_count": draw_mask_count(jax.random.fold_in(arg_keys[10], 71), 0),
        "wide_master": normal_values(arg_keys[4], (D, WCOLS), D ** -0.5, 0.21875, ((0, 8),), jnp.float32),
        "wide_first": normal_values(arg_keys[5], (D, WCOLS), (0.0055 / (D * WCOLS + TROWS * D) ** 0.5), 2.6702880859375e-05, ((0, 8),), jnp.float32),
        "wide_second": jnp.clip(jnp.exp(math.log(1.1872739119969666e-12) - 1.3862944 * jax.random.uniform(arg_keys[6], (D, WCOLS), jnp.float32) ** block_levels(arg_keys[6], (D, WCOLS), ((0, 8),), -0.2, 0.2)), 2.9681847799924166e-13, 1.1872739119969666e-12),
        "tall_master": draw_tall_master(jax.random.fold_in(arg_keys[10], 71), 0),
        "tall_first": normal_values(arg_keys[8], (TROWS, D), (0.0055 / (D * WCOLS + TROWS * D) ** 0.5), 2.6702880859375e-05, ((1, 8),), jnp.float32),
        "tall_second": jnp.clip(jnp.exp(math.log(1.1872739119969666e-12) - 1.3862944 * jax.random.uniform(arg_keys[9], (TROWS, D), jnp.float32) ** block_levels(arg_keys[9], (TROWS, D), ((1, 8),), -0.2, 0.2)), 2.9681847799924166e-13, 1.1872739119969666e-12),
    }


@jax.custom_vjp
def low(v):
    return lax.optimization_barrier(v.astype(jnp.bfloat16)).astype(jnp.float32)

@jax.custom_vjp
def low_back(v):
    return v

def low_keep(v):
    return (low(v), None)

def low_pass(kept, grad):
    return (grad,)

def back_keep(v):
    return (v, None)

def back_low(kept, grad):
    return (low(grad),)
low.defvjp(low_keep, low_pass)
low_back.defvjp(back_keep, back_low)
HUBER_BETA = 2.0
CLIP_NORM = 0.05
LEARN_RATE = 0.08
FIRST_DECAY = 0.9
SECOND_DECAY = 0.999
WEIGHT_DECAY = 0.05
ADAM_EPSILON = 1e-08
NORM_EPSILON = 1e-06
INSTANCE_EPSILON = 1e-05

def exact_dot(left, right):
    return jnp.dot(left, right, precision=lax.Precision.HIGHEST, preferred_element_type=jnp.float32)

def norm_rows(values, gain, shift):
    centered = values - lax.optimization_barrier(jnp.mean(values, axis=-1, keepdims=True))
    inv_std = lax.rsqrt(lax.optimization_barrier(jnp.mean(centered * centered, axis=-1, keepdims=True)) + NORM_EPSILON)
    return centered * inv_std * gain + shift

def split_weights(wide, tall):
    return (wide[:, :D], wide[:, D:4 * D], wide[:, 4 * D:5 * D], wide[:, 5 * D:5 * D + FF], wide[:, 5 * D + FF:], tall[:FF], tall[FF:FF + P_SIZE], tall[FF + P_SIZE:])

def mask_flags(masked_at, mask_count):
    slot_index = lax.broadcasted_iota(jnp.int32, masked_at.shape, masked_at.ndim - 1)
    chosen = (slot_index < mask_count[..., None]).astype(jnp.float32)
    patch_index = lax.broadcasted_iota(jnp.int32, (P_SIZE,), 0)
    matched = (masked_at[..., None] == patch_index).astype(jnp.float32)
    return lax.optimization_barrier(jnp.sum(chosen[..., None] * matched, axis=-2))

def targets_of(teacher):

    def one_group(block_in):
        values = block_in.astype(jnp.float32)
        centered = values - lax.optimization_barrier(jnp.mean(values, axis=-2, keepdims=True))
        normed = centered * lax.rsqrt(lax.optimization_barrier(jnp.mean(centered * centered, axis=-2, keepdims=True)) + INSTANCE_EPSILON)
        rounded = lax.optimization_barrier(normed.astype(jnp.bfloat16)).astype(jnp.float32)
        return lax.optimization_barrier(jnp.sum(rounded, axis=0)) / N_LAYER
    return lax.map(one_group, jnp.moveaxis(teacher, 1, 0))

def forward(wide, tall, pixel_block, flag_block, target_block):
    embed_w, qkv_w, out_w, up_w, head_w, down_w, position, vectors = split_weights(wide, tall)
    images = pixel_block.shape[0]
    flag_rows = flag_block.reshape(-1, 1)
    embedded = low_back(exact_dot(pixel_block.reshape(-1, PIX), embed_w)) + vectors[13]
    start = flag_rows * vectors[14] + (1.0 - flag_rows) * embedded
    start = (start.reshape(images, P_SIZE, D) + position).reshape(-1, D)
    normed_in = low(norm_rows(start, vectors[0], vectors[1]))
    bias_full = jnp.concatenate([vectors[2], jnp.zeros_like(vectors[2]), vectors[3]])
    projected = low(low_back(exact_dot(normed_in, qkv_w) + bias_full)).reshape(images, P_SIZE, 3, HEADS, HD)
    queries, key_rows, value_rows = (projected[:, :, 0], projected[:, :, 1], projected[:, :, 2])
    scores = low_back(jnp.einsum('iphd,iqhd->ihpq', queries, key_rows, precision=lax.Precision.HIGHEST) * (1.0 / math.sqrt(HD)))
    probs = low(jax.nn.softmax(scores, axis=-1))
    heads_out = low(low_back(jnp.einsum('ihpq,iqhd->iphd', probs, value_rows, precision=lax.Precision.HIGHEST))).reshape(-1, D)
    hidden_in = start + vectors[5] * (low_back(exact_dot(heads_out, out_w)) + vectors[4])
    normed_mid = low(norm_rows(hidden_in, vectors[6], vectors[7]))
    pre_act = low_back(exact_dot(normed_mid, up_w)) + vectors[15:].reshape(FF)
    activated = low(jax.nn.gelu(pre_act, approximate=False))
    block_out = hidden_in + vectors[9] * (low_back(exact_dot(activated, down_w)) + vectors[8])
    normed_out = low(norm_rows(block_out, vectors[10], vectors[11]))
    predicted = low_back(exact_dot(normed_out, head_w)) + vectors[12]
    error = predicted - target_block.reshape(-1, D)
    magnitude = jnp.abs(error)
    per_entry = jnp.where(magnitude < HUBER_BETA, 0.5 * error * error / HUBER_BETA, magnitude - 0.5 * HUBER_BETA)
    return jnp.sum(per_entry * flag_rows)

def adam_update(master, first, second, grad, decay):
    first_new = FIRST_DECAY * first + (1.0 - FIRST_DECAY) * grad
    second_new = SECOND_DECAY * second + (1.0 - SECOND_DECAY) * grad * grad
    first_hat = first_new / (1.0 - FIRST_DECAY ** STEP)
    second_hat = second_new / (1.0 - SECOND_DECAY ** STEP)
    master_new = master - LEARN_RATE * (first_hat / (jnp.sqrt(second_hat) + ADAM_EPSILON) + WEIGHT_DECAY * decay * master)
    return (master_new, first_new, second_new)

def reference(pixels, teacher, masked_at, mask_count, wide_master, wide_first, wide_second, tall_master, tall_first, tall_second):
    blocks = N_DP * N_LAYER
    pixel_blocks = pixels.astype(jnp.float32).reshape(blocks, IMG_DEV, P_SIZE, PIX)
    flag_blocks = mask_flags(masked_at, mask_count).reshape(blocks, IMG_DEV, P_SIZE)
    target_blocks = targets_of(teacher).reshape(blocks, IMG_DEV, P_SIZE, D)

    def total(wide, tall):
        wide_low, tall_low = (low(wide), low(tall))

        def one_block(item_args):
            return jax.checkpoint(forward)(wide_low, tall_low, item_args[0], item_args[1], item_args[2])
        return jnp.sum(lax.map(one_block, (pixel_blocks, flag_blocks, target_blocks)))
    loss_sum, back_fn = jax.vjp(total, wide_master, tall_master)
    mask_total = jnp.sum(mask_count.astype(jnp.float32))
    wide_grad, tall_grad = back_fn(jnp.float32(1.0) / mask_total)
    grad_norm = jnp.sqrt(jnp.sum(wide_grad * wide_grad) + jnp.sum(tall_grad * tall_grad))
    factor = CLIP_NORM / jnp.maximum(grad_norm, CLIP_NORM)
    wide_new, wide_first_new, wide_second_new = adam_update(wide_master, wide_first, wide_second, factor * wide_grad, 1.0)
    tall_decay = (lax.broadcasted_iota(jnp.int32, (TROWS, 1), 0) < FF).astype(jnp.float32)
    tall_new, tall_first_new, tall_second_new = adam_update(tall_master, tall_first, tall_second, factor * tall_grad, tall_decay)
    query_gradient = factor * tall_grad[FF + P_SIZE + 2]
    return (loss_sum, mask_total, grad_norm, wide_new, wide_first_new, wide_second_new, wide_new.astype(jnp.bfloat16), tall_new, tall_first_new, tall_second_new, tall_new.astype(jnp.bfloat16), query_gradient)
```

```python
import functools
import math

import jax
import jax.numpy as jnp
from jax import lax
from jax.experimental import pallas as pl
from jax.experimental.pallas import tpu as pltpu
from jax.sharding import PartitionSpec as P

D = 768
HEADS = 12
HD = 64
FF = 3072
PIX = 768
P_SIZE = 196
STEP = 10
VECS = 19
MOST = 144
TAIL = 256

HUBER_BETA = 2.0
CLIP_NORM = 0.05
LEARN_RATE = 0.08
FIRST_DECAY = 0.9
SECOND_DECAY = 0.999
WEIGHT_DECAY = 0.05
ADAM_EPSILON = 1e-08
NORM_EPSILON = 1e-06
INSTANCE_EPSILON = 1e-05
LOW = jnp.bfloat16
F32 = jnp.float32


def flip(size, bit):
    return [(i, i ^ bit) for i in range(size)]


def swap(value, axis, bit):
    return lax.ppermute(value, axis, flip(lax.axis_size(axis), bit))


def gather_part(shard, by_x):
    if lax.axis_size("dp") != 8:
        return [lax.all_gather(shard, "dp", axis=0, tiled=True)]
    from_x, from_y = swap(shard, "dp", 2), swap(shard, "dp", 4)
    diagonal = swap(from_x, "dp", 4) if by_x else swap(from_y, "dp", 2)
    pieces = []
    for piece in (shard, from_x, from_y, diagonal):
        pieces += [piece, swap(piece, "dp", 1)]
    return pieces


def arrived(pieces):
    return [pieces[2], pieces[4]] if len(pieces) > 1 else []


class Owned:
    def __init__(self, grads, by_x):
        self.grads, self.by_x, self.steps = grads, by_x, {}
        self.plain = lax.axis_size("dp") != 8

    def step(self, name, make):
        if name not in self.steps:
            self.steps[name] = make()
        return self.steps[name]

    def core(self):
        return [] if self.plain else self.step("core", lambda: [swap(self.grads[1], "dp", 1)])

    def sums(self):
        def make():
            total = self.grads[0].astype(F32) + self.core()[0].astype(F32)
            return total, total[1:].astype(LOW)

        return self.step("sums", make)

    def diagonal(self):
        if self.plain:
            return []
        first, bit = (0, 2) if self.by_x else (1, 4)

        def make():
            low = self.sums()[1]
            return [swap(low[2], "dp", bit), swap(low[first], "dp", bit)]

        return self.step("diagonal", make)

    def chips(self):
        if self.plain:
            return []
        other, bit = (2, 4) if self.by_x else (1, 2)

        def make():
            total = self.sums()[0][other] + self.diagonal()[0].astype(F32)
            return [swap(total.astype(LOW), "dp", bit)]

        return self.step("chips", make)

    def share(self):
        def make():
            if self.plain:
                low = lax.psum_scatter(self.grads[0][0], "dp", scatter_dimension=0, tiled=True)
                return low.astype(F32)
            return self.sums()[0][0] + (self.diagonal()[1].astype(F32) + self.chips()[0].astype(F32))

        return self.step("share", make)

    def inward(self):
        if lax.axis_size("layer") != 4:
            return []
        return self.step("inward", lambda: [lax.ppermute(self.share().astype(LOW), "layer", [(0, 1), (3, 2)])])

    def pair(self):
        return self.step("pair", lambda: (self.share() + self.inward()[0].astype(F32)).astype(LOW))

    def across(self):
        if lax.axis_size("layer") != 4:
            return []
        return self.step("across", lambda: [lax.ppermute(self.pair(), "layer", [(1, 2), (2, 1)])])

    def total(self):
        if lax.axis_size("layer") != 4:
            return lax.psum(self.share().astype(LOW), "layer").astype(F32)
        total = (self.pair().astype(F32) + self.across()[0].astype(F32)).astype(LOW)
        outward = lax.ppermute(total, "layer", [(1, 0), (2, 3)])
        place = lax.axis_index("layer")
        return jnp.where((place == 1) | (place == 2), total, outward).astype(F32)


def gathered_sum(value, axis):
    size = lax.axis_size(axis)
    sent = jnp.broadcast_to(value, (size, *value.shape))
    return jnp.sum(lax.all_to_all(sent, axis, split_axis=0, concat_axis=0), axis=0)
NAT = 208
TILE = 256
CHUNK = 48
VMEM_LIMIT = 20 * 2**20
HEAVY = 2.5e9
ROW = pl.BlockSpec(memory_space=pltpu.VMEM)
FAR = pl.BlockSpec(memory_space=pl.ANY)
NUMBERS = pl.BlockSpec(memory_space=pltpu.SMEM)


def shape(dims, dtype):
    return jax.ShapeDtypeStruct(dims, dtype)


def launch(kernel, us, in_specs, out_specs, out_shape, scratch_shapes=(), grid=(), prefetch=0, after=()):
    def call(*args):
        count = len(args)

        def body(*refs):
            kernel(*refs[:count], *refs[count + len(after) :])

        spec = pltpu.PrefetchScalarGridSpec(
            num_scalar_prefetch=prefetch,
            grid=grid,
            in_specs=list(in_specs) + [FAR] * len(after),
            out_specs=out_specs,
            scratch_shapes=list(scratch_shapes),
        )
        return pl.pallas_call(
            body,
            grid_spec=spec,
            out_shape=out_shape,
            compiler_params=pltpu.CompilerParams(vmem_limit_bytes=VMEM_LIMIT),
            cost_estimate=pl.CostEstimate(flops=int(us * HEAVY), bytes_accessed=1 << 20, transcendentals=0),
        )(*args, *after)

    return call


def dot(left, right):
    return jnp.dot(left, right, preferred_element_type=F32)


def dot_t(left, right):
    return lax.dot_general(left, right, (((1,), (1,)), ((), ())), preferred_element_type=F32)


def t_dot(left, right):
    return lax.dot_general(left, right, (((0,), (0,)), ((), ())), preferred_element_type=F32)


def fetch(order, pieces, weight, sems, columns=None):
    rows = pieces[0].shape[0]
    copies = []
    for index, piece in enumerate(pieces):
        source = piece if columns is None else piece.at[:, columns]
        at = pl.multiple_of(order[index] * rows, 16 if rows % 16 == 0 else 8)
        copies.append(pltpu.make_async_copy(source, weight.at[pl.ds(at, rows)], sems.at[index]))
    for copy in copies:
        copy.start()
    return copies


def wait_all(copies):
    for copy in copies:
        copy.wait()


def one_hot(masked, count, rows):
    patch = lax.broadcasted_iota(jnp.int32, (rows, MOST), 0)
    slot = lax.broadcasted_iota(jnp.int32, (rows, MOST), 1)
    return jnp.where((masked[:, :MOST] == patch) & (slot < count), 1.0, 0.0)


def normed(values):
    centered = values - jnp.mean(values, axis=-1, keepdims=True)
    inv_std = lax.rsqrt(jnp.mean(centered * centered, axis=-1, keepdims=True) + NORM_EPSILON)
    return centered * inv_std, inv_std


def norm_in(grad_in, hat, inv_std, gain):
    scaled = grad_in * gain
    return inv_std * (
        scaled
        - jnp.mean(scaled, axis=-1, keepdims=True)
        - hat * jnp.mean(scaled * hat, axis=-1, keepdims=True)
    )


def wide(column):
    return jnp.broadcast_to(column, (column.shape[0], 128))


def folded(values):
    return jnp.sum(values.reshape(-1, 8, values.shape[-1]), axis=0)


def total_row(values):
    return jnp.sum(values, axis=0, keepdims=True)


def split_store(keep, send, columns, grad):
    rows = keep.shape[1]
    blocks = grad.shape[0] // rows
    low = grad.astype(LOW)
    for index in range(blocks):
        into = keep if index % 2 == 0 else send
        into[index // 2, :, columns] = low[index * rows : (index + 1) * rows]


def split_shapes(blocks, columns):
    if blocks == 1:
        return [shape((1, D, columns), LOW)]
    return [shape((blocks // 2, D // blocks, columns), LOW)] * 2


def teacher_kernel(blocks, images, first, counts, teacher, masked, *refs):
    outs, (held, sems) = refs[:blocks], refs[blocks:]
    copies = [
        pltpu.make_async_copy(teacher.at[pl.ds(first[block] * images, images)], held.at[block], sems.at[block])
        for block in range(blocks)
    ]
    for copy in copies:
        copy.start()
    for block in range(blocks):
        copies[block].wait()
        for index in range(images):
            count = counts[block * images + index]
            pick = one_hot(masked[block * images + index], count, P_SIZE).astype(LOW)
            rows = slice(index * MOST, (index + 1) * MOST)
            for at in range(0, D, TILE):
                low = held[block, index, :, at : at + TILE]
                values = low.astype(F32)
                mean = jnp.sum(values, axis=0, keepdims=True) * (1.0 / P_SIZE)
                centered = values - mean
                square = jnp.sum(centered * centered, axis=0, keepdims=True) * (1.0 / P_SIZE)
                inv = lax.rsqrt(square + INSTANCE_EPSILON)
                outs[block][rows, at : at + TILE] = ((t_dot(pick, low) - mean) * inv).astype(LOW)


def teacher_rows(teacher, masks, first, images, after=()):
    blocks = first.shape[0]
    return launch(
        functools.partial(teacher_kernel, blocks, images),
        2 * blocks,
        in_specs=[NUMBERS, NUMBERS, FAR, ROW],
        out_specs=[ROW] * blocks,
        out_shape=[shape((images * MOST, D), LOW)] * blocks,
        scratch_shapes=[pltpu.VMEM((blocks, images, P_SIZE, D), LOW), pltpu.SemaphoreType.DMA((blocks,))],
        after=after,
    )(first, masks[:, P_SIZE], teacher, masks[:, None, :P_SIZE])


def part_kernel(spans, *refs):
    ins, out = refs[: len(spans)], refs[-1]
    at = 0
    for (source, start, size, *room), ref in zip(spans, ins):
        out[:, at : at + size] = ref[:, start : start + size].astype(LOW)
        at += size
        if room:
            out[:, at : at + room[0] - size] = jnp.zeros((out.shape[0], room[0] - size), LOW)
            at += room[0] - size


def part(spans, after=()):
    rows = spans[0][0].shape[0]
    return launch(
        functools.partial(part_kernel, spans),
        2,
        in_specs=[ROW] * len(spans),
        out_specs=ROW,
        out_shape=shape((rows, sum(span[-1] for span in spans)), LOW),
        after=after,
    )(*[span[0] for span in spans])


def embed_kernel(owners, order, counts, pixels, masked, *refs):
    pieces, refs = refs[:owners], refs[owners:]
    hat, inv, rows_in, position, vectors, hat_tab, inv_tab, tab_in, weight, sems = refs
    step = pl.program_id(0)

    @pl.when(step == 0)
    def _():
        wait_all(fetch(order, pieces, weight, sems, pl.ds(0, D + TAIL)))
        small = weight[:, D:].astype(F32).T
        vectors[...] = small[P_SIZE : P_SIZE + vectors.shape[0]]
        rows = small[:P_SIZE]
        zeros = jnp.zeros((NAT - P_SIZE, D), F32)
        position[...] = jnp.concatenate([rows, zeros], axis=0).astype(LOW)
        table, table_inv = normed(rows + small[P_SIZE + 14 : P_SIZE + 15])
        hat_tab[...] = jnp.concatenate([table, zeros], axis=0)
        inv_tab[...] = jnp.concatenate([wide(table_inv), zeros[:, :128]], axis=0)
        table = table * small[P_SIZE : P_SIZE + 1] + small[P_SIZE + 1 : P_SIZE + 2]
        tab_in[...] = jnp.concatenate([table, zeros], axis=0).astype(LOW)

    flag = jnp.sum(one_hot(masked[0], counts[step], P_SIZE), axis=1, keepdims=True)
    embedded = dot(pixels[0], weight[:, :D]) + vectors[13:14]
    start = flag * vectors[14:15] + (1.0 - flag) * embedded + position[...].astype(F32)[:P_SIZE]
    value, value_inv = normed(start)
    zeros = jnp.zeros((NAT - P_SIZE, D), F32)
    hat[0] = jnp.concatenate([value, zeros], axis=0)
    inv[0] = jnp.concatenate([wide(value_inv), zeros[:, :128]], axis=0)
    value = value * vectors[0:1] + vectors[1:2]
    rows_in[0] = jnp.concatenate([value, zeros], axis=0).astype(LOW)


def embed(order, counts, pixels, masked, pieces, after=()):
    images, owners = pixels.shape[0], len(pieces)
    whole = lambda *dims: pl.BlockSpec(dims, lambda i, order, counts: (0,) * len(dims))
    image = lambda *dims: pl.BlockSpec((1, *dims), lambda i, order, counts: (i,) + (0,) * len(dims))
    return launch(
        functools.partial(embed_kernel, owners),
        6,
        prefetch=2,
        grid=(images,),
        in_specs=[image(P_SIZE, PIX), image(1, P_SIZE)] + [FAR] * owners,
        out_specs=[
            image(NAT, D),
            image(NAT, 128),
            image(NAT, D),
            whole(NAT, D),
            whole(24, D),
            whole(NAT, D),
            whole(NAT, 128),
            whole(NAT, D),
        ],
        scratch_shapes=[pltpu.VMEM((D, D + TAIL), LOW), pltpu.SemaphoreType.DMA((owners,))],
        out_shape=[
            shape((images, NAT, D), F32),
            shape((images, NAT, 128), F32),
            shape((images, NAT, D), LOW),
            shape((NAT, D), LOW),
            shape((24, D), F32),
            shape((NAT, D), F32),
            shape((NAT, 128), F32),
            shape((NAT, D), LOW),
        ],
        after=after,
    )(order, counts, pixels, masked, *pieces)


def halves(pair):
    lane = lax.broadcasted_iota(jnp.int32, (1, 128), 1)
    first = jnp.where(lane < HD, 1.0, 0.0).astype(LOW)
    return jnp.concatenate([pair * first, pair * (1.0 - first.astype(F32)).astype(LOW)], axis=0)


def merged(both):
    lane = lax.broadcasted_iota(jnp.int32, (MOST, 128), 1)
    return jnp.where(lane < HD, both[:MOST], both[MOST:])


def attention_kernel(owners, order, counts, rows_in, masked, tab_in, vectors, *refs):
    pieces, refs = refs[:owners], refs[owners:]
    kv, queries, heads, weight, table, sems = refs
    step = pl.program_id(0)

    @pl.when(step == 0)
    def _():
        wait_all(fetch(order, pieces, weight, sems, pl.ds(D + TAIL, 3 * D)))
        table[...] = (dot(tab_in[...], weight[:, :D]) + vectors[2:3]).astype(LOW)

    kv[0, :, :D] = dot(rows_in[0], weight[:, D : 2 * D]).astype(LOW)
    kv[0, :, D:] = (dot(rows_in[0], weight[:, 2 * D :]) + vectors[3:4]).astype(LOW)
    pick = one_hot(masked[0], counts[step], NAT).astype(LOW)
    queries[0] = t_dot(pick, table[...]).astype(LOW)
    key_index = lax.broadcasted_iota(jnp.int32, (1, NAT), 1)
    for at in range(0, D, 128):
        pair = halves(queries[0, :, at : at + 128])
        scores = dot_t(pair, kv[0, :, at : at + 128]) * (1.0 / math.sqrt(HD))
        scores = jnp.where(key_index < P_SIZE, scores, -1e30)
        shifted = jnp.exp(scores - jnp.max(scores, axis=1, keepdims=True))
        probs = (shifted * (1.0 / jnp.sum(shifted, axis=1, keepdims=True))).astype(LOW)
        heads[0, :, at : at + 128] = merged(dot(probs, kv[0, :, D + at : D + at + 128])).astype(LOW)


def attention(order, counts, rows_in, masked, tab_in, vectors, pieces, after=()):
    images, owners = rows_in.shape[0], len(pieces)
    whole = lambda *dims: pl.BlockSpec(dims, lambda i, order, counts: (0,) * len(dims))
    image = lambda *dims: pl.BlockSpec((1, *dims), lambda i, order, counts: (i,) + (0,) * len(dims))
    return launch(
        functools.partial(attention_kernel, owners),
        12,
        prefetch=2,
        grid=(images,),
        in_specs=[image(NAT, D), image(1, P_SIZE), whole(NAT, D), whole(24, D)] + [FAR] * owners,
        out_specs=[image(NAT, 2 * D), image(MOST, D), image(MOST, D)],
        scratch_shapes=[
            pltpu.VMEM((D, 3 * D), LOW),
            pltpu.VMEM((NAT, D), LOW),
            pltpu.SemaphoreType.DMA((owners,)),
        ],
        out_shape=[shape((images, NAT, 2 * D), LOW), shape((images, MOST, D), LOW), shape((images, MOST, D), LOW)],
        after=after,
    )(order, counts, rows_in, masked, tab_in, vectors, *pieces)


def chunks(count, body):
    lax.fori_loop(0, count, lambda k, _: (body(k), 0)[1], 0)


def at_chunk(k, rows=CHUNK):
    return pl.ds(pl.multiple_of(k * rows, 16), rows)


def gelu_parts(value):
    size = jnp.abs(value) * math.sqrt(0.5)
    t = 1.0 / (1.0 + 0.3275911 * size)
    bell = jnp.exp(-size * size)
    poly = t * (0.254829592 + t * (-0.284496736 + t * (1.421413741 + t * (-1.453152027 + t * 1.061405429))))
    below = 0.5 * poly * bell
    share = jnp.where(value < 0, below, 1.0 - below)
    return value * share, share + value * bell * (1.0 / math.sqrt(2.0 * math.pi))


def up_kernel(owners, images, order, counts, masked, heads, position, vectors, *refs):
    pieces, refs = refs[:owners], refs[owners:]
    attn, hidden, hat, inv, rows_in, active, slope, weight, pre_a, pre_b, sems = refs
    copies = fetch(order, pieces, weight, sems)
    for index in range(images):
        pick = one_hot(masked[index], counts[index], NAT).astype(LOW)
        hidden[index * MOST : (index + 1) * MOST] = t_dot(pick, position[...]) + vectors[14:15]
    wait_all(copies)
    for at in range(0, D, TILE):
        attn[:, at : at + TILE] = dot(heads[...], weight[:, at : at + TILE])

    def first(k):
        rows = at_chunk(k)
        branch = attn[rows] + vectors[4:5]
        attn[rows] = branch
        value = hidden[rows] + vectors[5:6] * branch
        hidden[rows] = value
        value, value_inv = normed(value)
        hat[rows] = value
        inv[rows] = wide(value_inv)
        rows_in[rows] = (value * vectors[6:7] + vectors[7:8]).astype(LOW)

    chunks(hidden.shape[0] // CHUNK, first)

    def product(tile, into):
        into[...] = dot(rows_in[...], weight[:, pl.ds(pl.multiple_of(D + tile * TILE, TILE), TILE)])

    def finish(tile, source):
        columns = pl.ds(pl.multiple_of(tile * TILE, TILE), TILE)
        part = D // TILE
        bias = vectors[pl.ds(15 + tile // part, 1), pl.ds(pl.multiple_of((tile % part) * TILE, TILE), TILE)]
        for start in range(0, source.shape[0], 48):
            value, down = gelu_parts(source[start : start + 48] + bias)
            active[start : start + 48, columns] = value.astype(LOW)
            slope[start : start + 48, columns] = down.astype(LOW)

    tiles = FF // TILE
    product(0, pre_a)

    def pair(k):
        product(2 * k + 1, pre_b)
        finish(2 * k, pre_a)
        product(jnp.minimum(2 * k + 2, tiles - 1), pre_a)
        finish(2 * k + 1, pre_b)

    chunks(tiles // 2, pair)


def up(order, counts, masked, heads, position, vectors, pieces, after=()):
    rows, owners = heads.shape[0], len(pieces)
    return launch(
        functools.partial(up_kernel, owners, masked.shape[0]),
        20,
        in_specs=[NUMBERS, NUMBERS] + [ROW] * 4 + [FAR] * owners,
        out_specs=[ROW] * 7,
        out_shape=[
            shape((rows, D), F32),
            shape((rows, D), F32),
            shape((rows, D), F32),
            shape((rows, 128), F32),
            shape((rows, D), LOW),
            shape((rows, FF), LOW),
            shape((rows, FF), LOW),
        ],
        scratch_shapes=[
            pltpu.VMEM((D, D + FF), LOW),
            pltpu.VMEM((rows, TILE), F32),
            pltpu.VMEM((rows, TILE), F32),
            pltpu.SemaphoreType.DMA((owners,)),
        ],
        after=after,
    )(order, counts, masked, heads, position, vectors, *pieces)


def place(order, source, turned, scratch):
    blocks = order.shape[0]
    if blocks == 1:
        turned[...] = source.T
        return
    rows = D // blocks
    scratch[...] = source.T
    for index in range(blocks):
        at = pl.multiple_of(order[index] * rows, 16 if rows % 16 == 0 else 8)
        turned[index * rows : (index + 1) * rows] = scratch[pl.ds(at, rows)]


def head_kernel(owners, parts, images, order, counts, active, hidden, vectors, *refs):
    targets, pieces, refs = refs[:parts], refs[parts : parts + owners], refs[parts + owners :]
    loss, branch, hat, inv, error_low, sums, rows_in, weight, work, sems = refs
    wait_all(fetch(order, pieces, weight, sems))
    for at in range(0, D, TILE):
        branch[:, at : at + TILE] = dot_t(active[...], weight[at : at + TILE, :FF])

    def first(k):
        rows = at_chunk(k)
        value = branch[rows] + vectors[8:9]
        branch[rows] = value
        value, value_inv = normed(hidden[rows] + vectors[9:10] * value)
        hat[rows] = value
        inv[rows] = wide(value_inv)
        rows_in[rows] = (value * vectors[10:11] + vectors[11:12]).astype(LOW)

    steps = hidden.shape[0] // CHUNK
    chunks(steps, first)
    for at in range(0, D, TILE):
        work[:, at : at + TILE] = dot(rows_in[...], weight[:, FF + at : FF + at + TILE])
    sums[...] = jnp.zeros_like(sums)

    def second(k):
        rows = at_chunk(k)
        target = targets[0][rows].astype(F32)
        for other in targets[1:]:
            target = target + other[rows].astype(F32)
        error = work[rows] + vectors[12:13] - target * (1.0 / lax.axis_size("layer"))
        size = jnp.abs(error)
        entry = jnp.where(size < HUBER_BETA, error * error * (0.5 / HUBER_BETA), size - 0.5 * HUBER_BETA)
        per_image = MOST // CHUNK
        row = lax.broadcasted_iota(jnp.int32, (CHUNK, 1), 0) + lax.rem(k, per_image) * CHUNK
        flag = row < counts[k // per_image]
        sums[0] += folded(jnp.where(flag, entry, 0.0))
        grad = jnp.where(flag, jnp.clip(error * (1.0 / HUBER_BETA), -1.0, 1.0), 0.0)
        sums[1] += folded(grad)
        error_low[rows] = grad.astype(LOW)

    chunks(steps, second)
    loss[0, 0] = jnp.sum(sums[0])


def head(order, counts, active, hidden, vectors, targets, pieces, after=()):
    rows, owners = hidden.shape[0], len(pieces)
    images = counts.shape[0]
    return launch(
        functools.partial(head_kernel, owners, len(targets), images),
        15,
        in_specs=[NUMBERS, NUMBERS] + [ROW] * (3 + len(targets)) + [FAR] * owners,
        out_specs=[NUMBERS] + [ROW] * 6,
        out_shape=[
            shape((1, 1), F32),
            shape((rows, D), F32),
            shape((rows, D), F32),
            shape((rows, 128), F32),
            shape((rows, D), LOW),
            shape((2, 8, D), F32),
            shape((rows, D), LOW),
        ],
        scratch_shapes=[
            pltpu.VMEM((D, FF + D), LOW),
            pltpu.VMEM((rows, D), F32),
            pltpu.SemaphoreType.DMA((owners,)),
        ],
        after=after,
    )(order, counts, active, hidden, vectors, *targets, *pieces)


def down_kernel(owners, order, error_low, hat, inv, branch, active, vectors, rows_in, *refs):
    pieces, refs = refs[:owners], refs[owners:]
    outs = 2 if owners > 1 else 1
    keep, send = refs[0], refs[outs - 1]
    grad, grad_low, sums, weight, turned, spare, sems = refs[outs:]
    wait_all(fetch(order, pieces, weight, sems, pl.ds(FF, D)))
    for at in range(0, D, TILE):
        grad[:, at : at + TILE] = dot_t(error_low[...], weight[at : at + TILE])
    sums[...] = jnp.zeros_like(sums)

    def back(k):
        rows = at_chunk(k)
        grad_in, value = grad[rows], hat[rows]
        sums[0] += folded(grad_in * value)
        sums[1] += folded(grad_in)
        value = norm_in(grad_in, value, inv[rows, :1], vectors[10:11])
        grad[rows] = value
        sums[2] += folded(value * branch[rows])
        value = value * vectors[9:10]
        sums[3] += folded(value)
        grad_low[rows] = value.astype(LOW)

    chunks(grad.shape[0] // CHUNK, back)
    place(order, grad_low[...], turned, spare)

    for at in range(0, FF, TILE):
        columns = slice(at, at + TILE)
        split_store(keep, send, columns, dot(turned[...], active[:, columns]))
    place(order, rows_in[...], turned, spare)
    for at in range(0, D, TILE):
        columns = slice(FF + at, FF + at + TILE)
        split_store(keep, send, columns, dot(turned[...], error_low[:, at : at + TILE]))


def down(order, error_low, hat, inv, branch, active, vectors, rows_in, pieces, after=()):
    rows, owners = hat.shape[0], len(pieces)
    grads = split_shapes(owners, FF + D)
    return launch(
        functools.partial(down_kernel, owners),
        13,
        in_specs=[NUMBERS] + [ROW] * 7 + [FAR] * owners,
        out_specs=[ROW] * (len(grads) + 3),
        out_shape=grads + [shape((rows, D), F32), shape((rows, D), LOW), shape((4, 8, D), F32)],
        scratch_shapes=[
            pltpu.VMEM((D, D), LOW),
            pltpu.VMEM((D, rows), LOW),
            pltpu.VMEM((D, rows), LOW),
            pltpu.SemaphoreType.DMA((owners,)),
        ],
        after=after,
    )(order, error_low, hat, inv, branch, active, vectors, rows_in, *pieces)


def pre_kernel(owners, order, grad_low, slope, rows_in, *refs):
    pieces, refs = refs[:owners], refs[owners:]
    outs = 2 if owners > 1 else 1
    keep, send = refs[0], refs[outs - 1]
    pre_low, bias, weight, turned, spare, sems = refs[outs:]
    copies = fetch(order, pieces, weight, sems, pl.ds(0, FF))
    place(order, rows_in[...], turned, spare)
    wait_all(copies)

    for at in range(0, FF, TILE):
        columns = slice(at, at + TILE)
        value = dot(grad_low[...], weight[:, columns]) * slope[:, columns].astype(F32)
        bias[:, columns] = folded(value)
        pre_low[:, columns] = value.astype(LOW)
        split_store(keep, send, columns, dot(turned[...], pre_low[:, columns]))


def pre(order, grad_low, slope, rows_in, pieces, after=()):
    rows, owners = grad_low.shape[0], len(pieces)
    grads = split_shapes(owners, FF)
    return launch(
        functools.partial(pre_kernel, owners),
        12,
        in_specs=[NUMBERS] + [ROW] * 3 + [FAR] * owners,
        out_specs=[ROW] * (len(grads) + 2),
        out_shape=grads + [shape((rows, FF), LOW), shape((8, FF), F32)],
        scratch_shapes=[
            pltpu.VMEM((D, FF), LOW),
            pltpu.VMEM((D, rows), LOW),
            pltpu.VMEM((D, rows), LOW),
            pltpu.SemaphoreType.DMA((owners,)),
        ],
        after=after,
    )(order, grad_low, slope, rows_in, *pieces)


def out_kernel(owners, images, order, counts, masked, pre_low, grad, hat, inv, attn, vectors, *refs):
    pieces, refs = refs[:owners], refs[owners:]
    heads_grad, table, sums, attn_low, weight, work, high, rest, sems = refs
    wait_all(fetch(order, pieces, weight, sems))
    for at in range(0, D, TILE):
        work[:, at : at + TILE] = dot_t(pre_low[...], weight[at : at + TILE, D:])
    sums[...] = jnp.zeros_like(sums)

    def back(k):
        rows = at_chunk(k)
        grad_in, value = work[rows], hat[rows]
        sums[0] += folded(grad_in * value)
        sums[1] += folded(grad_in)
        value = grad[rows] + norm_in(grad_in, value, inv[rows, :1], vectors[6:7])
        low = value.astype(LOW)
        high[rows] = low
        rest[rows] = (value - low.astype(F32)).astype(LOW)
        sums[2] += folded(value * attn[rows])
        value = value * vectors[5:6]
        sums[3] += folded(value)
        attn_low[rows] = value.astype(LOW)

    chunks(work.shape[0] // CHUNK, back)
    for at in range(0, D, TILE):
        heads_grad[:, at : at + TILE] = dot_t(attn_low[...], weight[at : at + TILE, :D]).astype(LOW)
    for index in range(images):
        pick = one_hot(masked[index], counts[index], NAT).astype(LOW)
        rows = slice(index * MOST, (index + 1) * MOST)
        value = dot(pick, high[rows]) + dot(pick, rest[rows])
        table[...] = value if index == 0 else table[...] + value


def out_back(order, counts, masked, pre_low, grad, hat, inv, attn, vectors, pieces, after=()):
    rows, owners = grad.shape[0], len(pieces)
    return launch(
        functools.partial(out_kernel, owners, masked.shape[0]),
        14,
        in_specs=[NUMBERS, NUMBERS] + [ROW] * 7 + [FAR] * owners,
        out_specs=[ROW] * 4,
        out_shape=[shape((rows, D), LOW), shape((NAT, D), F32), shape((4, 8, D), F32), shape((rows, D), LOW)],
        scratch_shapes=[
            pltpu.VMEM((D, D + FF), LOW),
            pltpu.VMEM((rows, D), F32),
            pltpu.VMEM((rows, D), LOW),
            pltpu.VMEM((rows, D), LOW),
            pltpu.SemaphoreType.DMA((owners,)),
        ],
        after=after,
    )(order, counts, masked, pre_low, grad, hat, inv, attn, vectors, *pieces)


def attention_back_kernel(counts, queries, kv, heads_grad, masked, kv_low, table, sums, query_low):
    step = pl.program_id(0)

    @pl.when(step == 0)
    def _():
        table[...] = jnp.zeros_like(table)
        sums[...] = jnp.zeros_like(sums)

    scale = 1.0 / math.sqrt(HD)
    key_index = lax.broadcasted_iota(jnp.int32, (NAT, 1), 0)
    for at in range(0, D, 128):
        lanes = slice(at, at + 128)
        high = slice(D + at, D + at + 128)
        pair, grad = halves(queries[0, :, lanes]), halves(heads_grad[0, :, lanes])
        keys, values = kv[0, :, lanes], kv[0, :, high]
        scores = jnp.where(key_index < P_SIZE, dot_t(keys, pair) * scale, -1e30)
        shifted = jnp.exp(scores - jnp.max(scores, axis=0, keepdims=True))
        probs = shifted * (1.0 / jnp.sum(shifted, axis=0, keepdims=True))
        prob_grad = dot_t(values, grad)
        value_grad = dot(probs.astype(LOW), grad).astype(LOW)
        kv_low[0, :, high] = value_grad
        sums[1, :, lanes] += folded(value_grad.astype(F32))
        inner = jnp.sum(probs * prob_grad, axis=0, keepdims=True)
        score_grad = (probs * (prob_grad - inner)).astype(LOW)
        kv_low[0, :, lanes] = (dot(score_grad, pair) * scale).astype(LOW)
        query_grad = merged(t_dot(score_grad, keys) * scale).astype(LOW)
        query_low[:, lanes] = query_grad
        sums[0, :, lanes] += folded(query_grad.astype(F32))
    pick = one_hot(masked[0], counts[step], NAT).astype(LOW)
    table[...] += dot(pick, query_low[...])


def attention_back(counts, queries, kv, heads_grad, masked, after=()):
    images = kv.shape[0]
    whole = lambda *dims: pl.BlockSpec(dims, lambda i, counts: (0,) * len(dims))
    image = lambda *dims: pl.BlockSpec((1, *dims), lambda i, counts: (i,) + (0,) * len(dims))
    return launch(
        attention_back_kernel,
        15,
        prefetch=1,
        grid=(images,),
        in_specs=[image(MOST, D), image(NAT, 2 * D), image(MOST, D), image(1, P_SIZE)],
        out_specs=[image(NAT, 2 * D), whole(NAT, D), whole(2, 8, D)],
        scratch_shapes=[pltpu.VMEM((MOST, D), LOW)],
        out_shape=[shape((images, NAT, 2 * D), LOW), shape((NAT, D), F32), shape((2, 8, D), F32)],
        after=after,
    )(counts, queries, kv, heads_grad, masked)


def high_rest(value):
    high = value.astype(LOW)
    return jnp.concatenate([high, (value - high.astype(F32)).astype(LOW)], axis=0)


def qkv_kernel(blocks, order, rows_in, kv_low, tab_in, table, heads, attn_low, *refs):
    outs = 2 if blocks > 1 else 1
    keep, send = refs[0], refs[outs - 1]
    turned, spare, tab_turned, tab_spare, heads_turned, heads_spare = refs[outs:]
    place(order, heads[...], heads_turned, heads_spare)
    for at in range(0, D, TILE):
        columns = slice(3 * D + at, 3 * D + at + TILE)
        split_store(keep, send, columns, dot(heads_turned[...], attn_low[:, at : at + TILE]))
    place(order, tab_in[...], tab_turned, tab_spare)
    both = high_rest(table[...])
    twice = jnp.concatenate([tab_turned[...], tab_turned[...]], axis=1)
    for at in range(0, D, TILE):
        split_store(keep, send, slice(at, at + TILE), dot(twice, both[:, at : at + TILE]))
    place(order, rows_in[...], turned, spare)

    for at in range(0, 2 * D, TILE):
        split_store(keep, send, slice(D + at, D + at + TILE), dot(turned[...], kv_low[:, at : at + TILE]))


def qkv_back(order, rows_in, kv_low, tab_in, table, heads, attn_low, after=()):
    blocks, rows = order.shape[0], rows_in.shape[0]
    grads = split_shapes(blocks, 4 * D)
    return launch(
        functools.partial(qkv_kernel, blocks),
        7,
        in_specs=[NUMBERS] + [ROW] * 6,
        out_specs=[ROW] * len(grads),
        out_shape=grads,
        scratch_shapes=[
            pltpu.VMEM((D, rows), LOW),
            pltpu.VMEM((D, rows), LOW),
            pltpu.VMEM((D, NAT), LOW),
            pltpu.VMEM((D, NAT), LOW),
            pltpu.VMEM((D, heads.shape[0]), LOW),
            pltpu.VMEM((D, heads.shape[0]), LOW),
        ],
        after=after,
    )(order, rows_in, kv_low, tab_in, table, heads, attn_low)


def start_kernel(owners, images, order, counts, masked, pixels, kv_low, table, hidden_tab, hat, inv, hat_tab, inv_tab, vectors, head_sums, down_sums, up_bias, out_sums, qkv_sums, *refs):
    pieces, refs = refs[:owners], refs[owners:]
    outs = 2 if owners > 1 else 1
    keep, send = refs[0], refs[outs - 1]
    weight, work, start_low, small, sums, turned, spare, pixel_rows, small_low, sems = refs[outs:]
    copies = fetch(order, pieces, weight, sems, pl.ds(D + TAIL, 3 * D))
    for index in range(images):
        zeros = jnp.zeros((NAT - P_SIZE, PIX), F32)
        padded = jnp.concatenate([pixels[index].astype(F32), zeros], axis=0)
        pixel_rows[index * NAT : (index + 1) * NAT] = padded.astype(LOW)
    place(order, pixel_rows[...], turned, spare)
    wait_all(copies)
    for at in range(0, D, TILE):
        work[:, at : at + TILE] = dot_t(kv_low[...], weight[at : at + TILE, D:])
    both = high_rest(table[...])
    tab_in = dot_t(both, weight[:, :D])
    tab_in = tab_in[:NAT] + tab_in[NAT:]
    gain = vectors[0:1]
    sums[...] = jnp.zeros_like(sums)
    sums[0] += folded(tab_in * hat_tab[...])
    sums[1] += folded(tab_in)
    tab_grad = norm_in(tab_in, hat_tab[...], inv_tab[:, :1], gain) + hidden_tab[...]
    sums[2] += folded(tab_grad)
    small[:NAT] = tab_grad
    half = NAT // 2
    for index in range(images):
        flags = jnp.sum(one_hot(masked[index], counts[index], NAT), axis=1, keepdims=True)
        for part in range(2):
            rows = slice(index * NAT + part * half, index * NAT + (part + 1) * half)
            flag = flags[part * half : (part + 1) * half]
            grad_in, value = work[rows], hat[rows]
            sums[0] += folded(grad_in * value)
            sums[1] += folded(grad_in)
            value = norm_in(grad_in, value, inv[rows, :1], gain)
            small[part * half : (part + 1) * half] += value
            sums[2] += folded(value * flag)
            value = value * (1.0 - flag)
            sums[3] += folded(value)
            start_low[rows] = value.astype(LOW)
    line = [
        total_row(sums[0]),
        total_row(sums[1]),
        total_row(qkv_sums[0]),
        total_row(qkv_sums[1]),
        total_row(out_sums[3]),
        total_row(out_sums[2]),
        total_row(out_sums[0]),
        total_row(out_sums[1]),
        total_row(down_sums[3]),
        total_row(down_sums[2]),
        total_row(down_sums[0]),
        total_row(down_sums[1]),
        total_row(head_sums[1]),
        total_row(sums[3]),
        total_row(sums[2]),
    ]
    line += [total_row(up_bias[:, at : at + D]) for at in range(0, FF, D)]
    for index, value in enumerate(line):
        small[P_SIZE + index : P_SIZE + index + 1] = value
    small[P_SIZE + len(line) :] = jnp.zeros((TAIL - P_SIZE - len(line), D), F32)
    small_low[...] = small[...].T
    blocks = order.shape[0]
    rows = D // blocks
    for index in range(blocks):
        into = keep if index % 2 == 0 else send
        at = pl.multiple_of(order[index] * rows, 16 if rows % 16 == 0 else 8)
        into[index // 2, :, D:] = small_low[pl.ds(at, rows)].astype(LOW)
    for at in range(0, D, TILE):
        split_store(keep, send, slice(at, at + TILE), dot(turned[...], start_low[:, at : at + TILE]))


def start_back(order, counts, masked, pixels, kv_low, table, hidden_tab, hat, inv, hat_tab, inv_tab, vectors, head_sums, down_sums, up_bias, out_sums, qkv_sums, pieces, after=()):
    rows, owners, images = kv_low.shape[0], len(pieces), masked.shape[0]
    grads = split_shapes(owners, D + TAIL)
    return launch(
        functools.partial(start_kernel, owners, images),
        11,
        in_specs=[NUMBERS, NUMBERS] + [ROW] * 15 + [FAR] * owners,
        out_specs=[ROW] * len(grads),
        out_shape=grads,
        scratch_shapes=[
            pltpu.VMEM((D, 3 * D), LOW),
            pltpu.VMEM((rows, D), F32),
            pltpu.VMEM((rows, D), LOW),
            pltpu.VMEM((TAIL, D), F32),
            pltpu.VMEM((4, 8, D), F32),
            pltpu.VMEM((D, rows), LOW),
            pltpu.VMEM((D, rows), LOW),
            pltpu.VMEM((rows, D), LOW),
            pltpu.VMEM((D, TAIL), F32),
            pltpu.SemaphoreType.DMA((owners,)),
        ],
        after=after,
    )(order, counts, masked, pixels, kv_low, table, hidden_tab, hat, inv, hat_tab, inv_tab, vectors, head_sums, down_sums, up_bias, out_sums, qkv_sums, *pieces)


def adam_update(master, first, second, grad, decay):
    first_new = FIRST_DECAY * first + (1.0 - FIRST_DECAY) * grad
    second_new = SECOND_DECAY * second + (1.0 - SECOND_DECAY) * grad * grad
    first_hat = first_new / (1.0 - FIRST_DECAY**STEP)
    second_hat = second_new / (1.0 - SECOND_DECAY**STEP)
    master_new = master - LEARN_RATE * (
        first_hat / (jnp.sqrt(second_hat) + ADAM_EPSILON) + WEIGHT_DECAY * decay * master
    )
    return (master_new, first_new, second_new)


def targets_of(teacher, masked, counts, after):
    layers, images = lax.axis_size("layer"), masked.shape[0]
    masks = jnp.concatenate([masked, counts[:, None]], axis=1)
    if layers != 4:
        masks = lax.all_gather(masks, "layer", axis=0, tiled=False)
        picked = [
            teacher_rows(teacher, masks[block], jnp.full((1,), block, jnp.int32), images)[0]
            for block in range(layers)
        ]
        return [lax.psum_scatter(jnp.stack(picked), "layer", scatter_dimension=0, tiled=False)], picked[0]
    at = lax.axis_index("layer")
    near = swap(masks, "layer", 1)
    both = swap(jnp.concatenate([masks, near]), "layer", 2)
    (own_rows,) = teacher_rows(teacher, masks, at[None], images, after)
    first = jnp.stack([at ^ 3, at ^ 1])
    far, near = teacher_rows(teacher, jnp.concatenate([both[images:], near]), first, images, [own_rows])
    far, near = swap(far, "layer", 1), swap(near, "layer", 1)
    (third,) = teacher_rows(teacher, both[:images], (at ^ 2)[None], images, [own_rows])
    far = (third.astype(F32) + far.astype(F32)).astype(LOW)
    return [own_rows, near, swap(far, "layer", 2)], third


def body(
    pixels,
    teacher,
    masked_at,
    mask_count,
    wide_master,
    wide_first,
    wide_second,
    tall_master,
    tall_first,
    tall_second,
):
    owners, layers = lax.axis_size("dp"), lax.axis_size("layer")
    counts, masked = mask_count[0], masked_at[0][:, None, :]
    images = counts.shape[0]
    order = lax.axis_index("dp") ^ jnp.arange(8) if owners == 8 else jnp.zeros((1,), jnp.int32)
    tall_low = tall_master.T.astype(LOW)
    wide_embed = part(
        [(wide_master, 0, D), (tall_low, FF, P_SIZE + VECS, TAIL), (wide_master, D, 3 * D)]
    )
    pieces_in = gather_part(wide_embed, True)
    targets, third = targets_of(teacher[0, 0], masked_at[0], counts, [wide_embed])
    wide_up = part([(wide_master, 4 * D, D + FF)], arrived(pieces_in))
    pieces_up = gather_part(wide_up, False)

    hat_nat, inv_nat, in_nat, position, vectors, hat_tab, inv_tab, in_tab = embed(
        order, counts, pixels[0], masked, pieces_in, after=[third, wide_up]
    )
    wide_down = part([(tall_low, 0, FF), (wide_master, 5 * D + FF, D)], [in_tab] + arrived(pieces_up))
    pieces_down = gather_part(wide_down, True)
    kv, queries, heads = attention(order, counts, in_nat, masked, in_tab, vectors, pieces_in, after=[wide_down])
    heads = heads.reshape(images * MOST, D)
    attn, hidden, hat_mid, inv_mid, in_mid, active, slope = up(
        order, counts, masked, heads, position, vectors, pieces_up
    )
    loss, branch, hat_out, inv_out, error_low, head_sums, in_out = head(
        order, counts, active, hidden, vectors, targets, pieces_down
    )
    *down_g, grad, grad_low, down_sums = down(
        order, error_low, hat_out, inv_out, branch, active, vectors, in_out, pieces_down
    )
    down_s = Owned(down_g, False)
    *up_g, pre_low, up_bias = pre(order, grad_low, slope, in_mid, pieces_down)
    up_s = Owned(up_g, True)
    heads_grad, hidden_tab, out_sums, attn_low = out_back(
        order, counts, masked, pre_low, grad, hat_mid, inv_mid, attn, vectors, pieces_up, after=down_s.core()
    )
    kv_low, table, qkv_sums = attention_back(
        counts, queries, kv, heads_grad.reshape(images, MOST, D), masked, after=down_s.diagonal()[:1] + up_s.core()
    )
    flat = lambda value: value.reshape(images * NAT, -1)
    qkv_g = qkv_back(
        order, flat(in_nat), flat(kv_low), in_tab, table, heads, attn_low, after=up_s.diagonal()[:1] + down_s.diagonal()
    )
    qkv_s = Owned(qkv_g, False)
    embed_g = start_back(
        order, counts, masked, pixels[0], flat(kv_low), table, hidden_tab, flat(hat_nat), flat(inv_nat),
        hat_tab, inv_tab, vectors, head_sums, down_sums, up_bias, out_sums, qkv_sums, pieces_in,
        after=up_s.diagonal() + down_s.chips() + [qkv_g[0]],
    )
    embed_s = Owned(embed_g, True)
    down_s, up_s, qkv_s, embed_s = [owned.total() for owned in (down_s, up_s, qkv_s, embed_s)]
    wide_share = jnp.concatenate([embed_s[:, :D], qkv_s, up_s, down_s[:, FF:]], axis=1)
    tall_share = jnp.concatenate([down_s[:, :FF], embed_s[:, D : D + P_SIZE + VECS]], axis=1)
    squares = gathered_sum(jnp.sum(wide_share * wide_share) + jnp.sum(tall_share * tall_share), "dp")
    count = jnp.sum(mask_count.astype(F32))
    loss_sum, mask_total = gathered_sum(gathered_sum(jnp.stack([loss[0, 0], count]), "layer"), "dp")
    per_mask = 1.0 / mask_total
    grad_norm = jnp.sqrt(squares) * per_mask
    factor = CLIP_NORM / jnp.maximum(grad_norm, CLIP_NORM) * per_mask
    wide_new, wide_first_new, wide_second_new = adam_update(
        wide_master, wide_first, wide_second, factor * wide_share, 1.0
    )
    tall_decay = (lax.broadcasted_iota(jnp.int32, (tall_master.shape[0], 1), 0) < FF).astype(F32)
    tall_grad = factor * tall_share.T
    tall_new, tall_first_new, tall_second_new = adam_update(
        tall_master, tall_first, tall_second, tall_grad, tall_decay
    )
    return (
        loss_sum,
        mask_total,
        grad_norm,
        wide_new,
        wide_first_new,
        wide_second_new,
        wide_new.astype(LOW),
        tall_new,
        tall_first_new,
        tall_second_new,
        tall_new.astype(LOW),
        tall_grad[FF + P_SIZE + 2],
    )


def solution(mesh):
    in_specs = (
        P("dp", "layer", None, None),
        P("layer", "dp", None, None, None),
        P("dp", "layer", None),
        P("dp", "layer"),
        P("dp", None),
        P("dp", None),
        P("dp", None),
        P(None, "dp"),
        P(None, "dp"),
        P(None, "dp"),
    )
    out_specs = (
        P(),
        P(),
        P(),
        P("dp", None),
        P("dp", None),
        P("dp", None),
        P("dp", None),
        P(None, "dp"),
        P(None, "dp"),
        P(None, "dp"),
        P(None, "dp"),
        P("dp"),
    )
    return jax.shard_map(body, mesh=mesh, in_specs=in_specs, out_specs=out_specs, check_vma=False)
```

```python
import functools
import math

import jax
import jax.numpy as jnp
from jax import lax
from jax.experimental import pallas as pl
from jax.experimental.pallas import tpu as pltpu
from jax.sharding import PartitionSpec as P

D = 768
HEADS = 12
HD = 64
FF = 3072
PIX = 768
P_SIZE = 196
STEP = 10
VECS = 19
MOST = 144
TAIL = 256

HUBER_BETA = 2.0
CLIP_NORM = 0.05
LEARN_RATE = 0.08
FIRST_DECAY = 0.9
SECOND_DECAY = 0.999
WEIGHT_DECAY = 0.05
ADAM_EPSILON = 1e-08
NORM_EPSILON = 1e-06
INSTANCE_EPSILON = 1e-05
LOW = jnp.bfloat16
F32 = jnp.float32


def flip(size, bit):
    return [(i, i ^ bit) for i in range(size)]


def swap(value, axis, bit):
    return lax.ppermute(value, axis, flip(lax.axis_size(axis), bit))


def over_link(value):
    return lax.ppermute(value, "dp", [(i, i ^ (4 if i & 1 else 2)) for i in range(8)])


def over_other(value):
    return lax.ppermute(value, "dp", [(i, i ^ (2 if i & 1 else 4)) for i in range(8)])


def blocks_of(me):
    link = jnp.where(me & 1 == 1, 4, 2)
    other = 6 - link
    return jnp.stack([me, me ^ 1, me ^ link, me ^ link ^ 1, me ^ 6, me ^ other ^ 1, me ^ other, me ^ 7])


def gather_part(shard):
    if lax.axis_size("dp") != 8:
        return [lax.all_gather(shard, "dp", axis=0, tiled=True)]
    twin = swap(shard, "dp", 1)
    first, second = over_link(shard), over_link(twin)
    diagonal = over_other(first)
    return [shard, twin, first, second, diagonal] + [swap(piece, "dp", 1) for piece in (first, second, diagonal)]


def arrived(pieces, *indices):
    return [pieces[index] for index in indices] if len(pieces) > 1 else []


class Owned:
    def __init__(self, grads):
        self.grads, self.steps = grads, {}
        self.plain = lax.axis_size("dp") != 8
        self.line = lax.axis_size("layer") == 4

    def step(self, name, make, skip=False):
        if skip:
            return []
        if name not in self.steps:
            self.steps[name] = list(make())
        return self.steps[name]

    def core(self):
        return self.step("core", lambda: [swap(self.grads[2], "dp", 1)], self.plain)

    def first_sums(self, after=()):
        def make():
            plan = [[(0, 0), (1, 0)], [(0, 1), (1, 1)], [(0, 2), (1, 2)]]
            return add([self.grads[1], *self.core()], plan, [F32, LOW, LOW], after)

        return self.step("first", make, self.plain)

    def crossed(self):
        def make():
            _, second, diagonal = self.first_sums()
            return [over_other(diagonal), over_link(second)]

        return self.step("crossed", make, self.plain)

    def second_sums(self, after=()):
        def make():
            diagonal, second = self.crossed()
            arrays = [self.first_sums()[0], diagonal, self.grads[0], second]
            return add(arrays, [[(0, None), (1, None)], [(2, 1), (3, None)]], [LOW, LOW], after)

        return self.step("second", make, self.plain)

    def last(self):
        def make():
            first, twin = self.second_sums()
            return [over_link(first), swap(twin, "dp", 1)]

        return self.step("last", make, self.plain)

    def terms(self):
        return [self.grads[0], *self.last()]


class Line:
    def __init__(self, parts):
        self.parts, self.steps = parts, {}
        self.plain = parts[0].plain or lax.axis_size("layer") != 4
        self.half = lax.axis_index("layer") & 1

    def step(self, name, make):
        if self.plain:
            return []
        if name not in self.steps:
            self.steps[name] = list(make())
        return self.steps[name]

    def shares(self, after=()):
        def make():
            terms = [term for part in self.parts for term in part.terms()]
            return share_halves(self.half[None], terms, after)

        return self.step("shares", make)

    def near(self):
        return self.step("near", lambda: [swap(self.shares()[1], "layer", 1)])

    def pairs(self, after=()):
        plan = [[(0, None), (1, None)]]
        return self.step("pairs", lambda: add([self.shares()[0], *self.near()], plan, [LOW], after))

    def far(self):
        return self.step("far", lambda: [swap(*self.pairs(), "layer", 2)])

    def halves(self, after=()):
        plan = [[(0, None), (1, None)]]
        return self.step("halves", lambda: add([*self.pairs(), *self.far()], plan, [LOW], after))

    def back(self):
        return self.step("back", lambda: [swap(*self.halves(), "layer", 1)])

    def total(self):
        if self.plain:
            grads = [part.grads[0][0] for part in self.parts]
            shares = [lax.psum_scatter(grad, "dp", scatter_dimension=0, tiled=True) for grad in grads]
            return lax.psum(jnp.concatenate(shares, axis=1), "layer").astype(F32)
        (mine,), (other,) = self.halves(), self.back()
        first = jnp.where(self.half == 0, mine, other)
        return jnp.concatenate([first, jnp.where(self.half == 0, other, mine)], axis=0).astype(F32)


def gathered_sum(value, axes):
    size = lax.axis_size(axes)
    sent = jnp.broadcast_to(value, (size, *value.shape))
    return jnp.sum(lax.all_to_all(sent, axes, split_axis=0, concat_axis=0), axis=0)
NAT = 208
TILE = 256
CHUNK = 48
SPARE_VMEM = 6 * 2**20
HEAVY = 2.5e9
ROW = pl.BlockSpec(memory_space=pltpu.VMEM)
FAR = pl.BlockSpec(memory_space=pl.ANY)
NUMBERS = pl.BlockSpec(memory_space=pltpu.SMEM)


def shape(dims, dtype):
    return jax.ShapeDtypeStruct(dims, dtype)


def launch(kernel, us, in_specs, out_specs, out_shape, scratch_shapes=(), grid=(), prefetch=0, after=()):
    def call(*args):
        count = len(args)

        def body(*refs):
            kernel(*refs[:count], *refs[count + len(after) :])

        held = sum(
            math.prod(ref.shape) * jnp.dtype(ref.dtype).itemsize
            for ref in scratch_shapes
            if jnp.issubdtype(ref.dtype, jnp.floating)
        )
        spec = pltpu.PrefetchScalarGridSpec(
            num_scalar_prefetch=prefetch,
            grid=grid,
            in_specs=list(in_specs) + [FAR] * len(after),
            out_specs=out_specs,
            scratch_shapes=list(scratch_shapes),
        )
        return pl.pallas_call(
            body,
            grid_spec=spec,
            out_shape=out_shape,
            compiler_params=pltpu.CompilerParams(vmem_limit_bytes=held + SPARE_VMEM),
            cost_estimate=pl.CostEstimate(flops=int(us * HEAVY), bytes_accessed=1 << 20, transcendentals=0),
        )(*args, *after)

    return call


def dot(left, right):
    return jnp.dot(left, right, preferred_element_type=F32)


def dot_t(left, right):
    return lax.dot_general(left, right, (((1,), (1,)), ((), ())), preferred_element_type=F32)


def t_dot(left, right):
    return lax.dot_general(left, right, (((0,), (0,)), ((), ())), preferred_element_type=F32)


def fetch(order, pieces, weight, sems, columns=None):
    rows = pieces[0].shape[0]
    copies = []
    for index, piece in enumerate(pieces):
        source = piece if columns is None else piece.at[:, columns]
        at = pl.multiple_of(order[index] * rows, 16 if rows % 16 == 0 else 8)
        copies.append(pltpu.make_async_copy(source, weight.at[pl.ds(at, rows)], sems.at[index]))
    for copy in copies:
        copy.start()
    return copies


def wait_all(copies):
    for copy in copies:
        copy.wait()


def one_hot(masked, count, rows):
    patch = lax.broadcasted_iota(jnp.int32, (rows, MOST), 0)
    slot = lax.broadcasted_iota(jnp.int32, (rows, MOST), 1)
    return jnp.where((masked[:, :MOST] == patch) & (slot < count), 1.0, 0.0)


def normed(values):
    centered = values - jnp.mean(values, axis=-1, keepdims=True)
    inv_std = lax.rsqrt(jnp.mean(centered * centered, axis=-1, keepdims=True) + NORM_EPSILON)
    return centered * inv_std, inv_std


def norm_in(grad_in, hat, inv_std, gain):
    scaled = grad_in * gain
    return inv_std * (
        scaled
        - jnp.mean(scaled, axis=-1, keepdims=True)
        - hat * jnp.mean(scaled * hat, axis=-1, keepdims=True)
    )


def wide(column):
    return jnp.broadcast_to(column, (column.shape[0], 128))


def folded(values):
    return jnp.sum(values.reshape(-1, 8, values.shape[-1]), axis=0)


def total_row(values):
    return jnp.sum(values, axis=0, keepdims=True)


def split_store(outs, columns, grad):
    rows = outs[0].shape[1]
    low = grad.astype(LOW)
    at = 0
    for out in outs:
        for index in range(out.shape[0]):
            out[index, :, columns] = low[at : at + rows]
            at += rows


def split_shapes(blocks, columns):
    counts = (2, 3, 3) if blocks == 8 else (1,)
    return [shape((count, D // blocks, columns), LOW) for count in counts]


def teacher_kernel(blocks, images, first, counts, teacher, masked, *refs):
    outs, (held, sems) = refs[:blocks], refs[blocks:]
    copies = [
        pltpu.make_async_copy(teacher.at[pl.ds(first[block] * images, images)], held.at[block], sems.at[block])
        for block in range(blocks)
    ]
    for copy in copies:
        copy.start()
    for block in range(blocks):
        copies[block].wait()
        for index in range(images):
            count = counts[block * images + index]
            pick = one_hot(masked[block * images + index], count, P_SIZE).astype(LOW)
            rows = slice(index * MOST, (index + 1) * MOST)
            for at in range(0, D, TILE):
                low = held[block, index, :, at : at + TILE]
                values = low.astype(F32)
                mean = jnp.sum(values, axis=0, keepdims=True) * (1.0 / P_SIZE)
                centered = values - mean
                square = jnp.sum(centered * centered, axis=0, keepdims=True) * (1.0 / P_SIZE)
                inv = lax.rsqrt(square + INSTANCE_EPSILON)
                outs[block][rows, at : at + TILE] = ((t_dot(pick, low) - mean) * inv).astype(LOW)


def teacher_rows(teacher, masks, first, images, after=()):
    blocks = first.shape[0]
    return launch(
        functools.partial(teacher_kernel, blocks, images),
        0.2 * blocks,
        in_specs=[NUMBERS, NUMBERS, pl.BlockSpec(memory_space=pltpu.HBM), ROW],
        out_specs=[ROW] * blocks,
        out_shape=[shape((images * MOST, D), LOW)] * blocks,
        scratch_shapes=[pltpu.VMEM((blocks, images, P_SIZE, D), LOW), pltpu.SemaphoreType.DMA((blocks,))],
        after=after,
    )(first, masks[:, P_SIZE], teacher, masks[:, None, :P_SIZE])


def part_kernel(spans, *refs):
    ins, out = refs[: len(spans)], refs[-1]
    at = 0
    for (source, start, size, *room), ref in zip(spans, ins):
        out[:, at : at + size] = ref[:, start : start + size].astype(LOW)
        at += size
        if room:
            out[:, at : at + room[0] - size] = jnp.zeros((out.shape[0], room[0] - size), LOW)
            at += room[0] - size


def part(spans, after=()):
    rows = spans[0][0].shape[0]
    return launch(
        functools.partial(part_kernel, spans),
        0.2,
        in_specs=[ROW] * len(spans),
        out_specs=ROW,
        out_shape=shape((rows, sum(span[-1] for span in spans)), LOW),
        after=after,
    )(*[span[0] for span in spans])


def embed_kernel(owners, order, counts, pixels, masked, *refs):
    pieces, refs = refs[:owners], refs[owners:]
    hat, inv, rows_in, position, vectors, hat_tab, inv_tab, tab_in, weight, sems = refs
    step = pl.program_id(0)

    @pl.when(step == 0)
    def _():
        wait_all(fetch(order, pieces, weight, sems, pl.ds(0, D + TAIL)))
        small = weight[:, D:].astype(F32).T
        vectors[...] = small[P_SIZE : P_SIZE + vectors.shape[0]]
        rows = small[:P_SIZE]
        zeros = jnp.zeros((NAT - P_SIZE, D), F32)
        position[...] = jnp.concatenate([rows, zeros], axis=0).astype(LOW)
        table, table_inv = normed(rows + small[P_SIZE + 14 : P_SIZE + 15])
        hat_tab[...] = jnp.concatenate([table, zeros], axis=0)
        inv_tab[...] = jnp.concatenate([wide(table_inv), zeros[:, :128]], axis=0)
        table = table * small[P_SIZE : P_SIZE + 1] + small[P_SIZE + 1 : P_SIZE + 2]
        tab_in[...] = jnp.concatenate([table, zeros], axis=0).astype(LOW)

    flag = jnp.sum(one_hot(masked[0], counts[step], P_SIZE), axis=1, keepdims=True)
    embedded = dot(pixels[0], weight[:, :D]) + vectors[13:14]
    start = flag * vectors[14:15] + (1.0 - flag) * embedded + position[...].astype(F32)[:P_SIZE]
    value, value_inv = normed(start)
    zeros = jnp.zeros((NAT - P_SIZE, D), F32)
    hat[0] = jnp.concatenate([value, zeros], axis=0)
    inv[0] = jnp.concatenate([wide(value_inv), zeros[:, :128]], axis=0)
    value = value * vectors[0:1] + vectors[1:2]
    rows_in[0] = jnp.concatenate([value, zeros], axis=0).astype(LOW)


def embed(order, counts, pixels, masked, pieces, after=()):
    images, owners = pixels.shape[0], len(pieces)
    whole = lambda *dims: pl.BlockSpec(dims, lambda i, order, counts: (0,) * len(dims))
    image = lambda *dims: pl.BlockSpec((1, *dims), lambda i, order, counts: (i,) + (0,) * len(dims))
    return launch(
        functools.partial(embed_kernel, owners),
        1,
        prefetch=2,
        grid=(images,),
        in_specs=[image(P_SIZE, PIX), image(1, P_SIZE)] + [FAR] * owners,
        out_specs=[
            image(NAT, D),
            image(NAT, 128),
            image(NAT, D),
            whole(NAT, D),
            whole(24, D),
            whole(NAT, D),
            whole(NAT, 128),
            whole(NAT, D),
        ],
        scratch_shapes=[pltpu.VMEM((D, D + TAIL), LOW), pltpu.SemaphoreType.DMA((owners,))],
        out_shape=[
            shape((images, NAT, D), F32),
            shape((images, NAT, 128), F32),
            shape((images, NAT, D), LOW),
            shape((NAT, D), LOW),
            shape((24, D), F32),
            shape((NAT, D), F32),
            shape((NAT, 128), F32),
            shape((NAT, D), LOW),
        ],
        after=after,
    )(order, counts, pixels, masked, *pieces)


def halves(pair):
    lane = lax.broadcasted_iota(jnp.int32, (1, 128), 1)
    first = jnp.where(lane < HD, 1.0, 0.0).astype(LOW)
    return jnp.concatenate([pair * first, pair * (1.0 - first.astype(F32)).astype(LOW)], axis=0)


def merged(both):
    lane = lax.broadcasted_iota(jnp.int32, (MOST, 128), 1)
    return jnp.where(lane < HD, both[:MOST], both[MOST:])


def attention_kernel(owners, order, counts, rows_in, masked, tab_in, vectors, *refs):
    pieces, refs = refs[:owners], refs[owners:]
    kv, queries, heads, weight, table, sems = refs
    step = pl.program_id(0)

    @pl.when(step == 0)
    def _():
        wait_all(fetch(order, pieces, weight, sems, pl.ds(D + TAIL, 3 * D)))
        table[...] = (dot(tab_in[...], weight[:, :D]) + vectors[2:3]).astype(LOW)

    kv[0, :, :D] = dot(rows_in[0], weight[:, D : 2 * D]).astype(LOW)
    kv[0, :, D:] = (dot(rows_in[0], weight[:, 2 * D :]) + vectors[3:4]).astype(LOW)
    pick = one_hot(masked[0], counts[step], NAT).astype(LOW)
    queries[0] = t_dot(pick, table[...]).astype(LOW)
    key_index = lax.broadcasted_iota(jnp.int32, (1, NAT), 1)
    for at in range(0, D, 128):
        pair = halves(queries[0, :, at : at + 128])
        scores = dot_t(pair, kv[0, :, at : at + 128]) * (1.0 / math.sqrt(HD))
        scores = jnp.where(key_index < P_SIZE, scores, -1e30)
        shifted = jnp.exp(scores - jnp.max(scores, axis=1, keepdims=True))
        probs = (shifted * (1.0 / jnp.sum(shifted, axis=1, keepdims=True))).astype(LOW)
        heads[0, :, at : at + 128] = merged(dot(probs, kv[0, :, D + at : D + at + 128])).astype(LOW)


def attention(order, counts, rows_in, masked, tab_in, vectors, pieces, after=()):
    images, owners = rows_in.shape[0], len(pieces)
    whole = lambda *dims: pl.BlockSpec(dims, lambda i, order, counts: (0,) * len(dims))
    image = lambda *dims: pl.BlockSpec((1, *dims), lambda i, order, counts: (i,) + (0,) * len(dims))
    return launch(
        functools.partial(attention_kernel, owners),
        12,
        prefetch=2,
        grid=(images,),
        in_specs=[image(NAT, D), image(1, P_SIZE), whole(NAT, D), whole(24, D)] + [FAR] * owners,
        out_specs=[image(NAT, 2 * D), image(MOST, D), image(MOST, D)],
        scratch_shapes=[
            pltpu.VMEM((D, 3 * D), LOW),
            pltpu.VMEM((NAT, D), LOW),
            pltpu.SemaphoreType.DMA((owners,)),
        ],
        out_shape=[shape((images, NAT, 2 * D), LOW), shape((images, MOST, D), LOW), shape((images, MOST, D), LOW)],
        after=after,
    )(order, counts, rows_in, masked, tab_in, vectors, *pieces)


def chunks(count, body):
    lax.fori_loop(0, count, lambda k, _: (body(k), 0)[1], 0)


def at_chunk(k, rows=CHUNK):
    return pl.ds(pl.multiple_of(k * rows, 16), rows)


def gelu_parts(value):
    size = jnp.abs(value) * math.sqrt(0.5)
    t = 1.0 / (1.0 + 0.3275911 * size)
    bell = jnp.exp(-size * size)
    poly = t * (0.254829592 + t * (-0.284496736 + t * (1.421413741 + t * (-1.453152027 + t * 1.061405429))))
    below = 0.5 * poly * bell
    share = jnp.where(value < 0, below, 1.0 - below)
    return value * share, share + value * bell * (1.0 / math.sqrt(2.0 * math.pi))


def mid_kernel(owners, images, order, counts, masked, heads, position, vectors, *refs):
    pieces, refs = refs[:owners], refs[owners:]
    attn, hidden, hat, inv, rows_in, weight, sems = refs
    copies = fetch(order, pieces, weight, sems, pl.ds(0, D))
    for index in range(images):
        pick = one_hot(masked[index], counts[index], NAT).astype(LOW)
        hidden[index * MOST : (index + 1) * MOST] = t_dot(pick, position[...]) + vectors[14:15]
    wait_all(copies)
    for at in range(0, D, TILE):
        attn[:, at : at + TILE] = dot(heads[...], weight[:, at : at + TILE])

    def first(k):
        rows = at_chunk(k)
        branch = attn[rows] + vectors[4:5]
        attn[rows] = branch
        value = hidden[rows] + vectors[5:6] * branch
        hidden[rows] = value
        value, value_inv = normed(value)
        hat[rows] = value
        inv[rows] = wide(value_inv)
        rows_in[rows] = (value * vectors[6:7] + vectors[7:8]).astype(LOW)

    chunks(hidden.shape[0] // CHUNK, first)


def mid(order, counts, masked, heads, position, vectors, pieces, after=()):
    rows, owners = heads.shape[0], len(pieces)
    return launch(
        functools.partial(mid_kernel, owners, masked.shape[0]),
        6,
        in_specs=[NUMBERS, NUMBERS] + [ROW] * 4 + [FAR] * owners,
        out_specs=[ROW] * 5,
        out_shape=[
            shape((rows, D), F32),
            shape((rows, D), F32),
            shape((rows, D), F32),
            shape((rows, 128), F32),
            shape((rows, D), LOW),
        ],
        scratch_shapes=[pltpu.VMEM((D, D), LOW), pltpu.SemaphoreType.DMA((owners,))],
        after=after,
    )(order, counts, masked, heads, position, vectors, *pieces)


def up_kernel(owners, first, order, rows_in, vectors, *refs):
    pieces, refs = refs[:owners], refs[owners:]
    active, slope, weight, pre_a, pre_b, sems = refs
    wait_all(fetch(order, pieces, weight, sems, pl.ds(D + first, active.shape[1])))

    def product(tile, into):
        into[...] = dot(rows_in[...], weight[:, pl.ds(pl.multiple_of(tile * TILE, TILE), TILE)])

    def finish(tile, source):
        columns = pl.ds(pl.multiple_of(tile * TILE, TILE), TILE)
        part = D // TILE
        row = 15 + first // D + tile // part
        bias = vectors[pl.ds(row, 1), pl.ds(pl.multiple_of((tile % part) * TILE, TILE), TILE)]
        for start in range(0, source.shape[0], 48):
            value, down = gelu_parts(source[start : start + 48] + bias)
            active[start : start + 48, columns] = value.astype(LOW)
            slope[start : start + 48, columns] = down.astype(LOW)

    tiles = active.shape[1] // TILE
    product(0, pre_a)

    def pair(k):
        product(2 * k + 1, pre_b)
        finish(2 * k, pre_a)
        product(jnp.minimum(2 * k + 2, tiles - 1), pre_a)
        finish(2 * k + 1, pre_b)

    chunks(tiles // 2, pair)


def up(first, columns, order, rows_in, vectors, pieces, after=()):
    rows, owners = rows_in.shape[0], len(pieces)
    return launch(
        functools.partial(up_kernel, owners, first),
        7,
        in_specs=[NUMBERS] + [ROW] * 2 + [FAR] * owners,
        out_specs=[ROW] * 2,
        out_shape=[shape((rows, columns), LOW)] * 2,
        scratch_shapes=[
            pltpu.VMEM((D, columns), LOW),
            pltpu.VMEM((rows, TILE), F32),
            pltpu.VMEM((rows, TILE), F32),
            pltpu.SemaphoreType.DMA((owners,)),
        ],
        after=after,
    )(order, rows_in, vectors, *pieces)


def place(order, source, turned, scratch):
    blocks = order.shape[0]
    if blocks == 1:
        turned[...] = source.T
        return
    rows = D // blocks
    scratch[...] = source.T
    for index in range(blocks):
        at = pl.multiple_of(order[index] * rows, 16 if rows % 16 == 0 else 8)
        turned[index * rows : (index + 1) * rows] = scratch[pl.ds(at, rows)]


def head_kernel(owners, order, active_a, active_b, hidden, vectors, *refs):
    pieces, refs = refs[:owners], refs[owners:]
    branch, hat, inv, rows_in, work, weight, sems = refs
    wait_all(fetch(order, pieces, weight, sems))
    half = active_a.shape[1]
    for at in range(0, D, TILE):
        rows = slice(at, at + TILE)
        value = dot_t(active_a[...], weight[rows, :half])
        branch[:, rows] = value + dot_t(active_b[...], weight[rows, half:FF])

    def first(k):
        rows = at_chunk(k)
        value = branch[rows] + vectors[8:9]
        branch[rows] = value
        value, value_inv = normed(hidden[rows] + vectors[9:10] * value)
        hat[rows] = value
        inv[rows] = wide(value_inv)
        rows_in[rows] = (value * vectors[10:11] + vectors[11:12]).astype(LOW)

    chunks(hidden.shape[0] // CHUNK, first)
    for at in range(0, D, TILE):
        work[:, at : at + TILE] = dot(rows_in[...], weight[:, FF + at : FF + at + TILE])


def head(order, active, hidden, vectors, pieces, after=()):
    rows, owners = hidden.shape[0], len(pieces)
    return launch(
        functools.partial(head_kernel, owners),
        10,
        in_specs=[NUMBERS] + [ROW] * 4 + [FAR] * owners,
        out_specs=[ROW] * 5,
        out_shape=[
            shape((rows, D), F32),
            shape((rows, D), F32),
            shape((rows, 128), F32),
            shape((rows, D), LOW),
            shape((rows, D), F32),
        ],
        scratch_shapes=[pltpu.VMEM((D, FF + D), LOW), pltpu.SemaphoreType.DMA((owners,))],
        after=after,
    )(order, *active, hidden, vectors, *pieces)


def down_kernel(owners, parts, order, counts, work, hat, inv, branch, active_a, active_b, vectors, rows_in, *refs):
    targets, pieces, refs = refs[:parts], refs[parts : parts + owners], refs[parts + owners :]
    outs = 3 if owners > 1 else 1
    grads = refs[:outs]
    loss, head_sums, grad, grad_low, sums, weight, error_low, turned, spare, sems = refs[outs:]
    copies = fetch(order, pieces, weight, sems, pl.ds(FF, D))
    head_sums[...] = jnp.zeros_like(head_sums)
    sums[...] = jnp.zeros_like(sums)
    steps = grad.shape[0] // CHUNK

    def errors(k):
        rows = at_chunk(k)
        target = targets[0][rows].astype(F32)
        for other in targets[1:]:
            target = target + other[rows].astype(F32)
        error = work[rows] + vectors[12:13] - target * (1.0 / lax.axis_size("layer"))
        size = jnp.abs(error)
        entry = jnp.where(size < HUBER_BETA, error * error * (0.5 / HUBER_BETA), size - 0.5 * HUBER_BETA)
        per_image = MOST // CHUNK
        row = lax.broadcasted_iota(jnp.int32, (CHUNK, 1), 0) + lax.rem(k, per_image) * CHUNK
        flag = row < counts[k // per_image]
        head_sums[0] += folded(jnp.where(flag, entry, 0.0))
        value = jnp.where(flag, jnp.clip(error * (1.0 / HUBER_BETA), -1.0, 1.0), 0.0)
        head_sums[1] += folded(value)
        error_low[rows] = value.astype(LOW)

    chunks(steps, errors)
    loss[0, 0] = jnp.sum(head_sums[0])
    wait_all(copies)
    for at in range(0, D, TILE):
        grad[:, at : at + TILE] = dot_t(error_low[...], weight[at : at + TILE])

    def back(k):
        rows = at_chunk(k)
        grad_in, value = grad[rows], hat[rows]
        sums[0] += folded(grad_in * value)
        sums[1] += folded(grad_in)
        value = norm_in(grad_in, value, inv[rows, :1], vectors[10:11])
        grad[rows] = value
        sums[2] += folded(value * branch[rows])
        value = value * vectors[9:10]
        sums[3] += folded(value)
        grad_low[rows] = value.astype(LOW)

    chunks(steps, back)
    place(order, grad_low[...], turned, spare)
    half = active_a.shape[1]
    for at in range(0, FF, TILE):
        source = active_a[:, at : at + TILE] if at < half else active_b[:, at - half : at - half + TILE]
        split_store(grads, slice(at, at + TILE), dot(turned[...], source))
    place(order, rows_in[...], turned, spare)
    for at in range(0, D, TILE):
        columns = slice(FF + at, FF + at + TILE)
        split_store(grads, columns, dot(turned[...], error_low[:, at : at + TILE]))


def down(order, counts, work, hat, inv, branch, active, vectors, rows_in, targets, pieces, after=()):
    rows, owners = hat.shape[0], len(pieces)
    grads = split_shapes(owners, FF + D)
    return launch(
        functools.partial(down_kernel, owners, len(targets)),
        15,
        in_specs=[NUMBERS, NUMBERS] + [ROW] * (8 + len(targets)) + [FAR] * owners,
        out_specs=[ROW] * len(grads) + [NUMBERS] + [ROW] * 4,
        out_shape=grads
        + [
            shape((1, 1), F32),
            shape((2, 8, D), F32),
            shape((rows, D), F32),
            shape((rows, D), LOW),
            shape((4, 8, D), F32),
        ],
        scratch_shapes=[
            pltpu.VMEM((D, D), LOW),
            pltpu.VMEM((rows, D), LOW),
            pltpu.VMEM((D, rows), LOW),
            pltpu.VMEM((D, rows), LOW),
            pltpu.SemaphoreType.DMA((owners,)),
        ],
        after=after,
    )(order, counts, work, hat, inv, branch, *active, vectors, rows_in, *targets, *pieces)


def pre_kernel(owners, order, grad_low, slope_a, slope_b, rows_in, *refs):
    pieces, refs = refs[:owners], refs[owners:]
    outs = 3 if owners > 1 else 1
    grads = refs[:outs]
    pre_low, bias, weight, turned, spare, sems = refs[outs:]
    copies = fetch(order, pieces, weight, sems, pl.ds(0, FF))
    place(order, rows_in[...], turned, spare)
    wait_all(copies)

    half = slope_a.shape[1]
    for at in range(0, FF, TILE):
        columns = slice(at, at + TILE)
        slope, start = (slope_a, at) if at < half else (slope_b, at - half)
        value = dot(grad_low[...], weight[:, columns]) * slope[:, start : start + TILE].astype(F32)
        bias[:, columns] = folded(value)
        pre_low[:, columns] = value.astype(LOW)
        split_store(grads, columns, dot(turned[...], pre_low[:, columns]))


def pre(order, grad_low, slope, rows_in, pieces, after=()):
    rows, owners = grad_low.shape[0], len(pieces)
    grads = split_shapes(owners, FF)
    return launch(
        functools.partial(pre_kernel, owners),
        12,
        in_specs=[NUMBERS] + [ROW] * 4 + [FAR] * owners,
        out_specs=[ROW] * (len(grads) + 2),
        out_shape=grads + [shape((rows, FF), LOW), shape((8, FF), F32)],
        scratch_shapes=[
            pltpu.VMEM((D, FF), LOW),
            pltpu.VMEM((D, rows), LOW),
            pltpu.VMEM((D, rows), LOW),
            pltpu.SemaphoreType.DMA((owners,)),
        ],
        after=after,
    )(order, grad_low, *slope, rows_in, *pieces)


def out_kernel(owners, images, order, counts, masked, pre_low, grad, hat, inv, attn, vectors, *refs):
    pieces, refs = refs[:owners], refs[owners:]
    heads_grad, table, sums, attn_low, weight, work, high, rest, sems = refs
    wait_all(fetch(order, pieces, weight, sems))
    for at in range(0, D, TILE):
        work[:, at : at + TILE] = dot_t(pre_low[...], weight[at : at + TILE, D:])
    sums[...] = jnp.zeros_like(sums)

    def back(k):
        rows = at_chunk(k)
        grad_in, value = work[rows], hat[rows]
        sums[0] += folded(grad_in * value)
        sums[1] += folded(grad_in)
        value = grad[rows] + norm_in(grad_in, value, inv[rows, :1], vectors[6:7])
        low = value.astype(LOW)
        high[rows] = low
        rest[rows] = (value - low.astype(F32)).astype(LOW)
        sums[2] += folded(value * attn[rows])
        value = value * vectors[5:6]
        sums[3] += folded(value)
        attn_low[rows] = value.astype(LOW)

    chunks(work.shape[0] // CHUNK, back)
    for at in range(0, D, TILE):
        heads_grad[:, at : at + TILE] = dot_t(attn_low[...], weight[at : at + TILE, :D]).astype(LOW)
    for index in range(images):
        pick = one_hot(masked[index], counts[index], NAT).astype(LOW)
        rows = slice(index * MOST, (index + 1) * MOST)
        value = dot(pick, high[rows]) + dot(pick, rest[rows])
        table[...] = value if index == 0 else table[...] + value


def out_back(order, counts, masked, pre_low, grad, hat, inv, attn, vectors, pieces, after=()):
    rows, owners = grad.shape[0], len(pieces)
    return launch(
        functools.partial(out_kernel, owners, masked.shape[0]),
        14,
        in_specs=[NUMBERS, NUMBERS] + [ROW] * 7 + [FAR] * owners,
        out_specs=[ROW] * 4,
        out_shape=[shape((rows, D), LOW), shape((NAT, D), F32), shape((4, 8, D), F32), shape((rows, D), LOW)],
        scratch_shapes=[
            pltpu.VMEM((D, D + FF), LOW),
            pltpu.VMEM((rows, D), F32),
            pltpu.VMEM((rows, D), LOW),
            pltpu.VMEM((rows, D), LOW),
            pltpu.SemaphoreType.DMA((owners,)),
        ],
        after=after,
    )(order, counts, masked, pre_low, grad, hat, inv, attn, vectors, *pieces)


def attention_back_kernel(counts, queries, kv, heads_grad, masked, kv_low, table, sums, query_low):
    step = pl.program_id(0)

    @pl.when(step == 0)
    def _():
        table[...] = jnp.zeros_like(table)
        sums[...] = jnp.zeros_like(sums)

    scale = 1.0 / math.sqrt(HD)
    key_index = lax.broadcasted_iota(jnp.int32, (NAT, 1), 0)
    for at in range(0, D, 128):
        lanes = slice(at, at + 128)
        high = slice(D + at, D + at + 128)
        pair, grad = halves(queries[0, :, lanes]), halves(heads_grad[0, :, lanes])
        keys, values = kv[0, :, lanes], kv[0, :, high]
        scores = jnp.where(key_index < P_SIZE, dot_t(keys, pair) * scale, -1e30)
        shifted = jnp.exp(scores - jnp.max(scores, axis=0, keepdims=True))
        probs = shifted * (1.0 / jnp.sum(shifted, axis=0, keepdims=True))
        prob_grad = dot_t(values, grad)
        value_grad = dot(probs.astype(LOW), grad).astype(LOW)
        kv_low[0, :, high] = value_grad
        sums[1, :, lanes] += folded(value_grad.astype(F32))
        inner = jnp.sum(probs * prob_grad, axis=0, keepdims=True)
        score_grad = (probs * (prob_grad - inner)).astype(LOW)
        kv_low[0, :, lanes] = (dot(score_grad, pair) * scale).astype(LOW)
        query_grad = merged(t_dot(score_grad, keys) * scale).astype(LOW)
        query_low[:, lanes] = query_grad
        sums[0, :, lanes] += folded(query_grad.astype(F32))
    pick = one_hot(masked[0], counts[step], NAT).astype(LOW)
    table[...] += dot(pick, query_low[...])


def attention_back(counts, queries, kv, heads_grad, masked, after=()):
    images = kv.shape[0]
    whole = lambda *dims: pl.BlockSpec(dims, lambda i, counts: (0,) * len(dims))
    image = lambda *dims: pl.BlockSpec((1, *dims), lambda i, counts: (i,) + (0,) * len(dims))
    return launch(
        attention_back_kernel,
        15,
        prefetch=1,
        grid=(images,),
        in_specs=[image(MOST, D), image(NAT, 2 * D), image(MOST, D), image(1, P_SIZE)],
        out_specs=[image(NAT, 2 * D), whole(NAT, D), whole(2, 8, D)],
        scratch_shapes=[pltpu.VMEM((MOST, D), LOW)],
        out_shape=[shape((images, NAT, 2 * D), LOW), shape((NAT, D), F32), shape((2, 8, D), F32)],
        after=after,
    )(counts, queries, kv, heads_grad, masked)


def high_rest(value):
    high = value.astype(LOW)
    return jnp.concatenate([high, (value - high.astype(F32)).astype(LOW)], axis=0)


def qkv_kernel(blocks, order, rows_in, kv_low, tab_in, table, heads, attn_low, *refs):
    outs = 3 if blocks > 1 else 1
    grads = refs[:outs]
    turned, spare, tab_turned, tab_spare, heads_turned, heads_spare = refs[outs:]
    place(order, heads[...], heads_turned, heads_spare)
    for at in range(0, D, TILE):
        columns = slice(3 * D + at, 3 * D + at + TILE)
        split_store(grads, columns, dot(heads_turned[...], attn_low[:, at : at + TILE]))
    place(order, tab_in[...], tab_turned, tab_spare)
    both = high_rest(table[...])
    twice = jnp.concatenate([tab_turned[...], tab_turned[...]], axis=1)
    for at in range(0, D, TILE):
        split_store(grads, slice(at, at + TILE), dot(twice, both[:, at : at + TILE]))
    place(order, rows_in[...], turned, spare)

    for at in range(0, 2 * D, TILE):
        split_store(grads, slice(D + at, D + at + TILE), dot(turned[...], kv_low[:, at : at + TILE]))


def qkv_back(order, rows_in, kv_low, tab_in, table, heads, attn_low, after=()):
    blocks, rows = order.shape[0], rows_in.shape[0]
    grads = split_shapes(blocks, 4 * D)
    return launch(
        functools.partial(qkv_kernel, blocks),
        7,
        in_specs=[NUMBERS] + [ROW] * 6,
        out_specs=[ROW] * len(grads),
        out_shape=grads,
        scratch_shapes=[
            pltpu.VMEM((D, rows), LOW),
            pltpu.VMEM((D, rows), LOW),
            pltpu.VMEM((D, NAT), LOW),
            pltpu.VMEM((D, NAT), LOW),
            pltpu.VMEM((D, heads.shape[0]), LOW),
            pltpu.VMEM((D, heads.shape[0]), LOW),
        ],
        after=after,
    )(order, rows_in, kv_low, tab_in, table, heads, attn_low)


def start_kernel(owners, images, order, counts, masked, pixels, kv_low, table, hidden_tab, hat, inv, hat_tab, inv_tab, vectors, head_sums, down_sums, up_bias, out_sums, qkv_sums, *refs):
    pieces, refs = refs[:owners], refs[owners:]
    outs = 3 if owners > 1 else 1
    grads = refs[:outs]
    weight, work, start_low, small, sums, turned, spare, pixel_rows, small_low, sems = refs[outs:]
    copies = fetch(order, pieces, weight, sems, pl.ds(D + TAIL, 3 * D))
    for index in range(images):
        zeros = jnp.zeros((NAT - P_SIZE, PIX), F32)
        padded = jnp.concatenate([pixels[index].astype(F32), zeros], axis=0)
        pixel_rows[index * NAT : (index + 1) * NAT] = padded.astype(LOW)
    place(order, pixel_rows[...], turned, spare)
    wait_all(copies)
    for at in range(0, D, TILE):
        work[:, at : at + TILE] = dot_t(kv_low[...], weight[at : at + TILE, D:])
    both = high_rest(table[...])
    tab_in = dot_t(both, weight[:, :D])
    tab_in = tab_in[:NAT] + tab_in[NAT:]
    gain = vectors[0:1]
    sums[...] = jnp.zeros_like(sums)
    sums[0] += folded(tab_in * hat_tab[...])
    sums[1] += folded(tab_in)
    tab_grad = norm_in(tab_in, hat_tab[...], inv_tab[:, :1], gain) + hidden_tab[...]
    sums[2] += folded(tab_grad)
    small[:NAT] = tab_grad
    half = NAT // 2
    for index in range(images):
        flags = jnp.sum(one_hot(masked[index], counts[index], NAT), axis=1, keepdims=True)
        for part in range(2):
            rows = slice(index * NAT + part * half, index * NAT + (part + 1) * half)
            flag = flags[part * half : (part + 1) * half]
            grad_in, value = work[rows], hat[rows]
            sums[0] += folded(grad_in * value)
            sums[1] += folded(grad_in)
            value = norm_in(grad_in, value, inv[rows, :1], gain)
            small[part * half : (part + 1) * half] += value
            sums[2] += folded(value * flag)
            value = value * (1.0 - flag)
            sums[3] += folded(value)
            start_low[rows] = value.astype(LOW)
    line = [
        total_row(sums[0]),
        total_row(sums[1]),
        total_row(qkv_sums[0]),
        total_row(qkv_sums[1]),
        total_row(out_sums[3]),
        total_row(out_sums[2]),
        total_row(out_sums[0]),
        total_row(out_sums[1]),
        total_row(down_sums[3]),
        total_row(down_sums[2]),
        total_row(down_sums[0]),
        total_row(down_sums[1]),
        total_row(head_sums[1]),
        total_row(sums[3]),
        total_row(sums[2]),
    ]
    line += [total_row(up_bias[:, at : at + D]) for at in range(0, FF, D)]
    for index, value in enumerate(line):
        small[P_SIZE + index : P_SIZE + index + 1] = value
    small[P_SIZE + len(line) :] = jnp.zeros((TAIL - P_SIZE - len(line), D), F32)
    small_low[...] = small[...].T
    rows = D // order.shape[0]
    block = 0
    for out in grads:
        for index in range(out.shape[0]):
            at = pl.multiple_of(order[block] * rows, 16 if rows % 16 == 0 else 8)
            out[index, :, D:] = small_low[pl.ds(at, rows)].astype(LOW)
            block += 1
    for at in range(0, D, TILE):
        split_store(grads, slice(at, at + TILE), dot(turned[...], start_low[:, at : at + TILE]))


def start_back(order, counts, masked, pixels, kv_low, table, hidden_tab, hat, inv, hat_tab, inv_tab, vectors, head_sums, down_sums, up_bias, out_sums, qkv_sums, pieces, after=()):
    rows, owners, images = kv_low.shape[0], len(pieces), masked.shape[0]
    grads = split_shapes(owners, D + TAIL)
    return launch(
        functools.partial(start_kernel, owners, images),
        11,
        in_specs=[NUMBERS, NUMBERS] + [ROW] * 15 + [FAR] * owners,
        out_specs=[ROW] * len(grads),
        out_shape=grads,
        scratch_shapes=[
            pltpu.VMEM((D, 3 * D), LOW),
            pltpu.VMEM((rows, D), F32),
            pltpu.VMEM((rows, D), LOW),
            pltpu.VMEM((TAIL, D), F32),
            pltpu.VMEM((4, 8, D), F32),
            pltpu.VMEM((D, rows), LOW),
            pltpu.VMEM((D, rows), LOW),
            pltpu.VMEM((rows, D), LOW),
            pltpu.VMEM((D, TAIL), F32),
            pltpu.SemaphoreType.DMA((owners,)),
        ],
        after=after,
    )(order, counts, masked, pixels, kv_low, table, hidden_tab, hat, inv, hat_tab, inv_tab, vectors, head_sums, down_sums, up_bias, out_sums, qkv_sums, *pieces)


def add_kernel(plan, *refs):
    ins, outs = refs[: len(refs) - len(plan)], refs[len(refs) - len(plan) :]
    for terms, out in zip(plan, outs):
        total = None
        for source, block in terms:
            value = (ins[source][...] if block is None else ins[source][block]).astype(F32)
            total = value if total is None else total + value
        out[...] = total.astype(out.dtype)


def add(arrays, plan, types, after=()):
    rows, columns = arrays[0].shape[-2:]
    return launch(
        functools.partial(add_kernel, plan),
        1,
        in_specs=[ROW] * len(arrays),
        out_specs=[ROW] * len(plan),
        out_shape=[shape((rows, columns), kind) for kind in types],
        after=after,
    )(*arrays)


def share_kernel(count, half, *refs):
    ins, (keep, send, spare) = refs[: 3 * count], refs[3 * count :]
    at = 0
    for part in range(count):
        own, first, twin = ins[3 * part : 3 * part + 3]
        columns = slice(at, at + first.shape[1])
        spare[:, columns] = own[0].astype(F32) + (first[...].astype(F32) + twin[...].astype(F32))
        at += first.shape[1]
    rows = keep.shape[0]
    kept = half[0]
    keep[...] = spare[pl.ds(pl.multiple_of(kept * rows, 8), rows)]
    send[...] = spare[pl.ds(pl.multiple_of((1 - kept) * rows, 8), rows)].astype(LOW)


def share_halves(half, terms, after=()):
    count = len(terms) // 3
    rows = terms[0].shape[-2]
    columns = sum(terms[3 * part].shape[-1] for part in range(count))
    return launch(
        functools.partial(share_kernel, count),
        1,
        in_specs=[NUMBERS] + [ROW] * len(terms),
        out_specs=[ROW] * 2,
        out_shape=[shape((rows // 2, columns), F32), shape((rows // 2, columns), LOW)],
        scratch_shapes=[pltpu.VMEM((rows, columns), F32)],
        after=after,
    )(half, *terms)


def adam_update(master, first, second, grad, decay):
    first_new = FIRST_DECAY * first + (1.0 - FIRST_DECAY) * grad
    second_new = SECOND_DECAY * second + (1.0 - SECOND_DECAY) * grad * grad
    first_hat = first_new / (1.0 - FIRST_DECAY**STEP)
    second_hat = second_new / (1.0 - SECOND_DECAY**STEP)
    master_new = master - LEARN_RATE * (
        first_hat / (jnp.sqrt(second_hat) + ADAM_EPSILON) + WEIGHT_DECAY * decay * master
    )
    return (master_new, first_new, second_new)


def targets_of(teacher, masked, counts, after, twin, chips):
    layers, images = lax.axis_size("layer"), masked.shape[0]
    masks = jnp.concatenate([masked, counts[:, None]], axis=1)
    if layers != 4:
        masks = lax.all_gather(masks, "layer", axis=0, tiled=False)
        picked = [
            teacher_rows(teacher, masks[block], jnp.full((1,), block, jnp.int32), images)[0]
            for block in range(layers)
        ]
        total = lax.psum_scatter(jnp.stack(picked), "layer", scatter_dimension=0, tiled=False)
        return total, None, None, picked[0]
    at = lax.axis_index("layer")
    near, second, third = [swap(masks, "layer", bit) for bit in (1, 2, 3)]

    def rows_of(masks, bit, after):
        return teacher_rows(teacher, masks, (at ^ bit)[None], images, after)[0]

    own_rows = rows_of(masks, 0, after)
    far_rows = rows_of(third, 3, [own_rows, near, second])
    far = swap(far_rows, "layer", 1)
    second_rows = rows_of(second, 2, [far_rows, *twin, *chips])

    def near_sum(after):
        rows = rows_of(near, 1, after)
        return rows, swap(rows, "layer", 1)

    far_sum = lambda after: add([second_rows, far], [[(0, None), (1, None)]], [LOW], after)[0]
    return own_rows, near_sum, far_sum, second_rows


def body(
    pixels,
    teacher,
    masked_at,
    mask_count,
    wide_master,
    wide_first,
    wide_second,
    tall_master,
    tall_first,
    tall_second,
):
    owners, layers = lax.axis_size("dp"), lax.axis_size("layer")
    counts, masked = mask_count[0], masked_at[0][:, None, :]
    images = counts.shape[0]
    order = blocks_of(lax.axis_index("dp")) if owners == 8 else jnp.zeros((1,), jnp.int32)
    tall_low = tall_master.T.astype(LOW)
    wide_embed = part(
        [(wide_master, 0, D), (tall_low, FF, P_SIZE + VECS, TAIL), (wide_master, D, 3 * D)]
    )
    pieces_in = gather_part(wide_embed)
    own_rows, near_sum, far_sum, second_rows = targets_of(
        teacher[0, 0], masked_at[0], counts, [wide_embed], arrived(pieces_in, 1), arrived(pieces_in, 2)
    )
    wide_up = part([(wide_master, 4 * D, D + FF)], [second_rows] + arrived(pieces_in, 4))
    pieces_up = gather_part(wide_up)

    hat_nat, inv_nat, in_nat, position, vectors, hat_tab, inv_tab, in_tab = embed(
        order, counts, pixels[0], masked, pieces_in, after=[wide_up]
    )
    targets, waits = [own_rows], arrived(pieces_up, 2)
    if far_sum:
        near_rows, near = near_sum([in_tab])
        far = far_sum([near_rows])
        targets += [near, swap(far, "layer", 2)]
        waits += [far]
    kv, queries, heads = attention(order, counts, in_nat, masked, in_tab, vectors, pieces_in, after=waits)
    heads = heads.reshape(images * MOST, D)
    wide_down = part([(tall_low, 0, FF), (wide_master, 5 * D + FF, D)], [heads] + arrived(pieces_up, 4))
    pieces_down = gather_part(wide_down)
    attn, hidden, hat_mid, inv_mid, in_mid = mid(
        order, counts, masked, heads, position, vectors, pieces_up, after=[wide_down]
    )
    active_a, slope_a = up(0, FF // 2, order, in_mid, vectors, pieces_up)
    active_b, slope_b = up(
        FF // 2, FF // 2, order, in_mid, vectors, pieces_up, after=[active_a] + arrived(pieces_down, 2)
    )
    active, slope = (active_a, active_b), (slope_a, slope_b)
    branch, hat_out, inv_out, in_out, work = head(order, active, hidden, vectors, pieces_down)
    *down_g, loss, head_sums, grad, grad_low, down_sums = down(
        order, counts, work, hat_out, inv_out, branch, active, vectors, in_out, targets, pieces_down
    )
    down_s = Owned(down_g)
    *up_g, pre_low, up_bias = pre(order, grad_low, slope, in_mid, pieces_down)
    up_s = Owned(up_g)
    heads_grad, hidden_tab, out_sums, attn_low = out_back(
        order, counts, masked, pre_low, grad, hat_mid, inv_mid, attn, vectors, pieces_up,
        after=down_s.first_sums([pre_low]),
    )
    kv_low, table, qkv_sums = attention_back(
        counts, queries, kv, heads_grad.reshape(images, MOST, D), masked,
        after=down_s.second_sums([heads_grad]) + up_s.first_sums([heads_grad]),
    )
    flat = lambda value: value.reshape(images * NAT, -1)
    down_l = Line([down_s])
    qkv_g = qkv_back(
        order, flat(in_nat), flat(kv_low), in_tab, table, heads, attn_low,
        after=down_l.shares([table]) + up_s.second_sums([table]),
    )
    qkv_s, up_l = Owned(qkv_g), Line([up_s])
    embed_g = start_back(
        order, counts, masked, pixels[0], flat(kv_low), table, hidden_tab, flat(hat_nat), flat(inv_nat),
        hat_tab, inv_tab, vectors, head_sums, down_sums, up_bias, out_sums, qkv_sums, pieces_in,
        after=down_l.pairs([qkv_g[0]]) + up_l.shares([qkv_g[0]]),
    )
    embed_s = Owned(embed_g)
    last_l = Line([qkv_s, embed_s])
    qkv_s.first_sums([embed_g[0]])
    up_l.pairs([embed_g[0]])
    down_s, up_s, last_s = down_l.total(), up_l.total(), last_l.total()
    qkv_s, embed_s = last_s[:, : 4 * D], last_s[:, 4 * D :]
    wide_share = jnp.concatenate([embed_s[:, :D], qkv_s, up_s, down_s[:, FF:]], axis=1)
    tall_share = jnp.concatenate([down_s[:, :FF], embed_s[:, D : D + P_SIZE + VECS]], axis=1)
    squares = (jnp.sum(wide_share * wide_share) + jnp.sum(tall_share * tall_share)) / layers
    count = jnp.sum(mask_count.astype(F32))
    loss_sum, mask_total, squares = gathered_sum(jnp.stack([loss[0, 0], count, squares]), ("layer", "dp"))
    per_mask = 1.0 / mask_total
    grad_norm = jnp.sqrt(squares) * per_mask
    factor = CLIP_NORM / jnp.maximum(grad_norm, CLIP_NORM) * per_mask
    wide_new, wide_first_new, wide_second_new = adam_update(
        wide_master, wide_first, wide_second, factor * wide_share, 1.0
    )
    tall_decay = (lax.broadcasted_iota(jnp.int32, (tall_master.shape[0], 1), 0) < FF).astype(F32)
    tall_grad = factor * tall_share.T
    tall_new, tall_first_new, tall_second_new = adam_update(
        tall_master, tall_first, tall_second, tall_grad, tall_decay
    )
    return (
        loss_sum,
        mask_total,
        grad_norm,
        wide_new,
        wide_first_new,
        wide_second_new,
        wide_new.astype(LOW),
        tall_new,
        tall_first_new,
        tall_second_new,
        tall_new.astype(LOW),
        tall_grad[FF + P_SIZE + 2],
    )


def solution(mesh):
    in_specs = (
        P("dp", "layer", None, None),
        P("layer", "dp", None, None, None),
        P("dp", "layer", None),
        P("dp", "layer"),
        P("dp", None),
        P("dp", None),
        P("dp", None),
        P(None, "dp"),
        P(None, "dp"),
        P(None, "dp"),
    )
    out_specs = (
        P(),
        P(),
        P(),
        P("dp", None),
        P("dp", None),
        P("dp", None),
        P("dp", None),
        P(None, "dp"),
        P(None, "dp"),
        P(None, "dp"),
        P(None, "dp"),
        P("dp"),
    )
    return jax.shard_map(body, mesh=mesh, in_specs=in_specs, out_specs=out_specs, check_vma=False)
```

```python
import functools
import math

import jax
import jax.numpy as jnp
from jax import lax
from jax.experimental import pallas as pl
from jax.experimental.pallas import tpu as pltpu
from jax.sharding import PartitionSpec as P

D = 768
HEADS = 12
HD = 64
FF = 3072
PIX = 768
P_SIZE = 196
STEP = 10
VECS = 19
MOST = 144
TAIL = 256

HUBER_BETA = 2.0
CLIP_NORM = 0.05
LEARN_RATE = 0.08
FIRST_DECAY = 0.9
SECOND_DECAY = 0.999
WEIGHT_DECAY = 0.05
ADAM_EPSILON = 1e-08
NORM_EPSILON = 1e-06
INSTANCE_EPSILON = 1e-05
LOW = jnp.bfloat16
F32 = jnp.float32


def flip(size, bit):
    return [(i, i ^ bit) for i in range(size)]


def swap(value, axis, bit):
    return lax.ppermute(value, axis, flip(lax.axis_size(axis), bit))


def over_link(value):
    return lax.ppermute(value, "dp", [(i, i ^ (4 if i & 1 else 2)) for i in range(8)])


def over_other(value):
    return lax.ppermute(value, "dp", [(i, i ^ (2 if i & 1 else 4)) for i in range(8)])


def blocks_of(me):
    link = jnp.where(me & 1 == 1, 4, 2)
    other = 6 - link
    return jnp.stack([me, me ^ 1, me ^ link, me ^ link ^ 1, me ^ 6, me ^ other ^ 1, me ^ other, me ^ 7])


def gather_part(shard, after=None):
    if lax.axis_size("dp") != 8:
        return [lax.all_gather(shard, "dp", axis=0, tiled=True)]
    twin = swap(shard, "dp", 1)
    first, second = over_link(shard), over_link(twin)
    diagonal = over_other(first if after is None else copied(first, after))
    return [shard, twin, first, second, diagonal] + [swap(piece, "dp", 1) for piece in (first, second, diagonal)]


def arrived(pieces, *indices):
    return [pieces[index] for index in indices] if len(pieces) > 1 else []


class Steps:
    def __init__(self):
        self.made = {}
        self.plain = lax.axis_size("dp") != 8 or lax.axis_size("layer") != 4

    def step(self, name, make):
        if self.plain:
            return []
        if name not in self.made:
            self.made[name] = list(make())
        return self.made[name]


class Part(Steps):
    def __init__(self, grads):
        super().__init__()
        self.grads = grads

    def core(self):
        return self.step("core", lambda: [swap(self.grads[2], "dp", 1)])

    def sums(self, after=()):
        def make():
            plan = [[[(0, block), (1, block)]] for block in range(3)]
            return add([self.grads[1], *self.core()], plan, [F32, LOW, LOW], after)

        return self.step("sums", make)

    def crossed(self):
        def make():
            _, second, diagonal = self.sums()
            return [over_other(diagonal), over_link(second)]

        return self.step("crossed", make)


    def sums_out(self, after=()):
        def make():
            diagonal, second = self.crossed()
            arrays = [self.sums()[0], diagonal, self.grads[0], second]
            return add(arrays, [[[(0, None), (1, None)]], [[(2, 1), (3, None)]]], [LOW, LOW], after)

        return self.step("sums_out", make)

    def last(self):
        def make():
            ahead, twin = self.sums_out()
            return [over_link(ahead), swap(twin, "dp", 1)]

        return self.step("last", make)

    def terms(self):
        return [1, self.grads[0], *self.last()]


def blocks_by_chip(me):
    chips, core = 2 * jnp.arange(4), me & 1
    return jnp.concatenate([chips + core, chips + 1 - core])


class Direct(Steps):
    def __init__(self, grads):
        super().__init__()
        self.grads = grads

    def core(self):
        return self.step("core", lambda: [swap(self.grads[1], "dp", 1)])

    def sums(self, after=()):
        return self.step("sums", lambda: [pair_sums(self.grads[0], *self.core(), after)])

    def last(self):
        groups = [[0, 2, 4, 6], [1, 3, 5, 7]]
        spread = functools.partial(lax.all_to_all, axis_name="dp", split_axis=0, concat_axis=0)
        return self.step("last", lambda: [spread(*self.sums(), axis_index_groups=groups, tiled=True)])

    def terms(self):
        return [4, *self.last()]


class Owned(Steps):
    def __init__(self, parts, by_halves):
        super().__init__()
        self.parts, self.by_halves = parts, by_halves
        self.place = lax.axis_index("layer")

    def shares(self, after=()):
        def make():
            if self.by_halves:
                return share_halves((self.place & 1)[None], [part.terms() for part in self.parts], after)
            terms = self.parts[0].terms()[1:]
            plan = [[[(0, 0), (1, None), (2, None)]]] * 2
            return add(terms, plan, [F32, LOW], after)

        return self.step("shares", make)

    def near(self):
        def make():
            sent = self.shares()[1]
            if self.by_halves:
                return [swap(sent, "layer", 1)]
            return [lax.ppermute(sent, "layer", [(0, 1), (3, 2)])]

        return self.step("near", make)

    def pairs(self, after=()):
        plan = [[[(0, None), (1, None)]]]
        return self.step("pairs", lambda: add([self.shares()[0], *self.near()], plan, [LOW], after))

    def far(self):
        def make():
            if self.by_halves:
                return [swap(*self.pairs(), "layer", 2)]
            return [lax.ppermute(*self.pairs(), "layer", [(1, 2), (2, 1)])]

        return self.step("far", make)

    def sum_all(self, after=()):
        plan = [[[(0, None), (1, None)]]]
        return self.step("all", lambda: add([*self.pairs(), *self.far()], plan, [LOW], after))

    def back(self):
        def make():
            if self.by_halves:
                return [swap(*self.sum_all(), "layer", 1)]
            return [lax.ppermute(*self.sum_all(), "layer", [(1, 0), (2, 3)])]

        return self.step("back", make)

    def scattered(self):
        grads = [part.grads[0].reshape(D, -1) for part in self.parts]
        shares = [lax.psum_scatter(grad, "dp", scatter_dimension=0, tiled=True) for grad in grads]
        return jnp.concatenate(shares, axis=1)

    def total(self):
        if self.plain:
            return lax.psum(self.scattered(), "layer").astype(F32)
        (mine,), (other,) = self.sum_all(), self.back()
        if not self.by_halves:
            return jnp.where((self.place == 1) | (self.place == 2), mine, other).astype(F32)
        even = self.place & 1 == 0
        halves = [jnp.where(even, mine, other), jnp.where(even, other, mine)]
        return jnp.concatenate(halves, axis=0).astype(F32)


def layer_sums(*owned):
    lows = [one.shares()[1] if not one.plain else one.scattered() for one in owned]
    return [total.astype(F32) for total in lax.psum(tuple(lows), "layer")]


def gathered_sum(value, axes):
    size = lax.axis_size(axes)
    sent = jnp.broadcast_to(value, (size, *value.shape))
    return jnp.sum(lax.all_to_all(sent, axes, split_axis=0, concat_axis=0), axis=0)
NAT = 208
TILE = 256
CHUNK = 48
SPARE_VMEM = 6 * 2**20
COST_TEACHER = 1
HEAVY = 2.5e9
ROW = pl.BlockSpec(memory_space=pltpu.VMEM)
FAR = pl.BlockSpec(memory_space=pl.ANY)
NUMBERS = pl.BlockSpec(memory_space=pltpu.SMEM)


def late(dims, dtype):
    return pltpu.HBM(dims, dtype)


def shape(dims, dtype):
    return jax.ShapeDtypeStruct(dims, dtype)


def launch(kernel, us, in_specs, out_specs, out_shape, scratch_shapes=(), grid=(), prefetch=0, after=()):
    def call(*args):
        count = len(args)

        def body(*refs):
            kernel(*refs[:count], *refs[count + len(after) :])

        held = sum(
            math.prod(ref.shape) * jnp.dtype(ref.dtype).itemsize
            for ref in scratch_shapes
            if jnp.issubdtype(ref.dtype, jnp.floating)
        )
        spec = pltpu.PrefetchScalarGridSpec(
            num_scalar_prefetch=prefetch,
            grid=grid,
            in_specs=list(in_specs) + [FAR] * len(after),
            out_specs=out_specs,
            scratch_shapes=list(scratch_shapes),
        )
        return pl.pallas_call(
            body,
            grid_spec=spec,
            out_shape=out_shape,
            compiler_params=pltpu.CompilerParams(vmem_limit_bytes=held + SPARE_VMEM),
            cost_estimate=pl.CostEstimate(flops=int(us * HEAVY), bytes_accessed=1 << 20 if us else 1, transcendentals=0),
        )(*args, *after)

    return call


def dot(left, right):
    return jnp.dot(left, right, preferred_element_type=F32)


def dot_t(left, right):
    return lax.dot_general(left, right, (((1,), (1,)), ((), ())), preferred_element_type=F32)


def t_dot(left, right):
    return lax.dot_general(left, right, (((0,), (0,)), ((), ())), preferred_element_type=F32)


def fetch(order, pieces, weight, sems, columns=None):
    rows = pieces[0].shape[0]
    copies = []
    for index, piece in enumerate(pieces):
        source = piece if columns is None else piece.at[:, columns]
        at = pl.multiple_of(order[index] * rows, 16 if rows % 16 == 0 else 8)
        copies.append(pltpu.make_async_copy(source, weight.at[pl.ds(at, rows)], sems.at[index]))
    for copy in copies:
        copy.start()
    return copies


def wait_all(copies):
    for copy in copies:
        copy.wait()


def one_hot(masked, count, rows):
    patch = lax.broadcasted_iota(jnp.int32, (rows, MOST), 0)
    slot = lax.broadcasted_iota(jnp.int32, (rows, MOST), 1)
    return jnp.where((masked[:, :MOST] == patch) & (slot < count), 1.0, 0.0)


def normed_with(values):
    mean = jnp.mean(values, axis=-1, keepdims=True)
    centered = values - mean
    inv_std = lax.rsqrt(jnp.mean(centered * centered, axis=-1, keepdims=True) + NORM_EPSILON)
    lane = lax.broadcasted_iota(jnp.int32, (1, 128), 1)
    return centered * inv_std, jnp.where(lane == 0, mean, inv_std)


def normed(values):
    centered = values - jnp.mean(values, axis=-1, keepdims=True)
    inv_std = lax.rsqrt(jnp.mean(centered * centered, axis=-1, keepdims=True) + NORM_EPSILON)
    return centered * inv_std, inv_std


def norm_in(grad_in, hat, inv_std, gain):
    scaled = grad_in * gain
    return inv_std * (
        scaled
        - jnp.mean(scaled, axis=-1, keepdims=True)
        - hat * jnp.mean(scaled * hat, axis=-1, keepdims=True)
    )


def wide(column):
    return jnp.broadcast_to(column, (column.shape[0], 128))


def folded(values):
    return jnp.sum(values.reshape(-1, 8, values.shape[-1]), axis=0)


def total_row(values):
    return jnp.sum(values, axis=0, keepdims=True)


def split_store(outs, columns, grad):
    rows = outs[0].shape[1]
    low = grad.astype(LOW)
    at = 0
    for out in outs:
        for index in range(out.shape[0]):
            out[index, :, columns] = low[at : at + rows]
            at += rows


def split_shapes(blocks, columns, counts=(2, 3, 3)):
    if blocks == 1:
        counts = (1,)
    return [shape((count, D // blocks, columns), LOW) for count in counts]


def teacher_kernel(counts, teacher, masked, out):
    for index in range(teacher.shape[0]):
        pick = one_hot(masked[index], counts[index], P_SIZE).astype(LOW)
        rows = slice(index * MOST, (index + 1) * MOST)
        for at in range(0, D, TILE):
            low = teacher[index, :, at : at + TILE]
            values = low.astype(F32)
            mean = jnp.sum(values, axis=0, keepdims=True) * (1.0 / P_SIZE)
            centered = values - mean
            square = jnp.sum(centered * centered, axis=0, keepdims=True) * (1.0 / P_SIZE)
            inv = lax.rsqrt(square + INSTANCE_EPSILON)
            out[rows, at : at + TILE] = ((t_dot(pick, low) - mean) * inv).astype(LOW)


def teacher_rows(teacher, masks, block, after=()):
    images = masks.shape[0]
    return launch(
        teacher_kernel,
        COST_TEACHER,
        in_specs=[NUMBERS, ROW, ROW],
        out_specs=ROW,
        out_shape=shape((images * MOST, D), LOW),
        after=after,
    )(masks[:, P_SIZE], lax.dynamic_slice_in_dim(teacher, block * images, images), masks[:, None, :P_SIZE])


def part_kernel(spans, *refs):
    ins, out = refs[: len(spans)], refs[-1]
    at = 0
    for (source, start, size, *room), ref in zip(spans, ins):
        out[:, at : at + size] = ref[:, start : start + size].astype(LOW)
        at += size
        if room:
            out[:, at : at + room[0] - size] = jnp.zeros((out.shape[0], room[0] - size), LOW)
            at += room[0] - size


def part(spans, after=()):
    rows = spans[0][0].shape[0]
    return launch(
        functools.partial(part_kernel, spans),
        0.2,
        in_specs=[ROW] * len(spans),
        out_specs=ROW,
        out_shape=shape((rows, sum(span[-1] for span in spans)), LOW),
        after=after,
    )(*[span[0] for span in spans])


def embed_kernel(owners, order, counts, pixels, masked, *refs):
    pieces, refs = refs[:owners], refs[owners:]
    hat, inv, rows_in, position, vectors, hat_tab, inv_tab, tab_in, weight, sems = refs
    step = pl.program_id(0)

    @pl.when(step == 0)
    def _():
        wait_all(fetch(order, pieces, weight, sems, pl.ds(0, D + TAIL)))
        small = weight[:, D:].astype(F32).T
        vectors[...] = small[P_SIZE : P_SIZE + vectors.shape[0]]
        rows = small[:P_SIZE]
        zeros = jnp.zeros((NAT - P_SIZE, D), F32)
        position[...] = jnp.concatenate([rows, zeros], axis=0).astype(LOW)
        table, table_inv = normed(rows + small[P_SIZE + 14 : P_SIZE + 15])
        hat_tab[...] = jnp.concatenate([table, zeros], axis=0)
        inv_tab[...] = jnp.concatenate([wide(table_inv), zeros[:, :128]], axis=0)
        table = table * small[P_SIZE : P_SIZE + 1] + small[P_SIZE + 1 : P_SIZE + 2]
        tab_in[...] = jnp.concatenate([table, zeros], axis=0).astype(LOW)

    flag = jnp.sum(one_hot(masked[0], counts[step], P_SIZE), axis=1, keepdims=True)
    embedded = dot(pixels[0], weight[:, :D]) + vectors[13:14]
    start = flag * vectors[14:15] + (1.0 - flag) * embedded + position[...].astype(F32)[:P_SIZE]
    value, value_inv = normed(start)
    zeros = jnp.zeros((NAT - P_SIZE, D), F32)
    hat[0] = jnp.concatenate([value, zeros], axis=0)
    inv[0] = jnp.concatenate([wide(value_inv), zeros[:, :128]], axis=0)
    value = value * vectors[0:1] + vectors[1:2]
    rows_in[0] = jnp.concatenate([value, zeros], axis=0).astype(LOW)


def embed(order, counts, pixels, masked, pieces, after=()):
    images, owners = pixels.shape[0], len(pieces)
    whole = lambda *dims: pl.BlockSpec(dims, lambda i, order, counts: (0,) * len(dims))
    image = lambda *dims: pl.BlockSpec((1, *dims), lambda i, order, counts: (i,) + (0,) * len(dims))
    return launch(
        functools.partial(embed_kernel, owners),
        1,
        prefetch=2,
        grid=(images,),
        in_specs=[image(P_SIZE, PIX), image(1, P_SIZE)] + [FAR] * owners,
        out_specs=[
            image(NAT, D),
            image(NAT, 128),
            image(NAT, D),
            whole(NAT, D),
            whole(24, D),
            whole(NAT, D),
            whole(NAT, 128),
            whole(NAT, D),
        ],
        scratch_shapes=[pltpu.VMEM((D, D + TAIL), LOW), pltpu.SemaphoreType.DMA((owners,))],
        out_shape=[
            late((images, NAT, D), F32),
            late((images, NAT, 128), F32),
            shape((images, NAT, D), LOW),
            shape((NAT, D), LOW),
            shape((24, D), F32),
            late((NAT, D), F32),
            late((NAT, 128), F32),
            shape((NAT, D), LOW),
        ],
        after=after,
    )(order, counts, pixels, masked, *pieces)


def halves(pair):
    lane = lax.broadcasted_iota(jnp.int32, (1, 128), 1)
    first = jnp.where(lane < HD, 1.0, 0.0).astype(LOW)
    return jnp.concatenate([pair * first, pair * (1.0 - first.astype(F32)).astype(LOW)], axis=0)


def merged(both):
    lane = lax.broadcasted_iota(jnp.int32, (MOST, 128), 1)
    return jnp.where(lane < HD, both[:MOST], both[MOST:])


def attention_kernel(owners, order, counts, rows_in, masked, tab_in, vectors, *refs):
    pieces, refs = refs[:owners], refs[owners:]
    kv, queries, heads, weight, table, sems = refs
    step = pl.program_id(0)

    @pl.when(step == 0)
    def _():
        wait_all(fetch(order, pieces, weight, sems, pl.ds(D + TAIL, 3 * D)))
        table[...] = (dot(tab_in[...], weight[:, :D]) + vectors[2:3]).astype(LOW)

    kv[0, :, :D] = dot(rows_in[0], weight[:, D : 2 * D]).astype(LOW)
    kv[0, :, D:] = (dot(rows_in[0], weight[:, 2 * D :]) + vectors[3:4]).astype(LOW)
    pick = one_hot(masked[0], counts[step], NAT).astype(LOW)
    queries[0] = t_dot(pick, table[...]).astype(LOW)
    key_index = lax.broadcasted_iota(jnp.int32, (1, NAT), 1)
    for at in range(0, D, 128):
        pair = halves(queries[0, :, at : at + 128]) * jnp.asarray(1.0 / math.sqrt(HD), LOW)
        scores = dot_t(pair, kv[0, :, at : at + 128])
        scores = jnp.where(key_index < P_SIZE, scores, -1e30)
        shifted = jnp.exp(scores - jnp.max(scores, axis=1, keepdims=True))
        probs = (shifted * (1.0 / jnp.sum(shifted, axis=1, keepdims=True))).astype(LOW)
        heads[0, :, at : at + 128] = merged(dot(probs, kv[0, :, D + at : D + at + 128])).astype(LOW)


def attention(order, counts, rows_in, masked, tab_in, vectors, pieces, after=()):
    images, owners = rows_in.shape[0], len(pieces)
    whole = lambda *dims: pl.BlockSpec(dims, lambda i, order, counts: (0,) * len(dims))
    image = lambda *dims: pl.BlockSpec((1, *dims), lambda i, order, counts: (i,) + (0,) * len(dims))
    return launch(
        functools.partial(attention_kernel, owners),
        12,
        prefetch=2,
        grid=(images,),
        in_specs=[image(NAT, D), image(1, P_SIZE), whole(NAT, D), whole(24, D)] + [FAR] * owners,
        out_specs=[image(NAT, 2 * D), image(MOST, D), image(MOST, D)],
        scratch_shapes=[
            pltpu.VMEM((D, 3 * D), LOW),
            pltpu.VMEM((NAT, D), LOW),
            pltpu.SemaphoreType.DMA((owners,)),
        ],
        out_shape=[late((images, NAT, 2 * D), LOW), late((images, MOST, D), LOW), shape((images, MOST, D), LOW)],
        after=after,
    )(order, counts, rows_in, masked, tab_in, vectors, *pieces)


def chunks(count, body):
    lax.fori_loop(0, count, lambda k, _: (body(k), 0)[1], 0, unroll=3)


def at_chunk(k, rows=CHUNK):
    return pl.ds(pl.multiple_of(k * rows, 16), rows)


def gelu_parts(value):
    size = jnp.abs(value) * math.sqrt(0.5)
    t = 1.0 / (1.0 + 0.3275911 * size)
    bell = jnp.exp(-size * size)
    poly = t * (0.254829592 + t * (-0.284496736 + t * (1.421413741 + t * (-1.453152027 + t * 1.061405429))))
    below = 0.5 * poly * bell
    share = jnp.where(value < 0, below, 1.0 - below)
    return value * share, share + value * bell * (1.0 / math.sqrt(2.0 * math.pi))


def mid_kernel(owners, images, order, counts, masked, heads, position, vectors, *refs):
    pieces, refs = refs[:owners], refs[owners:]
    attn, hidden, stats, rows_in, weight, sems = refs
    copies = fetch(order, pieces, weight, sems, pl.ds(0, D))
    for index in range(images):
        pick = one_hot(masked[index], counts[index], NAT).astype(LOW)
        hidden[index * MOST : (index + 1) * MOST] = t_dot(pick, position[...]) + vectors[14:15]
    wait_all(copies)
    for at in range(0, D, TILE):
        attn[:, at : at + TILE] = dot(heads[...], weight[:, at : at + TILE])

    def first(k):
        rows = at_chunk(k)
        branch = attn[rows] + vectors[4:5]
        attn[rows] = branch
        value = hidden[rows] + vectors[5:6] * branch
        hidden[rows] = value
        value, stats[rows] = normed_with(value)
        rows_in[rows] = (value * vectors[6:7] + vectors[7:8]).astype(LOW)

    chunks(hidden.shape[0] // CHUNK, first)


def mid(order, counts, masked, heads, position, vectors, pieces, after=()):
    rows, owners = heads.shape[0], len(pieces)
    return launch(
        functools.partial(mid_kernel, owners, masked.shape[0]),
        6,
        in_specs=[NUMBERS, NUMBERS] + [ROW] * 4 + [FAR] * owners,
        out_specs=[ROW] * 4,
        out_shape=[
            shape((rows, D), F32),
            shape((rows, D), F32),
            shape((rows, 128), F32),
            shape((rows, D), LOW),
        ],
        scratch_shapes=[pltpu.VMEM((D, D), LOW), pltpu.SemaphoreType.DMA((owners,))],
        after=after,
    )(order, counts, masked, heads, position, vectors, *pieces)


def up_kernel(owners, first, order, rows_in, vectors, *refs):
    pieces, refs = refs[:owners], refs[owners:]
    active, slope, weight, pre_a, pre_b, sems = refs
    wait_all(fetch(order, pieces, weight, sems, pl.ds(D + first, active.shape[1])))

    def product(tile, into):
        into[...] = dot(rows_in[...], weight[:, pl.ds(pl.multiple_of(tile * TILE, TILE), TILE)])

    def finish(tile, source):
        columns = pl.ds(pl.multiple_of(tile * TILE, TILE), TILE)
        part = D // TILE
        row = 15 + first // D + tile // part
        bias = vectors[pl.ds(row, 1), pl.ds(pl.multiple_of((tile % part) * TILE, TILE), TILE)]
        for start in range(0, source.shape[0], 48):
            value, down = gelu_parts(source[start : start + 48] + bias)
            active[start : start + 48, columns] = value.astype(LOW)
            slope[start : start + 48, columns] = down.astype(LOW)

    tiles = active.shape[1] // TILE
    product(0, pre_a)

    def pair(k):
        product(2 * k + 1, pre_b)
        finish(2 * k, pre_a)
        product(jnp.minimum(2 * k + 2, tiles - 1), pre_a)
        finish(2 * k + 1, pre_b)

    chunks(tiles // 2, pair)


def up(first, columns, order, rows_in, vectors, pieces, after=()):
    rows, owners = rows_in.shape[0], len(pieces)
    return launch(
        functools.partial(up_kernel, owners, first),
        7,
        in_specs=[NUMBERS] + [ROW] * 2 + [FAR] * owners,
        out_specs=[ROW] * 2,
        out_shape=[shape((rows, columns), LOW)] * 2,
        scratch_shapes=[
            pltpu.VMEM((D, columns), LOW),
            pltpu.VMEM((rows, TILE), F32),
            pltpu.VMEM((rows, TILE), F32),
            pltpu.SemaphoreType.DMA((owners,)),
        ],
        after=after,
    )(order, rows_in, vectors, *pieces)


def place(order, source, turned, scratch):
    blocks = order.shape[0]
    if blocks == 1:
        turned[...] = source.T
        return
    rows = D // blocks
    scratch[...] = source.T
    for index in range(blocks):
        at = pl.multiple_of(order[index] * rows, 16 if rows % 16 == 0 else 8)
        turned[index * rows : (index + 1) * rows] = scratch[pl.ds(at, rows)]


def head_kernel(owners, order, active_a, active_b, hidden, vectors, *refs):
    pieces, refs = refs[:owners], refs[owners:]
    branch, stats, rows_in, work, weight, sems = refs
    wait_all(fetch(order, pieces, weight, sems))
    half = active_a.shape[1]
    for at in range(0, D, TILE):
        rows = slice(at, at + TILE)
        value = dot_t(active_a[...], weight[rows, :half])
        branch[:, rows] = value + dot_t(active_b[...], weight[rows, half:FF])

    def first(k):
        rows = at_chunk(k)
        value = branch[rows] + vectors[8:9]
        branch[rows] = value
        value, stats[rows] = normed_with(hidden[rows] + vectors[9:10] * value)
        rows_in[rows] = (value * vectors[10:11] + vectors[11:12]).astype(LOW)

    chunks(hidden.shape[0] // CHUNK, first)
    for at in range(0, D, TILE):
        work[:, at : at + TILE] = dot(rows_in[...], weight[:, FF + at : FF + at + TILE])


def head(order, active, hidden, vectors, pieces, after=()):
    rows, owners = hidden.shape[0], len(pieces)
    return launch(
        functools.partial(head_kernel, owners),
        10,
        in_specs=[NUMBERS] + [ROW] * 4 + [FAR] * owners,
        out_specs=[ROW] * 4,
        out_shape=[
            shape((rows, D), F32),
            shape((rows, 128), F32),
            shape((rows, D), LOW),
            shape((rows, D), F32),
        ],
        scratch_shapes=[pltpu.VMEM((D, FF + D), LOW), pltpu.SemaphoreType.DMA((owners,))],
        after=after,
    )(order, *active, hidden, vectors, *pieces)


def down_kernel(owners, parts, order, counts, work, stats, hidden, branch, active_a, active_b, vectors, rows_in, *refs):
    targets, pieces, refs = refs[:parts], refs[parts : parts + owners], refs[parts + owners :]
    outs = 3 if owners > 1 else 1
    grads = refs[:outs]
    loss, head_sums, grad, grad_low, sums, weight, error_low, turned, spare, sems = refs[outs:]
    copies = fetch(order, pieces, weight, sems, pl.ds(FF, D))
    head_sums[...] = jnp.zeros_like(head_sums)
    sums[...] = jnp.zeros_like(sums)
    steps = grad.shape[0] // CHUNK

    def errors(k):
        rows = at_chunk(k)
        target = targets[0][rows].astype(F32)
        for other in targets[1:]:
            target = target + other[rows].astype(F32)
        error = work[rows] + vectors[12:13] - target * (1.0 / lax.axis_size("layer"))
        size = jnp.abs(error)
        entry = jnp.where(size < HUBER_BETA, error * error * (0.5 / HUBER_BETA), size - 0.5 * HUBER_BETA)
        per_image = MOST // CHUNK
        row = lax.broadcasted_iota(jnp.int32, (CHUNK, 1), 0) + lax.rem(k, per_image) * CHUNK
        flag = row < counts[k // per_image]
        head_sums[0] += folded(jnp.where(flag, entry, 0.0))
        value = jnp.where(flag, jnp.clip(error * (1.0 / HUBER_BETA), -1.0, 1.0), 0.0)
        head_sums[1] += folded(value)
        error_low[rows] = value.astype(LOW)

    chunks(steps, errors)
    loss[0, 0] = jnp.sum(head_sums[0])
    wait_all(copies)
    for at in range(0, D, TILE):
        grad[:, at : at + TILE] = dot_t(error_low[...], weight[at : at + TILE])

    def back(k):
        rows = at_chunk(k)
        grad_in, branch_rows = grad[rows], branch[rows]
        block = hidden[rows] + vectors[9:10] * branch_rows
        value = (block - stats[rows, :1]) * stats[rows, 1:2]
        sums[0] += folded(grad_in * value)
        sums[1] += folded(grad_in)
        value = norm_in(grad_in, value, stats[rows, 1:2], vectors[10:11])
        grad[rows] = value
        sums[2] += folded(value * branch_rows)
        value = value * vectors[9:10]
        sums[3] += folded(value)
        grad_low[rows] = value.astype(LOW)

    chunks(steps, back)
    place(order, grad_low[...], turned, spare)
    half = active_a.shape[1]
    for at in range(0, FF, TILE):
        source = active_a[:, at : at + TILE] if at < half else active_b[:, at - half : at - half + TILE]
        split_store(grads, slice(at, at + TILE), dot(turned[...], source))
    place(order, rows_in[...], turned, spare)
    for at in range(0, D, TILE):
        columns = slice(FF + at, FF + at + TILE)
        split_store(grads, columns, dot(turned[...], error_low[:, at : at + TILE]))


def down(order, counts, work, stats, hidden, branch, active, vectors, rows_in, targets, pieces, after=()):
    rows, owners = hidden.shape[0], len(pieces)
    grads = split_shapes(owners, FF + D)
    return launch(
        functools.partial(down_kernel, owners, len(targets)),
        15,
        in_specs=[NUMBERS, NUMBERS] + [ROW] * (8 + len(targets)) + [FAR] * owners,
        out_specs=[ROW] * len(grads) + [NUMBERS] + [ROW] * 4,
        out_shape=grads
        + [
            shape((1, 1), F32),
            shape((2, 8, D), F32),
            shape((rows, D), F32),
            shape((rows, D), LOW),
            shape((4, 8, D), F32),
        ],
        scratch_shapes=[
            pltpu.VMEM((D, D), LOW),
            pltpu.VMEM((rows, D), LOW),
            pltpu.VMEM((D, rows), LOW),
            pltpu.VMEM((D, rows), LOW),
            pltpu.SemaphoreType.DMA((owners,)),
        ],
        after=after,
    )(order, counts, work, stats, hidden, branch, *active, vectors, rows_in, *targets, *pieces)


def pre_kernel(owners, order, grad_low, slope_a, slope_b, rows_in, *refs):
    pieces, refs = refs[:owners], refs[owners:]
    outs = 3 if owners > 1 else 1
    grads = refs[:outs]
    pre_low, bias, weight, turned, spare, sems = refs[outs:]
    copies = fetch(order, pieces, weight, sems, pl.ds(0, FF))
    place(order, rows_in[...], turned, spare)
    wait_all(copies)

    half = slope_a.shape[1]
    for at in range(0, FF, TILE):
        columns = slice(at, at + TILE)
        slope, start = (slope_a, at) if at < half else (slope_b, at - half)
        value = dot(grad_low[...], weight[:, columns]) * slope[:, start : start + TILE].astype(F32)
        bias[:, columns] = folded(value)
        pre_low[:, columns] = value.astype(LOW)
        split_store(grads, columns, dot(turned[...], pre_low[:, columns]))


def pre(order, grad_low, slope, rows_in, pieces, after=()):
    rows, owners = grad_low.shape[0], len(pieces)
    grads = split_shapes(owners, FF)
    return launch(
        functools.partial(pre_kernel, owners),
        12,
        in_specs=[NUMBERS] + [ROW] * 4 + [FAR] * owners,
        out_specs=[ROW] * (len(grads) + 2),
        out_shape=grads + [shape((rows, FF), LOW), shape((8, FF), F32)],
        scratch_shapes=[
            pltpu.VMEM((D, FF), LOW),
            pltpu.VMEM((D, rows), LOW),
            pltpu.VMEM((D, rows), LOW),
            pltpu.SemaphoreType.DMA((owners,)),
        ],
        after=after,
    )(order, grad_low, *slope, rows_in, *pieces)


def out_kernel(owners, images, order, counts, masked, pre_low, grad, stats, hidden, attn, vectors, *refs):
    pieces, refs = refs[:owners], refs[owners:]
    heads_grad, table, sums, attn_low, weight, work, high, rest, sems = refs
    wait_all(fetch(order, pieces, weight, sems))
    for at in range(0, D, TILE):
        work[:, at : at + TILE] = dot_t(pre_low[...], weight[at : at + TILE, D:])
    sums[...] = jnp.zeros_like(sums)

    def back(k):
        rows = at_chunk(k)
        grad_in = work[rows]
        value = (hidden[rows] - stats[rows, :1]) * stats[rows, 1:2]
        sums[0] += folded(grad_in * value)
        sums[1] += folded(grad_in)
        value = grad[rows] + norm_in(grad_in, value, stats[rows, 1:2], vectors[6:7])
        low = value.astype(LOW)
        high[rows] = low
        rest[rows] = (value - low.astype(F32)).astype(LOW)
        sums[2] += folded(value * attn[rows])
        value = value * vectors[5:6]
        sums[3] += folded(value)
        attn_low[rows] = value.astype(LOW)

    chunks(work.shape[0] // CHUNK, back)
    for at in range(0, D, TILE):
        heads_grad[:, at : at + TILE] = dot_t(attn_low[...], weight[at : at + TILE, :D]).astype(LOW)
    for index in range(images):
        pick = one_hot(masked[index], counts[index], NAT).astype(LOW)
        rows = slice(index * MOST, (index + 1) * MOST)
        value = dot(pick, high[rows]) + dot(pick, rest[rows])
        table[...] = value if index == 0 else table[...] + value


def out_back(order, counts, masked, pre_low, grad, stats, hidden, attn, vectors, pieces, after=()):
    rows, owners = grad.shape[0], len(pieces)
    return launch(
        functools.partial(out_kernel, owners, masked.shape[0]),
        14,
        in_specs=[NUMBERS, NUMBERS] + [ROW] * 7 + [FAR] * owners,
        out_specs=[ROW] * 4,
        out_shape=[shape((rows, D), LOW), shape((NAT, D), F32), shape((4, 8, D), F32), shape((rows, D), LOW)],
        scratch_shapes=[
            pltpu.VMEM((D, D + FF), LOW),
            pltpu.VMEM((rows, D), F32),
            pltpu.VMEM((rows, D), LOW),
            pltpu.VMEM((rows, D), LOW),
            pltpu.SemaphoreType.DMA((owners,)),
        ],
        after=after,
    )(order, counts, masked, pre_low, grad, stats, hidden, attn, vectors, *pieces)


def attention_back_kernel(counts, queries, kv, heads_grad, masked, kv_low, table, sums, query_low):
    step = pl.program_id(0)

    @pl.when(step == 0)
    def _():
        table[...] = jnp.zeros_like(table)
        sums[...] = jnp.zeros_like(sums)

    scale = 1.0 / math.sqrt(HD)
    key_index = lax.broadcasted_iota(jnp.int32, (NAT, 1), 0)
    for at in range(0, D, 128):
        lanes = slice(at, at + 128)
        high = slice(D + at, D + at + 128)
        pair = halves(queries[0, :, lanes]) * jnp.asarray(scale, LOW)
        grad = halves(heads_grad[0, :, lanes])
        keys, values = kv[0, :, lanes], kv[0, :, high]
        scores = jnp.where(key_index < P_SIZE, dot_t(keys, pair), -1e30)
        shifted = jnp.exp(scores - jnp.max(scores, axis=0, keepdims=True))
        probs = shifted * (1.0 / jnp.sum(shifted, axis=0, keepdims=True))
        prob_grad = dot_t(values, grad)
        value_grad = dot(probs.astype(LOW), grad).astype(LOW)
        kv_low[0, :, high] = value_grad
        sums[1, :, lanes] += folded(value_grad.astype(F32))
        inner = jnp.sum(probs * prob_grad, axis=0, keepdims=True)
        score_grad = (probs * (prob_grad - inner)).astype(LOW)
        kv_low[0, :, lanes] = dot(score_grad, pair).astype(LOW)
        query_grad = merged(t_dot(score_grad, keys) * scale).astype(LOW)
        query_low[:, lanes] = query_grad
        sums[0, :, lanes] += folded(query_grad.astype(F32))
    pick = one_hot(masked[0], counts[step], NAT).astype(LOW)
    table[...] += dot(pick, query_low[...])


def attention_back(counts, queries, kv, heads_grad, masked, after=()):
    images = kv.shape[0]
    whole = lambda *dims: pl.BlockSpec(dims, lambda i, counts: (0,) * len(dims))
    image = lambda *dims: pl.BlockSpec((1, *dims), lambda i, counts: (i,) + (0,) * len(dims))
    return launch(
        attention_back_kernel,
        15,
        prefetch=1,
        grid=(images,),
        in_specs=[image(MOST, D), image(NAT, 2 * D), image(MOST, D), image(1, P_SIZE)],
        out_specs=[image(NAT, 2 * D), whole(NAT, D), whole(2, 8, D)],
        scratch_shapes=[pltpu.VMEM((MOST, D), LOW)],
        out_shape=[shape((images, NAT, 2 * D), LOW), shape((NAT, D), F32), shape((2, 8, D), F32)],
        after=after,
    )(counts, queries, kv, heads_grad, masked)


def high_rest(value):
    high = value.astype(LOW)
    return jnp.concatenate([high, (value - high.astype(F32)).astype(LOW)], axis=0)


def qkv_kernel(blocks, order, rows_in, kv_low, tab_in, table, heads, attn_low, *refs):
    outs = 3 if blocks > 1 else 1
    grads = refs[:outs]
    turned, spare, tab_turned, tab_spare, heads_turned, heads_spare = refs[outs:]
    place(order, heads[...], heads_turned, heads_spare)
    for at in range(0, D, TILE):
        columns = slice(3 * D + at, 3 * D + at + TILE)
        split_store(grads, columns, dot(heads_turned[...], attn_low[:, at : at + TILE]))
    place(order, tab_in[...], tab_turned, tab_spare)
    both = high_rest(table[...])
    twice = jnp.concatenate([tab_turned[...], tab_turned[...]], axis=1)
    for at in range(0, D, TILE):
        split_store(grads, slice(at, at + TILE), dot(twice, both[:, at : at + TILE]))
    place(order, rows_in[...], turned, spare)

    for at in range(0, 2 * D, TILE):
        split_store(grads, slice(D + at, D + at + TILE), dot(turned[...], kv_low[:, at : at + TILE]))


def qkv_back(order, rows_in, kv_low, tab_in, table, heads, attn_low, after=()):
    blocks, rows = order.shape[0], rows_in.shape[0]
    grads = split_shapes(blocks, 4 * D)
    return launch(
        functools.partial(qkv_kernel, blocks),
        7,
        in_specs=[NUMBERS] + [ROW] * 6,
        out_specs=[ROW] * len(grads),
        out_shape=grads,
        scratch_shapes=[
            pltpu.VMEM((D, rows), LOW),
            pltpu.VMEM((D, rows), LOW),
            pltpu.VMEM((D, NAT), LOW),
            pltpu.VMEM((D, NAT), LOW),
            pltpu.VMEM((D, heads.shape[0]), LOW),
            pltpu.VMEM((D, heads.shape[0]), LOW),
        ],
        after=after,
    )(order, rows_in, kv_low, tab_in, table, heads, attn_low)


def start_kernel(owners, images, order, counts, masked, kv_low, table, hidden_tab, hat, inv, hat_tab, inv_tab, vectors, head_sums, down_sums, up_bias, out_sums, qkv_sums, *refs):
    pieces, refs = refs[:owners], refs[owners:]
    start_low, small_low, weight, work, small, sums, sems = refs
    copies = fetch(order, pieces, weight, sems, pl.ds(D + TAIL, 3 * D))
    wait_all(copies)
    for at in range(0, D, TILE):
        work[:, at : at + TILE] = dot_t(kv_low[...], weight[at : at + TILE, D:])
    both = high_rest(table[...])
    tab_in = dot_t(both, weight[:, :D])
    tab_in = tab_in[:NAT] + tab_in[NAT:]
    gain = vectors[0:1]
    sums[...] = jnp.zeros_like(sums)
    sums[0] += folded(tab_in * hat_tab[...])
    sums[1] += folded(tab_in)
    tab_grad = norm_in(tab_in, hat_tab[...], inv_tab[:, :1], gain) + hidden_tab[...]
    sums[2] += folded(tab_grad)
    small[:NAT] = tab_grad
    half = NAT // 2
    for index in range(images):
        flags = jnp.sum(one_hot(masked[index], counts[index], NAT), axis=1, keepdims=True)
        for part in range(2):
            rows = slice(index * NAT + part * half, index * NAT + (part + 1) * half)
            flag = flags[part * half : (part + 1) * half]
            grad_in, value = work[rows], hat[rows]
            sums[0] += folded(grad_in * value)
            sums[1] += folded(grad_in)
            value = norm_in(grad_in, value, inv[rows, :1], gain)
            small[part * half : (part + 1) * half] += value
            sums[2] += folded(value * flag)
            value = value * (1.0 - flag)
            sums[3] += folded(value)
            start_low[rows] = value.astype(LOW)
    line = [
        total_row(sums[0]),
        total_row(sums[1]),
        total_row(qkv_sums[0]),
        total_row(qkv_sums[1]),
        total_row(out_sums[3]),
        total_row(out_sums[2]),
        total_row(out_sums[0]),
        total_row(out_sums[1]),
        total_row(down_sums[3]),
        total_row(down_sums[2]),
        total_row(down_sums[0]),
        total_row(down_sums[1]),
        total_row(head_sums[1]),
        total_row(sums[3]),
        total_row(sums[2]),
    ]
    line += [total_row(up_bias[:, at : at + D]) for at in range(0, FF, D)]
    for index, value in enumerate(line):
        small[P_SIZE + index : P_SIZE + index + 1] = value
    small[P_SIZE + len(line) :] = jnp.zeros((TAIL - P_SIZE - len(line), D), F32)
    small_low[...] = small[...].T


def start_back(order, counts, masked, kv_low, table, hidden_tab, hat, inv, hat_tab, inv_tab, vectors, head_sums, down_sums, up_bias, out_sums, qkv_sums, pieces, after=()):
    rows, owners, images = kv_low.shape[0], len(pieces), masked.shape[0]
    return launch(
        functools.partial(start_kernel, owners, images),
        8,
        in_specs=[NUMBERS, NUMBERS] + [ROW] * 14 + [FAR] * owners,
        out_specs=[ROW] * 2,
        out_shape=[shape((rows, D), LOW), shape((D, TAIL), F32)],
        scratch_shapes=[
            pltpu.VMEM((D, 3 * D), LOW),
            pltpu.VMEM((rows, D), F32),
            pltpu.VMEM((TAIL, D), F32),
            pltpu.VMEM((4, 8, D), F32),
            pltpu.SemaphoreType.DMA((owners,)),
        ],
        after=after,
    )(order, counts, masked, kv_low, table, hidden_tab, hat, inv, hat_tab, inv_tab, vectors, head_sums, down_sums, up_bias, out_sums, qkv_sums, *pieces)


def embed_back_kernel(images, blocks, order, pixels, start_low, small_low, *refs):
    outs = 2 if blocks > 1 else 1
    grads = refs[:outs]
    turned, spare, pixel_rows = refs[outs:]
    for index in range(images):
        zeros = jnp.zeros((NAT - P_SIZE, PIX), F32)
        padded = jnp.concatenate([pixels[index].astype(F32), zeros], axis=0)
        pixel_rows[index * NAT : (index + 1) * NAT] = padded.astype(LOW)
    place(order, pixel_rows[...], turned, spare)
    rows = D // order.shape[0]
    block = 0
    for out in grads:
        for index in range(out.shape[0]):
            at = pl.multiple_of(order[block] * rows, 16 if rows % 16 == 0 else 8)
            out[index, :, D:] = small_low[pl.ds(at, rows)].astype(LOW)
            block += 1
    for at in range(0, D, TILE):
        split_store(grads, slice(at, at + TILE), dot(turned[...], start_low[:, at : at + TILE]))


def embed_back(order, pixels, start_low, small_low, after=()):
    rows, blocks = start_low.shape[0], order.shape[0]
    grads = split_shapes(blocks, D + TAIL, (4, 4))
    return launch(
        functools.partial(embed_back_kernel, pixels.shape[0], blocks),
        0.1,
        in_specs=[NUMBERS] + [ROW] * 3,
        out_specs=[ROW] * len(grads),
        out_shape=grads,
        scratch_shapes=[
            pltpu.VMEM((D, rows), LOW),
            pltpu.VMEM((D, rows), LOW),
            pltpu.VMEM((rows, D), LOW),
        ],
        after=after,
    )(order, pixels, start_low, small_low)


def add_kernel(plan, *refs):
    ins, outs = refs[: len(refs) - len(plan)], refs[len(refs) - len(plan) :]
    for segments, out in zip(plan, outs):
        at = 0
        for terms in segments:
            total = None
            for source, block in terms:
                value = (ins[source][...] if block is None else ins[source][block]).astype(F32)
                total = value if total is None else total + value
            out[:, at : at + total.shape[1]] = total.astype(out.dtype)
            at += total.shape[1]


def add(arrays, plan, types, after=(), us=0):
    rows = arrays[0].shape[-2]
    widths = [sum(arrays[terms[0][0]].shape[-1] for terms in segments) for segments in plan]
    return launch(
        functools.partial(add_kernel, plan),
        us,
        in_specs=[ROW] * len(arrays),
        out_specs=[ROW] * len(plan),
        out_shape=[shape((rows, width), kind) for width, kind in zip(widths, types)],
        after=after,
    )(*arrays)


def copy_kernel(source, out):
    out[...] = source[...]


def copied(array, after):
    return launch(
        copy_kernel, 1, in_specs=[ROW], out_specs=ROW, out_shape=shape(array.shape, array.dtype), after=after
    )(array)


def pair_kernel(first, second, out):
    out[...] = (first[...].astype(F32) + second[...].astype(F32)).astype(LOW)


def pair_sums(first, second, after=()):
    return launch(
        pair_kernel, 0, in_specs=[ROW] * 2, out_specs=ROW, out_shape=shape(first.shape, LOW), after=after
    )(first, second)


def share_kernel(counts, half, *refs):
    terms, (keep, send, spare) = list(refs[:-3]), refs[-3:]
    at = 0
    for count, blocks in counts:
        own, *others = [terms.pop(0) for _ in range(count)]
        total = own[0].astype(F32)
        for chip in range(1, blocks):
            total = total + own[chip].astype(F32)
        for other in others:
            total = total + other[...].astype(F32)
        spare[:, at : at + total.shape[1]] = total
        at += total.shape[1]
    rows = keep.shape[0]
    kept = half[0]
    keep[...] = spare[pl.ds(pl.multiple_of(kept * rows, 8), rows)]
    send[...] = spare[pl.ds(pl.multiple_of((1 - kept) * rows, 8), rows)].astype(LOW)


def share_halves(half, parts, after=()):
    rows = parts[0][1].shape[1]
    columns = sum(part[1].shape[2] for part in parts)
    terms = [term for part in parts for term in part[1:]]
    return launch(
        functools.partial(share_kernel, [(len(part) - 1, part[0]) for part in parts]),
        0,
        in_specs=[NUMBERS] + [ROW] * len(terms),
        out_specs=[ROW] * 2,
        out_shape=[shape((rows // 2, columns), F32), shape((rows // 2, columns), LOW)],
        scratch_shapes=[pltpu.VMEM((rows, columns), F32)],
        after=after,
    )(half, *terms)


def adam_update(master, first, second, grad, decay):
    first_new = FIRST_DECAY * first + (1.0 - FIRST_DECAY) * grad
    second_new = SECOND_DECAY * second + (1.0 - SECOND_DECAY) * grad * grad
    first_hat = first_new / (1.0 - FIRST_DECAY**STEP)
    second_hat = second_new / (1.0 - SECOND_DECAY**STEP)
    master_new = master - LEARN_RATE * (
        first_hat / (jnp.sqrt(second_hat) + ADAM_EPSILON) + WEIGHT_DECAY * decay * master
    )
    return (master_new, first_new, second_new)


def targets_of(teacher, masked, counts, after, twin, chips):
    layers, images = lax.axis_size("layer"), masked.shape[0]
    masks = jnp.concatenate([masked, counts[:, None]], axis=1)
    if layers != 4:
        masks = lax.all_gather(masks, "layer", axis=0, tiled=False)
        picked = [teacher_rows(teacher, masks[block], block) for block in range(layers)]
        total = lax.psum_scatter(jnp.stack(picked), "layer", scatter_dimension=0, tiled=False)
        return total, None, None, picked[0]
    at = lax.axis_index("layer")
    near, second, third = [swap(masks, "layer", bit) for bit in (1, 2, 3)]
    own_rows = teacher_rows(teacher, masks, at, after)
    far_rows = teacher_rows(teacher, third, at ^ 3, [own_rows, near, second])
    far = swap(far_rows, "layer", 1)
    second_rows = teacher_rows(teacher, second, at ^ 2, [far_rows, *twin, *chips])

    def near_sum(after):
        rows = teacher_rows(teacher, near, at ^ 1, after)
        return rows, swap(rows, "layer", 1)

    far_sum = lambda after: add([second_rows, far], [[[(0, None), (1, None)]]], [LOW], after, 1)[0]
    return own_rows, near_sum, far_sum, second_rows


def body(
    pixels,
    teacher,
    masked_at,
    mask_count,
    wide_master,
    wide_first,
    wide_second,
    tall_master,
    tall_first,
    tall_second,
):
    owners, layers = lax.axis_size("dp"), lax.axis_size("layer")
    counts, masked = mask_count[0], masked_at[0][:, None, :]
    images = counts.shape[0]
    order = blocks_of(lax.axis_index("dp")) if owners == 8 else jnp.zeros((1,), jnp.int32)
    by_chip = blocks_by_chip(lax.axis_index("dp")) if owners == 8 else order
    tall_low = tall_master.T.astype(LOW)
    wide_embed = part(
        [(wide_master, 0, D), (tall_low, FF, P_SIZE + VECS, TAIL), (wide_master, D, 3 * D)]
    )
    pieces_in = gather_part(wide_embed)
    own_rows, near_sum, far_sum, second_rows = targets_of(
        teacher[0, 0], masked_at[0], counts, [wide_embed], arrived(pieces_in, 1), arrived(pieces_in, 2)
    )
    wide_up = part([(wide_master, 4 * D, D + FF)], [second_rows] + arrived(pieces_in, 4))
    pieces_up = gather_part(wide_up)

    hat_nat, inv_nat, in_nat, position, vectors, hat_tab, inv_tab, in_tab = embed(
        order, counts, pixels[0], masked, pieces_in, after=[wide_up]
    )
    targets, waits = [own_rows], arrived(pieces_up, 2)
    if far_sum:
        near_rows, near = near_sum([in_tab])
        far = far_sum([near_rows])
        targets += [near, swap(far, "layer", 2)]
        waits += [far]
    kv, queries, heads = attention(order, counts, in_nat, masked, in_tab, vectors, pieces_in, after=waits)
    heads = heads.reshape(images * MOST, D)
    wide_down = part([(tall_low, 0, FF), (wide_master, 5 * D + FF, D)], [heads] + arrived(pieces_up, 4))
    pieces_down = gather_part(wide_down)
    attn, hidden, stats_mid, in_mid = mid(
        order, counts, masked, heads, position, vectors, pieces_up, after=[wide_down]
    )
    active_a, slope_a = up(0, FF // 2, order, in_mid, vectors, pieces_up)
    active_b, slope_b = up(
        FF // 2, FF // 2, order, in_mid, vectors, pieces_up, after=[active_a] + arrived(pieces_down, 2)
    )
    active, slope = (active_a, active_b), (slope_a, slope_b)
    branch, stats_out, in_out, work = head(order, active, hidden, vectors, pieces_down)
    *down_g, loss, head_sums, grad, grad_low, down_sums = down(
        order, counts, work, stats_out, hidden, branch, active, vectors, in_out, targets, pieces_down
    )
    down_p = Part(down_g)
    *up_g, pre_low, up_bias = pre(order, grad_low, slope, in_mid, pieces_down)
    up_p = Part(up_g)
    down_s, up_s = Owned([down_p], False), Owned([up_p], False)
    heads_grad, hidden_tab, out_sums, attn_low = out_back(
        order, counts, masked, pre_low, grad, stats_mid, hidden, attn, vectors, pieces_up,
        after=down_p.sums([pre_low]),
    )
    kv_low, table, qkv_sums = attention_back(
        counts, queries, kv, heads_grad.reshape(images, MOST, D), masked,
        after=down_p.sums_out([heads_grad]) + up_p.sums([heads_grad]),
    )
    flat = lambda value: value.reshape(images * NAT, -1)
    qkv_g = qkv_back(
        order, flat(in_nat), flat(kv_low), in_tab, table, heads, attn_low,
        after=down_s.shares([table]) + up_p.sums_out([table]),
    )
    qkv_p = Part(qkv_g)
    start_low, small_low = start_back(
        order, counts, masked, flat(kv_low), table, hidden_tab, flat(hat_nat), flat(inv_nat),
        hat_tab, inv_tab, vectors, head_sums, down_sums, up_bias, out_sums, qkv_sums, pieces_in,
        after=up_s.shares([qkv_g[0]]),
    )
    embed_g = embed_back(
        by_chip, pixels[0], start_low, small_low, after=qkv_p.sums([start_low]) + down_s.pairs([start_low])
    )
    embed_p = Direct(embed_g)
    last_s = Owned([qkv_p, embed_p], True)
    ready = qkv_p.sums_out([embed_g[0]])
    ready = embed_p.sums(ready)
    ready = up_s.pairs(ready)
    ready = down_s.sum_all(ready)
    ready = last_s.shares(ready)
    ready = up_s.sum_all(ready)
    last_s.pairs(ready)
    down_s, up_s, last_s = down_s.total(), up_s.total(), last_s.total()
    qkv_s, embed_s = last_s[:, : 4 * D], last_s[:, 4 * D :]
    wide_share = jnp.concatenate([embed_s[:, :D], qkv_s, up_s, down_s[:, FF:]], axis=1)
    tall_share = jnp.concatenate([down_s[:, :FF], embed_s[:, D : D + P_SIZE + VECS]], axis=1)
    squares = (jnp.sum(wide_share * wide_share) + jnp.sum(tall_share * tall_share)) / layers
    count = jnp.sum(mask_count.astype(F32))
    loss_sum, mask_total, squares = gathered_sum(jnp.stack([loss[0, 0], count, squares]), ("layer", "dp"))
    per_mask = 1.0 / mask_total
    grad_norm = jnp.sqrt(squares) * per_mask
    factor = CLIP_NORM / jnp.maximum(grad_norm, CLIP_NORM) * per_mask
    wide_new, wide_first_new, wide_second_new = adam_update(
        wide_master, wide_first, wide_second, factor * wide_share, 1.0
    )
    tall_decay = (lax.broadcasted_iota(jnp.int32, (tall_master.shape[0], 1), 0) < FF).astype(F32)
    tall_grad = factor * tall_share.T
    tall_new, tall_first_new, tall_second_new = adam_update(
        tall_master, tall_first, tall_second, tall_grad, tall_decay
    )
    return (
        loss_sum,
        mask_total,
        grad_norm,
        wide_new,
        wide_first_new,
        wide_second_new,
        wide_new.astype(LOW),
        tall_new,
        tall_first_new,
        tall_second_new,
        tall_new.astype(LOW),
        tall_grad[FF + P_SIZE + 2],
    )


def solution(mesh):
    in_specs = (
        P("dp", "layer", None, None),
        P("layer", "dp", None, None, None),
        P("dp", "layer", None),
        P("dp", "layer"),
        P("dp", None),
        P("dp", None),
        P("dp", None),
        P(None, "dp"),
        P(None, "dp"),
        P(None, "dp"),
    )
    out_specs = (
        P(),
        P(),
        P(),
        P("dp", None),
        P("dp", None),
        P("dp", None),
        P("dp", None),
        P(None, "dp"),
        P(None, "dp"),
        P(None, "dp"),
        P(None, "dp"),
        P("dp"),
    )
    return jax.shard_map(body, mesh=mesh, in_specs=in_specs, out_specs=out_specs, check_vma=False)
```

```python
import functools
import math

import jax
import jax.numpy as jnp
from jax import lax
from jax.experimental import pallas as pl
from jax.experimental.pallas import tpu as pltpu
from jax.sharding import PartitionSpec as P

D = 768
HEADS = 12
HD = 64
FF = 3072
PIX = 768
P_SIZE = 196
STEP = 10
VECS = 19
MOST = 144
TAIL = 256

HUBER_BETA = 2.0
CLIP_NORM = 0.05
LEARN_RATE = 0.08
FIRST_DECAY = 0.9
SECOND_DECAY = 0.999
WEIGHT_DECAY = 0.05
ADAM_EPSILON = 1e-08
NORM_EPSILON = 1e-06
INSTANCE_EPSILON = 1e-05
LOW = jnp.bfloat16
F32 = jnp.float32


def flip(size, bit):
    return [(i, i ^ bit) for i in range(size)]


def swap(value, axis, bit):
    return lax.ppermute(value, axis, flip(lax.axis_size(axis), bit))


def over_link(value):
    return lax.ppermute(value, "dp", [(i, i ^ (4 if i & 1 else 2)) for i in range(8)])


def over_other(value):
    return lax.ppermute(value, "dp", [(i, i ^ (2 if i & 1 else 4)) for i in range(8)])


def blocks_of(me):
    link = jnp.where(me & 1 == 1, 4, 2)
    other = 6 - link
    return jnp.stack([me, me ^ 1, me ^ link, me ^ link ^ 1, me ^ 6, me ^ other ^ 1, me ^ other, me ^ 7])


def gather_part(shard, after=None):
    if lax.axis_size("dp") != 8:
        return [lax.all_gather(shard, "dp", axis=0, tiled=True)]
    twin = swap(shard, "dp", 1)
    first, second = over_link(shard), over_link(twin)
    diagonal = over_other(first if after is None else copied(first, after))
    return [shard, twin, first, second, diagonal] + [swap(piece, "dp", 1) for piece in (first, second, diagonal)]


def arrived(pieces, *indices):
    return [pieces[index] for index in indices] if len(pieces) > 1 else []


class Steps:
    def __init__(self):
        self.made = {}
        self.plain = lax.axis_size("dp") != 8 or lax.axis_size("layer") != 4

    def step(self, name, make):
        if self.plain:
            return []
        if name not in self.made:
            self.made[name] = list(make())
        return self.made[name]


class Part(Steps):
    def __init__(self, grads):
        super().__init__()
        self.grads = grads

    def core(self):
        return self.step("core", lambda: [swap(self.grads[2], "dp", 1)])

    def sums(self, after=()):
        def make():
            plan = [[[(0, block), (1, block)]] for block in range(3)]
            return add([self.grads[1], *self.core()], plan, [F32, LOW, LOW], after)

        return self.step("sums", make)

    def crossed(self):
        def make():
            _, second, diagonal = self.sums()
            return [over_other(diagonal), over_link(second)]

        return self.step("crossed", make)


    def sums_out(self, after=()):
        def make():
            diagonal, second = self.crossed()
            arrays = [self.sums()[0], diagonal, self.grads[0], second]
            return add(arrays, [[[(0, None), (1, None)]], [[(2, 1), (3, None)]]], [LOW, LOW], after)

        return self.step("sums_out", make)

    def last(self):
        def make():
            ahead, twin = self.sums_out()
            return [over_link(ahead), swap(twin, "dp", 1)]

        return self.step("last", make)

    def terms(self):
        return [1, self.grads[0], *self.last()]


def blocks_by_chip(me):
    chips, core = 2 * jnp.arange(4), me & 1
    return jnp.concatenate([chips + core, chips + 1 - core])


class Direct(Steps):
    def __init__(self, grads):
        super().__init__()
        self.grads = grads

    def core(self):
        return self.step("core", lambda: [swap(self.grads[1], "dp", 1)])

    def sums(self, after=()):
        return self.step("sums", lambda: [pair_sums(self.grads[0], *self.core(), after)])

    def last(self):
        groups = [[0, 2, 4, 6], [1, 3, 5, 7]]
        spread = functools.partial(lax.all_to_all, axis_name="dp", split_axis=0, concat_axis=0)
        return self.step("last", lambda: [spread(*self.sums(), axis_index_groups=groups, tiled=True)])

    def terms(self):
        return [4, *self.last()]


class Owned(Steps):
    def __init__(self, parts, by_halves):
        super().__init__()
        self.parts, self.by_halves = parts, by_halves
        self.place = lax.axis_index("layer")

    def shares(self, after=()):
        def make():
            if self.by_halves:
                return share_halves((self.place & 1)[None], [part.terms() for part in self.parts], after)
            terms = self.parts[0].terms()[1:]
            plan = [[[(0, 0), (1, None), (2, None)]]] * 2
            return add(terms, plan, [F32, LOW], after)

        return self.step("shares", make)

    def near(self):
        def make():
            sent = self.shares()[1]
            if self.by_halves:
                return [swap(sent, "layer", 1)]
            return [lax.ppermute(sent, "layer", [(0, 1), (3, 2)])]

        return self.step("near", make)

    def pairs(self, after=()):
        plan = [[[(0, None), (1, None)]]]
        return self.step("pairs", lambda: add([self.shares()[0], *self.near()], plan, [LOW], after))

    def far(self):
        def make():
            if self.by_halves:
                return [swap(*self.pairs(), "layer", 2)]
            return [lax.ppermute(*self.pairs(), "layer", [(1, 2), (2, 1)])]

        return self.step("far", make)

    def sum_all(self, after=()):
        plan = [[[(0, None), (1, None)]]]
        return self.step("all", lambda: add([*self.pairs(), *self.far()], plan, [LOW], after))

    def back(self):
        def make():
            if self.by_halves:
                return [swap(*self.sum_all(), "layer", 1)]
            return [lax.ppermute(*self.sum_all(), "layer", [(1, 0), (2, 3)])]

        return self.step("back", make)

    def scattered(self):
        grads = [part.grads[0].reshape(D, -1) for part in self.parts]
        shares = [lax.psum_scatter(grad, "dp", scatter_dimension=0, tiled=True) for grad in grads]
        return jnp.concatenate(shares, axis=1)

    def total(self):
        if self.plain:
            return lax.psum(self.scattered(), "layer").astype(F32)
        (mine,), (other,) = self.sum_all(), self.back()
        if not self.by_halves:
            return jnp.where((self.place == 1) | (self.place == 2), mine, other).astype(F32)
        even = self.place & 1 == 0
        halves = [jnp.where(even, mine, other), jnp.where(even, other, mine)]
        return jnp.concatenate(halves, axis=0).astype(F32)


def layer_sums(*owned):
    lows = [one.shares()[1] if not one.plain else one.scattered() for one in owned]
    return [total.astype(F32) for total in lax.psum(tuple(lows), "layer")]


def gathered_sum(value, axes):
    size = lax.axis_size(axes)
    sent = jnp.broadcast_to(value, (size, *value.shape))
    return jnp.sum(lax.all_to_all(sent, axes, split_axis=0, concat_axis=0), axis=0)
NAT = 208
TILE = 256
CHUNK = 48
SPARE_VMEM = 6 * 2**20
COST_TEACHER = 1
HEAVY = 2.5e9
ROW = pl.BlockSpec(memory_space=pltpu.VMEM)
FAR = pl.BlockSpec(memory_space=pl.ANY)
NUMBERS = pl.BlockSpec(memory_space=pltpu.SMEM)


def late(dims, dtype):
    return pltpu.HBM(dims, dtype)


def shape(dims, dtype):
    return jax.ShapeDtypeStruct(dims, dtype)


def launch(kernel, us, in_specs, out_specs, out_shape, scratch_shapes=(), grid=(), prefetch=0, after=()):
    def call(*args):
        count = len(args)

        def body(*refs):
            kernel(*refs[:count], *refs[count + len(after) :])

        held = sum(
            math.prod(ref.shape) * jnp.dtype(ref.dtype).itemsize
            for ref in scratch_shapes
            if jnp.issubdtype(ref.dtype, jnp.floating)
        )
        spec = pltpu.PrefetchScalarGridSpec(
            num_scalar_prefetch=prefetch,
            grid=grid,
            in_specs=list(in_specs) + [FAR] * len(after),
            out_specs=out_specs,
            scratch_shapes=list(scratch_shapes),
        )
        return pl.pallas_call(
            body,
            grid_spec=spec,
            out_shape=out_shape,
            compiler_params=pltpu.CompilerParams(vmem_limit_bytes=held + SPARE_VMEM),
            cost_estimate=pl.CostEstimate(flops=int(us * HEAVY), bytes_accessed=1 << 20 if us else 1, transcendentals=0),
        )(*args, *after)

    return call


def dot(left, right):
    return jnp.dot(left, right, preferred_element_type=F32)


def dot_t(left, right):
    return lax.dot_general(left, right, (((1,), (1,)), ((), ())), preferred_element_type=F32)


def t_dot(left, right):
    return lax.dot_general(left, right, (((0,), (0,)), ((), ())), preferred_element_type=F32)


def fetch(order, pieces, weight, sems, columns=None):
    rows = pieces[0].shape[0]
    copies = []
    for index, piece in enumerate(pieces):
        source = piece if columns is None else piece.at[:, columns]
        at = pl.multiple_of(order[index] * rows, 16 if rows % 16 == 0 else 8)
        copies.append(pltpu.make_async_copy(source, weight.at[pl.ds(at, rows)], sems.at[index]))
    for copy in copies:
        copy.start()
    return copies


def wait_all(copies):
    for copy in copies:
        copy.wait()


def one_hot(masked, count, rows):
    patch = lax.broadcasted_iota(jnp.int32, (rows, MOST), 0)
    slot = lax.broadcasted_iota(jnp.int32, (rows, MOST), 1)
    return jnp.where((masked[:, :MOST] == patch) & (slot < count), 1.0, 0.0)


def normed_with(values):
    mean = jnp.mean(values, axis=-1, keepdims=True)
    centered = values - mean
    inv_std = lax.rsqrt(jnp.mean(centered * centered, axis=-1, keepdims=True) + NORM_EPSILON)
    lane = lax.broadcasted_iota(jnp.int32, (1, 128), 1)
    return centered * inv_std, jnp.where(lane == 0, mean, inv_std)


def normed(values):
    centered = values - jnp.mean(values, axis=-1, keepdims=True)
    inv_std = lax.rsqrt(jnp.mean(centered * centered, axis=-1, keepdims=True) + NORM_EPSILON)
    return centered * inv_std, inv_std


def norm_in(grad_in, hat, inv_std, gain):
    scaled = grad_in * gain
    return inv_std * (
        scaled
        - jnp.mean(scaled, axis=-1, keepdims=True)
        - hat * jnp.mean(scaled * hat, axis=-1, keepdims=True)
    )


def wide(column):
    return jnp.broadcast_to(column, (column.shape[0], 128))


def folded(values):
    return jnp.sum(values.reshape(-1, 8, values.shape[-1]), axis=0)


def total_row(values):
    return jnp.sum(values, axis=0, keepdims=True)


def split_store(outs, columns, grad):
    rows = outs[0].shape[1]
    low = grad.astype(LOW)
    at = 0
    for out in outs:
        for index in range(out.shape[0]):
            out[index, :, columns] = low[at : at + rows]
            at += rows


def split_shapes(blocks, columns, counts=(2, 3, 3)):
    if blocks == 1:
        counts = (1,)
    return [shape((count, D // blocks, columns), LOW) for count in counts]


def teacher_kernel(counts, teacher, masked, out):
    for index in range(teacher.shape[0]):
        pick = one_hot(masked[index], counts[index], P_SIZE).astype(LOW)
        rows = slice(index * MOST, (index + 1) * MOST)
        for at in range(0, D, TILE):
            low = teacher[index, :, at : at + TILE]
            values = low.astype(F32)
            mean = jnp.sum(values, axis=0, keepdims=True) * (1.0 / P_SIZE)
            centered = values - mean
            square = jnp.sum(centered * centered, axis=0, keepdims=True) * (1.0 / P_SIZE)
            inv = lax.rsqrt(square + INSTANCE_EPSILON)
            out[rows, at : at + TILE] = ((t_dot(pick, low) - mean) * inv).astype(LOW)


def teacher_rows(teacher, masks, block, after=()):
    images = masks.shape[0]
    return launch(
        teacher_kernel,
        COST_TEACHER,
        in_specs=[NUMBERS, ROW, ROW],
        out_specs=ROW,
        out_shape=shape((images * MOST, D), LOW),
        after=after,
    )(masks[:, P_SIZE], lax.dynamic_slice_in_dim(teacher, block * images, images), masks[:, None, :P_SIZE])


def far_kernel(mine, other, first, second):
    total = (mine[...].astype(F32) + other[...].astype(F32)).astype(LOW)
    half = first.shape[1]
    first[...] = total[:, :half]
    second[...] = total[:, half:]


def far_sums(mine, other, after=()):
    rows = mine.shape[0]
    return launch(
        far_kernel,
        1,
        in_specs=[ROW] * 2,
        out_specs=[ROW] * 2,
        out_shape=[shape((rows, D // 2), LOW)] * 2,
        after=after,
    )(mine, other)


def part_kernel(spans, *refs):
    ins, out = refs[: len(spans)], refs[-1]
    at = 0
    for (source, start, size, *room), ref in zip(spans, ins):
        out[:, at : at + size] = ref[:, start : start + size].astype(LOW)
        at += size
        if room:
            out[:, at : at + room[0] - size] = jnp.zeros((out.shape[0], room[0] - size), LOW)
            at += room[0] - size


def part(spans, after=()):
    rows = spans[0][0].shape[0]
    return launch(
        functools.partial(part_kernel, spans),
        0.2,
        in_specs=[ROW] * len(spans),
        out_specs=ROW,
        out_shape=shape((rows, sum(span[-1] for span in spans)), LOW),
        after=after,
    )(*[span[0] for span in spans])


def embed_kernel(owners, order, counts, pixels, masked, *refs):
    pieces, refs = refs[:owners], refs[owners:]
    hat, inv, rows_in, position, vectors, hat_tab, inv_tab, tab_in, weight, sems = refs
    step = pl.program_id(0)

    @pl.when(step == 0)
    def _():
        wait_all(fetch(order, pieces, weight, sems, pl.ds(0, D + TAIL)))
        small = weight[:, D:].astype(F32).T
        vectors[...] = small[P_SIZE : P_SIZE + vectors.shape[0]]
        rows = small[:P_SIZE]
        zeros = jnp.zeros((NAT - P_SIZE, D), F32)
        position[...] = jnp.concatenate([rows, zeros], axis=0).astype(LOW)
        table, table_inv = normed(rows + small[P_SIZE + 14 : P_SIZE + 15])
        hat_tab[...] = jnp.concatenate([table, zeros], axis=0)
        inv_tab[...] = jnp.concatenate([wide(table_inv), zeros[:, :128]], axis=0)
        table = table * small[P_SIZE : P_SIZE + 1] + small[P_SIZE + 1 : P_SIZE + 2]
        tab_in[...] = jnp.concatenate([table, zeros], axis=0).astype(LOW)

    flag = jnp.sum(one_hot(masked[0], counts[step], P_SIZE), axis=1, keepdims=True)
    embedded = dot(pixels[0], weight[:, :D]) + vectors[13:14]
    start = flag * vectors[14:15] + (1.0 - flag) * embedded + position[...].astype(F32)[:P_SIZE]
    value, value_inv = normed(start)
    zeros = jnp.zeros((NAT - P_SIZE, D), F32)
    hat[0] = jnp.concatenate([value, zeros], axis=0)
    inv[0] = jnp.concatenate([wide(value_inv), zeros[:, :128]], axis=0)
    value = value * vectors[0:1] + vectors[1:2]
    rows_in[0] = jnp.concatenate([value, zeros], axis=0).astype(LOW)


def embed(order, counts, pixels, masked, pieces, after=()):
    images, owners = pixels.shape[0], len(pieces)
    whole = lambda *dims: pl.BlockSpec(dims, lambda i, order, counts: (0,) * len(dims))
    image = lambda *dims: pl.BlockSpec((1, *dims), lambda i, order, counts: (i,) + (0,) * len(dims))
    return launch(
        functools.partial(embed_kernel, owners),
        1,
        prefetch=2,
        grid=(images,),
        in_specs=[image(P_SIZE, PIX), image(1, P_SIZE)] + [FAR] * owners,
        out_specs=[
            image(NAT, D),
            image(NAT, 128),
            image(NAT, D),
            whole(NAT, D),
            whole(24, D),
            whole(NAT, D),
            whole(NAT, 128),
            whole(NAT, D),
        ],
        scratch_shapes=[pltpu.VMEM((D, D + TAIL), LOW), pltpu.SemaphoreType.DMA((owners,))],
        out_shape=[
            late((images, NAT, D), F32),
            late((images, NAT, 128), F32),
            shape((images, NAT, D), LOW),
            shape((NAT, D), LOW),
            shape((24, D), F32),
            late((NAT, D), F32),
            late((NAT, 128), F32),
            shape((NAT, D), LOW),
        ],
        after=after,
    )(order, counts, pixels, masked, *pieces)


def halves(pair):
    lane = lax.broadcasted_iota(jnp.int32, (1, 128), 1)
    first = jnp.where(lane < HD, 1.0, 0.0).astype(LOW)
    return jnp.concatenate([pair * first, pair * (1.0 - first.astype(F32)).astype(LOW)], axis=0)


def merged(both):
    lane = lax.broadcasted_iota(jnp.int32, (MOST, 128), 1)
    return jnp.where(lane < HD, both[:MOST], both[MOST:])


def attention_kernel(owners, order, counts, rows_in, masked, tab_in, vectors, *refs):
    pieces, refs = refs[:owners], refs[owners:]
    kv, queries, heads, weight, table, sems = refs
    step = pl.program_id(0)

    @pl.when(step == 0)
    def _():
        wait_all(fetch(order, pieces, weight, sems, pl.ds(D + TAIL, 3 * D)))
        table[...] = (dot(tab_in[...], weight[:, :D]) + vectors[2:3]).astype(LOW)

    kv[0, :, :D] = dot(rows_in[0], weight[:, D : 2 * D]).astype(LOW)
    kv[0, :, D:] = (dot(rows_in[0], weight[:, 2 * D :]) + vectors[3:4]).astype(LOW)
    pick = one_hot(masked[0], counts[step], NAT).astype(LOW)
    queries[0] = t_dot(pick, table[...]).astype(LOW)
    key_index = lax.broadcasted_iota(jnp.int32, (1, NAT), 1)
    for at in range(0, D, 128):
        pair = halves(queries[0, :, at : at + 128]) * jnp.asarray(1.0 / math.sqrt(HD), LOW)
        scores = dot_t(pair, kv[0, :, at : at + 128])
        scores = jnp.where(key_index < P_SIZE, scores, -1e30)
        shifted = jnp.exp(scores - jnp.max(scores, axis=1, keepdims=True))
        probs = (shifted * (1.0 / jnp.sum(shifted, axis=1, keepdims=True))).astype(LOW)
        heads[0, :, at : at + 128] = merged(dot(probs, kv[0, :, D + at : D + at + 128])).astype(LOW)


def attention(order, counts, rows_in, masked, tab_in, vectors, pieces, after=()):
    images, owners = rows_in.shape[0], len(pieces)
    whole = lambda *dims: pl.BlockSpec(dims, lambda i, order, counts: (0,) * len(dims))
    image = lambda *dims: pl.BlockSpec((1, *dims), lambda i, order, counts: (i,) + (0,) * len(dims))
    return launch(
        functools.partial(attention_kernel, owners),
        12,
        prefetch=2,
        grid=(images,),
        in_specs=[image(NAT, D), image(1, P_SIZE), whole(NAT, D), whole(24, D)] + [FAR] * owners,
        out_specs=[image(NAT, 2 * D), image(MOST, D), image(MOST, D), whole(D, 3 * D)],
        scratch_shapes=[
            pltpu.VMEM((NAT, D), LOW),
            pltpu.SemaphoreType.DMA((owners,)),
        ],
        out_shape=[late((images, NAT, 2 * D), LOW), late((images, MOST, D), LOW), shape((images, MOST, D), LOW), late((D, 3 * D), LOW)],
        after=after,
    )(order, counts, rows_in, masked, tab_in, vectors, *pieces)


def chunks(count, body):
    lax.fori_loop(0, count, lambda k, _: (body(k), 0)[1], 0, unroll=3)


def at_chunk(k, rows=CHUNK):
    return pl.ds(pl.multiple_of(k * rows, 16), rows)


def gelu_parts(value):
    size = jnp.abs(value) * math.sqrt(0.5)
    t = 1.0 / (1.0 + 0.3275911 * size)
    bell = jnp.exp(-size * size)
    poly = t * (0.254829592 + t * (-0.284496736 + t * (1.421413741 + t * (-1.453152027 + t * 1.061405429))))
    below = 0.5 * poly * bell
    share = jnp.where(value < 0, below, 1.0 - below)
    return value * share, share + value * bell * (1.0 / math.sqrt(2.0 * math.pi))


def mid_kernel(owners, images, order, counts, masked, heads, position, vectors, *refs):
    pieces, refs = refs[:owners], refs[owners:]
    attn, hidden, stats, rows_in, weight, sems, up_sems = refs
    copies = fetch(order, pieces, weight.at[:, pl.ds(0, D)], sems, pl.ds(0, D))
    up_copies = fetch(order, pieces, weight.at[:, pl.ds(D, FF)], up_sems, pl.ds(D, FF))
    for index in range(images):
        pick = one_hot(masked[index], counts[index], NAT).astype(LOW)
        hidden[index * MOST : (index + 1) * MOST] = t_dot(pick, position[...]) + vectors[14:15]
    wait_all(copies)
    for at in range(0, D, TILE):
        attn[:, at : at + TILE] = dot(heads[...], weight[:, at : at + TILE])

    def first(k):
        rows = at_chunk(k)
        branch = attn[rows] + vectors[4:5]
        attn[rows] = branch
        value = hidden[rows] + vectors[5:6] * branch
        hidden[rows] = value
        value, stats[rows] = normed_with(value)
        rows_in[rows] = (value * vectors[6:7] + vectors[7:8]).astype(LOW)

    chunks(hidden.shape[0] // CHUNK, first)
    wait_all(up_copies)


def mid(order, counts, masked, heads, position, vectors, pieces, after=()):
    rows, owners = heads.shape[0], len(pieces)
    return launch(
        functools.partial(mid_kernel, owners, masked.shape[0]),
        6,
        in_specs=[NUMBERS, NUMBERS] + [ROW] * 4 + [FAR] * owners,
        out_specs=[ROW] * 5,
        out_shape=[
            shape((rows, D), F32),
            shape((rows, D), F32),
            shape((rows, 128), F32),
            shape((rows, D), LOW),
            shape((D, D + FF), LOW),
        ],
        scratch_shapes=[pltpu.SemaphoreType.DMA((owners,))] * 2,
        after=after,
    )(order, counts, masked, heads, position, vectors, *pieces)


def up_kernel(first, rows_in, vectors, weight, active, slope, pre_a, pre_b):
    def product(tile, into):
        into[...] = dot(rows_in[...], weight[:, pl.ds(pl.multiple_of(D + first + tile * TILE, TILE), TILE)])

    def finish(tile, source):
        columns = pl.ds(pl.multiple_of(tile * TILE, TILE), TILE)
        part = D // TILE
        row = 15 + first // D + tile // part
        bias = vectors[pl.ds(row, 1), pl.ds(pl.multiple_of((tile % part) * TILE, TILE), TILE)]
        for start in range(0, source.shape[0], 48):
            value, down = gelu_parts(source[start : start + 48] + bias)
            active[start : start + 48, columns] = value.astype(LOW)
            slope[start : start + 48, columns] = down.astype(LOW)

    tiles = active.shape[1] // TILE
    product(0, pre_a)

    def pair(k):
        product(2 * k + 1, pre_b)
        finish(2 * k, pre_a)
        product(jnp.minimum(2 * k + 2, tiles - 1), pre_a)
        finish(2 * k + 1, pre_b)

    chunks(tiles // 2, pair)


def up(first, columns, rows_in, vectors, weight, after=()):
    rows = rows_in.shape[0]
    return launch(
        functools.partial(up_kernel, first),
        7,
        in_specs=[ROW] * 3,
        out_specs=[ROW] * 2,
        out_shape=[shape((rows, columns), LOW)] * 2,
        scratch_shapes=[
            pltpu.VMEM((rows, TILE), F32),
            pltpu.VMEM((rows, TILE), F32),
        ],
        after=after,
    )(rows_in, vectors, weight)


def place(order, source, turned, scratch):
    blocks = order.shape[0]
    if blocks == 1:
        turned[...] = source.T
        return
    rows = D // blocks
    scratch[...] = source.T
    for index in range(blocks):
        at = pl.multiple_of(order[index] * rows, 16 if rows % 16 == 0 else 8)
        turned[index * rows : (index + 1) * rows] = scratch[pl.ds(at, rows)]


def head_kernel(owners, order, active_a, active_b, hidden, vectors, *refs):
    pieces, refs = refs[:owners], refs[owners:]
    branch, stats, rows_in, work, weight, sems, head_sems = refs
    copies = fetch(order, pieces, weight.at[:, pl.ds(0, FF)], sems, pl.ds(0, FF))
    head_copies = fetch(order, pieces, weight.at[:, pl.ds(FF, D)], head_sems, pl.ds(FF, D))
    wait_all(copies)
    half = active_a.shape[1]
    for at in range(0, D, TILE):
        rows = slice(at, at + TILE)
        value = dot_t(active_a[...], weight[rows, :half])
        branch[:, rows] = value + dot_t(active_b[...], weight[rows, half:FF])

    def first(k):
        rows = at_chunk(k)
        value = branch[rows] + vectors[8:9]
        branch[rows] = value
        value, stats[rows] = normed_with(hidden[rows] + vectors[9:10] * value)
        rows_in[rows] = (value * vectors[10:11] + vectors[11:12]).astype(LOW)

    chunks(hidden.shape[0] // CHUNK, first)
    wait_all(head_copies)
    for at in range(0, D, TILE):
        work[:, at : at + TILE] = dot(rows_in[...], weight[:, FF + at : FF + at + TILE])


def head(order, active, hidden, vectors, pieces, after=()):
    rows, owners = hidden.shape[0], len(pieces)
    return launch(
        functools.partial(head_kernel, owners),
        10,
        in_specs=[NUMBERS] + [ROW] * 4 + [FAR] * owners,
        out_specs=[ROW] * 5,
        out_shape=[
            shape((rows, D), F32),
            shape((rows, 128), F32),
            shape((rows, D), LOW),
            shape((rows, D), F32),
            shape((D, FF + D), LOW),
        ],
        scratch_shapes=[pltpu.SemaphoreType.DMA((owners,))] * 2,
        after=after,
    )(order, *active, hidden, vectors, *pieces)


def down_kernel(parts, order, counts, work, stats, hidden, branch, active_a, active_b, vectors, rows_in, weight, *refs):
    targets, refs = refs[:parts], refs[parts:]
    outs = 3 if order.shape[0] > 1 else 1
    grads = refs[:outs]
    loss, head_sums, grad, grad_low, sums, error_low, turned, spare = refs[outs:]
    head_sums[...] = jnp.zeros_like(head_sums)
    sums[...] = jnp.zeros_like(sums)
    steps = grad.shape[0] // CHUNK

    def errors(k):
        rows = at_chunk(k)
        target = targets[0][rows].astype(F32)
        if len(targets) > 1:
            near, first, second = [other[rows].astype(F32) for other in targets[1:]]
            target = target + near + jnp.concatenate([first, second], axis=1)
        error = work[rows] + vectors[12:13] - target * (1.0 / lax.axis_size("layer"))
        size = jnp.abs(error)
        entry = jnp.where(size < HUBER_BETA, error * error * (0.5 / HUBER_BETA), size - 0.5 * HUBER_BETA)
        per_image = MOST // CHUNK
        row = lax.broadcasted_iota(jnp.int32, (CHUNK, 1), 0) + lax.rem(k, per_image) * CHUNK
        flag = row < counts[k // per_image]
        head_sums[0] += folded(jnp.where(flag, entry, 0.0))
        value = jnp.where(flag, jnp.clip(error * (1.0 / HUBER_BETA), -1.0, 1.0), 0.0)
        head_sums[1] += folded(value)
        error_low[rows] = value.astype(LOW)

    chunks(steps, errors)
    loss[0, 0] = jnp.sum(head_sums[0])
    for at in range(0, D, TILE):
        grad[:, at : at + TILE] = dot_t(error_low[...], weight[at : at + TILE, FF:])

    def back(k):
        rows = at_chunk(k)
        grad_in, branch_rows = grad[rows], branch[rows]
        block = hidden[rows] + vectors[9:10] * branch_rows
        value = (block - stats[rows, :1]) * stats[rows, 1:2]
        sums[0] += folded(grad_in * value)
        sums[1] += folded(grad_in)
        value = norm_in(grad_in, value, stats[rows, 1:2], vectors[10:11])
        grad[rows] = value
        sums[2] += folded(value * branch_rows)
        value = value * vectors[9:10]
        sums[3] += folded(value)
        grad_low[rows] = value.astype(LOW)

    chunks(steps, back)
    place(order, grad_low[...], turned, spare)
    half = active_a.shape[1]
    for at in range(0, FF, TILE):
        source = active_a[:, at : at + TILE] if at < half else active_b[:, at - half : at - half + TILE]
        split_store(grads, slice(at, at + TILE), dot(turned[...], source))
    place(order, rows_in[...], turned, spare)
    for at in range(0, D, TILE):
        columns = slice(FF + at, FF + at + TILE)
        split_store(grads, columns, dot(turned[...], error_low[:, at : at + TILE]))


def down(order, counts, work, stats, hidden, branch, active, vectors, rows_in, targets, weight, after=()):
    rows = hidden.shape[0]
    grads = split_shapes(order.shape[0], FF + D)
    return launch(
        functools.partial(down_kernel, len(targets)),
        15,
        in_specs=[NUMBERS, NUMBERS] + [ROW] * (9 + len(targets)),
        out_specs=[ROW] * len(grads) + [NUMBERS] + [ROW] * 4,
        out_shape=grads
        + [
            shape((1, 1), F32),
            shape((2, 8, D), F32),
            shape((rows, D), F32),
            shape((rows, D), LOW),
            shape((4, 8, D), F32),
        ],
        scratch_shapes=[
            pltpu.VMEM((rows, D), LOW),
            pltpu.VMEM((D, rows), LOW),
            pltpu.VMEM((D, rows), LOW),
        ],
        after=after,
    )(order, counts, work, stats, hidden, branch, *active, vectors, rows_in, weight, *targets)


def pre_kernel(order, grad_low, slope_a, slope_b, rows_in, weight, *refs):
    outs = 3 if order.shape[0] > 1 else 1
    grads = refs[:outs]
    pre_low, bias, turned, spare = refs[outs:]
    place(order, rows_in[...], turned, spare)

    half = slope_a.shape[1]
    for at in range(0, FF, TILE):
        columns = slice(at, at + TILE)
        slope, start = (slope_a, at) if at < half else (slope_b, at - half)
        value = dot(grad_low[...], weight[:, columns]) * slope[:, start : start + TILE].astype(F32)
        bias[:, columns] = folded(value)
        pre_low[:, columns] = value.astype(LOW)
        split_store(grads, columns, dot(turned[...], pre_low[:, columns]))


def pre(order, grad_low, slope, rows_in, weight, after=()):
    rows = grad_low.shape[0]
    grads = split_shapes(order.shape[0], FF)
    return launch(
        pre_kernel,
        12,
        in_specs=[NUMBERS] + [ROW] * 5,
        out_specs=[ROW] * (len(grads) + 2),
        out_shape=grads + [shape((rows, FF), LOW), shape((8, FF), F32)],
        scratch_shapes=[
            pltpu.VMEM((D, rows), LOW),
            pltpu.VMEM((D, rows), LOW),
        ],
        after=after,
    )(order, grad_low, *slope, rows_in, weight)


def out_kernel(images, counts, masked, pre_low, grad, stats, hidden, attn, vectors, weight, *refs):
    heads_grad, table, sums, attn_low, work, high, rest = refs
    for at in range(0, D, TILE):
        work[:, at : at + TILE] = dot_t(pre_low[...], weight[at : at + TILE, D:])
    sums[...] = jnp.zeros_like(sums)

    def back(k):
        rows = at_chunk(k)
        grad_in = work[rows]
        value = (hidden[rows] - stats[rows, :1]) * stats[rows, 1:2]
        sums[0] += folded(grad_in * value)
        sums[1] += folded(grad_in)
        value = grad[rows] + norm_in(grad_in, value, stats[rows, 1:2], vectors[6:7])
        low = value.astype(LOW)
        high[rows] = low
        rest[rows] = (value - low.astype(F32)).astype(LOW)
        sums[2] += folded(value * attn[rows])
        value = value * vectors[5:6]
        sums[3] += folded(value)
        attn_low[rows] = value.astype(LOW)

    chunks(work.shape[0] // CHUNK, back)
    for at in range(0, D, TILE):
        heads_grad[:, at : at + TILE] = dot_t(attn_low[...], weight[at : at + TILE, :D]).astype(LOW)
    for index in range(images):
        pick = one_hot(masked[index], counts[index], NAT).astype(LOW)
        rows = slice(index * MOST, (index + 1) * MOST)
        value = dot(pick, high[rows]) + dot(pick, rest[rows])
        table[...] = value if index == 0 else table[...] + value


def out_back(counts, masked, pre_low, grad, stats, hidden, attn, vectors, weight, after=()):
    rows = grad.shape[0]
    return launch(
        functools.partial(out_kernel, masked.shape[0]),
        14,
        in_specs=[NUMBERS] + [ROW] * 8,
        out_specs=[ROW] * 4,
        out_shape=[shape((rows, D), LOW), shape((NAT, D), F32), shape((4, 8, D), F32), shape((rows, D), LOW)],
        scratch_shapes=[
            pltpu.VMEM((rows, D), F32),
            pltpu.VMEM((rows, D), LOW),
            pltpu.VMEM((rows, D), LOW),
        ],
        after=after,
    )(counts, masked, pre_low, grad, stats, hidden, attn, vectors, weight)


def attention_back_kernel(counts, queries, kv, heads_grad, masked, kv_low, table, sums, query_low):
    step = pl.program_id(0)

    @pl.when(step == 0)
    def _():
        table[...] = jnp.zeros_like(table)
        sums[...] = jnp.zeros_like(sums)

    scale = 1.0 / math.sqrt(HD)
    key_index = lax.broadcasted_iota(jnp.int32, (NAT, 1), 0)
    for at in range(0, D, 128):
        lanes = slice(at, at + 128)
        high = slice(D + at, D + at + 128)
        pair = halves(queries[0, :, lanes]) * jnp.asarray(scale, LOW)
        grad = halves(heads_grad[0, :, lanes])
        keys, values = kv[0, :, lanes], kv[0, :, high]
        scores = jnp.where(key_index < P_SIZE, dot_t(keys, pair), -1e30)
        shifted = jnp.exp(scores - jnp.max(scores, axis=0, keepdims=True))
        probs = shifted * (1.0 / jnp.sum(shifted, axis=0, keepdims=True))
        prob_grad = dot_t(values, grad)
        value_grad = dot(probs.astype(LOW), grad).astype(LOW)
        kv_low[0, :, high] = value_grad
        sums[1, :, lanes] += folded(value_grad.astype(F32))
        inner = jnp.sum(probs * prob_grad, axis=0, keepdims=True)
        score_grad = (probs * (prob_grad - inner)).astype(LOW)
        kv_low[0, :, lanes] = dot(score_grad, pair).astype(LOW)
        query_grad = merged(t_dot(score_grad, keys) * scale).astype(LOW)
        query_low[:, lanes] = query_grad
        sums[0, :, lanes] += folded(query_grad.astype(F32))
    pick = one_hot(masked[0], counts[step], NAT).astype(LOW)
    table[...] += dot(pick, query_low[...])


def attention_back(counts, queries, kv, heads_grad, masked, after=()):
    images = kv.shape[0]
    whole = lambda *dims: pl.BlockSpec(dims, lambda i, counts: (0,) * len(dims))
    image = lambda *dims: pl.BlockSpec((1, *dims), lambda i, counts: (i,) + (0,) * len(dims))
    return launch(
        attention_back_kernel,
        15,
        prefetch=1,
        grid=(images,),
        in_specs=[image(MOST, D), image(NAT, 2 * D), image(MOST, D), image(1, P_SIZE)],
        out_specs=[image(NAT, 2 * D), whole(NAT, D), whole(2, 8, D)],
        scratch_shapes=[pltpu.VMEM((MOST, D), LOW)],
        out_shape=[shape((images, NAT, 2 * D), LOW), shape((NAT, D), F32), shape((2, 8, D), F32)],
        after=after,
    )(counts, queries, kv, heads_grad, masked)


def high_rest(value):
    high = value.astype(LOW)
    return jnp.concatenate([high, (value - high.astype(F32)).astype(LOW)], axis=0)


def qkv_kernel(blocks, order, rows_in, kv_low, tab_in, table, heads, attn_low, *refs):
    outs = 3 if blocks > 1 else 1
    grads = refs[:outs]
    turned, spare, tab_turned, tab_spare, heads_turned, heads_spare = refs[outs:]
    place(order, heads[...], heads_turned, heads_spare)
    for at in range(0, D, TILE):
        columns = slice(3 * D + at, 3 * D + at + TILE)
        split_store(grads, columns, dot(heads_turned[...], attn_low[:, at : at + TILE]))
    place(order, tab_in[...], tab_turned, tab_spare)
    both = high_rest(table[...])
    twice = jnp.concatenate([tab_turned[...], tab_turned[...]], axis=1)
    for at in range(0, D, TILE):
        split_store(grads, slice(at, at + TILE), dot(twice, both[:, at : at + TILE]))
    place(order, rows_in[...], turned, spare)

    for at in range(0, 2 * D, TILE):
        split_store(grads, slice(D + at, D + at + TILE), dot(turned[...], kv_low[:, at : at + TILE]))


def qkv_back(order, rows_in, kv_low, tab_in, table, heads, attn_low, after=()):
    blocks, rows = order.shape[0], rows_in.shape[0]
    grads = split_shapes(blocks, 4 * D)
    return launch(
        functools.partial(qkv_kernel, blocks),
        7,
        in_specs=[NUMBERS] + [ROW] * 6,
        out_specs=[ROW] * len(grads),
        out_shape=grads,
        scratch_shapes=[
            pltpu.VMEM((D, rows), LOW),
            pltpu.VMEM((D, rows), LOW),
            pltpu.VMEM((D, NAT), LOW),
            pltpu.VMEM((D, NAT), LOW),
            pltpu.VMEM((D, heads.shape[0]), LOW),
            pltpu.VMEM((D, heads.shape[0]), LOW),
        ],
        after=after,
    )(order, rows_in, kv_low, tab_in, table, heads, attn_low)


def start_kernel(images, counts, masked, kv_low, table, hidden_tab, hat, inv, hat_tab, inv_tab, vectors, head_sums, down_sums, up_bias, out_sums, qkv_sums, weight, *refs):
    start_low, small_low, work, small, sums = refs
    for at in range(0, D, TILE):
        work[:, at : at + TILE] = dot_t(kv_low[...], weight[at : at + TILE, D:])
    both = high_rest(table[...])
    tab_in = dot_t(both, weight[:, :D])
    tab_in = tab_in[:NAT] + tab_in[NAT:]
    gain = vectors[0:1]
    sums[...] = jnp.zeros_like(sums)
    sums[0] += folded(tab_in * hat_tab[...])
    sums[1] += folded(tab_in)
    tab_grad = norm_in(tab_in, hat_tab[...], inv_tab[:, :1], gain) + hidden_tab[...]
    sums[2] += folded(tab_grad)
    small[:NAT] = tab_grad
    half = NAT // 2
    for index in range(images):
        flags = jnp.sum(one_hot(masked[index], counts[index], NAT), axis=1, keepdims=True)
        for part in range(2):
            rows = slice(index * NAT + part * half, index * NAT + (part + 1) * half)
            flag = flags[part * half : (part + 1) * half]
            grad_in, value = work[rows], hat[rows]
            sums[0] += folded(grad_in * value)
            sums[1] += folded(grad_in)
            value = norm_in(grad_in, value, inv[rows, :1], gain)
            small[part * half : (part + 1) * half] += value
            sums[2] += folded(value * flag)
            value = value * (1.0 - flag)
            sums[3] += folded(value)
            start_low[rows] = value.astype(LOW)
    line = [
        total_row(sums[0]),
        total_row(sums[1]),
        total_row(qkv_sums[0]),
        total_row(qkv_sums[1]),
        total_row(out_sums[3]),
        total_row(out_sums[2]),
        total_row(out_sums[0]),
        total_row(out_sums[1]),
        total_row(down_sums[3]),
        total_row(down_sums[2]),
        total_row(down_sums[0]),
        total_row(down_sums[1]),
        total_row(head_sums[1]),
        total_row(sums[3]),
        total_row(sums[2]),
    ]
    line += [total_row(up_bias[:, at : at + D]) for at in range(0, FF, D)]
    for index, value in enumerate(line):
        small[P_SIZE + index : P_SIZE + index + 1] = value
    small[P_SIZE + len(line) :] = jnp.zeros((TAIL - P_SIZE - len(line), D), F32)
    small_low[...] = small[...].T


def start_back(counts, masked, kv_low, table, hidden_tab, hat, inv, hat_tab, inv_tab, vectors, head_sums, down_sums, up_bias, out_sums, qkv_sums, weight, after=()):
    rows, images = kv_low.shape[0], masked.shape[0]
    return launch(
        functools.partial(start_kernel, images),
        8,
        in_specs=[NUMBERS] + [ROW] * 15,
        out_specs=[ROW] * 2,
        out_shape=[shape((rows, D), LOW), shape((D, TAIL), F32)],
        scratch_shapes=[
            pltpu.VMEM((rows, D), F32),
            pltpu.VMEM((TAIL, D), F32),
            pltpu.VMEM((4, 8, D), F32),
        ],
        after=after,
    )(counts, masked, kv_low, table, hidden_tab, hat, inv, hat_tab, inv_tab, vectors, head_sums, down_sums, up_bias, out_sums, qkv_sums, weight)


def embed_back_kernel(images, blocks, order, pixels, start_low, small_low, *refs):
    outs = 2 if blocks > 1 else 1
    grads = refs[:outs]
    turned, spare, pixel_rows = refs[outs:]
    for index in range(images):
        zeros = jnp.zeros((NAT - P_SIZE, PIX), F32)
        padded = jnp.concatenate([pixels[index].astype(F32), zeros], axis=0)
        pixel_rows[index * NAT : (index + 1) * NAT] = padded.astype(LOW)
    place(order, pixel_rows[...], turned, spare)
    rows = D // order.shape[0]
    block = 0
    for out in grads:
        for index in range(out.shape[0]):
            at = pl.multiple_of(order[block] * rows, 16 if rows % 16 == 0 else 8)
            out[index, :, D:] = small_low[pl.ds(at, rows)].astype(LOW)
            block += 1
    for at in range(0, D, TILE):
        split_store(grads, slice(at, at + TILE), dot(turned[...], start_low[:, at : at + TILE]))


def embed_back(order, pixels, start_low, small_low, after=()):
    rows, blocks = start_low.shape[0], order.shape[0]
    grads = split_shapes(blocks, D + TAIL, (4, 4))
    return launch(
        functools.partial(embed_back_kernel, pixels.shape[0], blocks),
        0.1,
        in_specs=[NUMBERS] + [ROW] * 3,
        out_specs=[ROW] * len(grads),
        out_shape=grads,
        scratch_shapes=[
            pltpu.VMEM((D, rows), LOW),
            pltpu.VMEM((D, rows), LOW),
            pltpu.VMEM((rows, D), LOW),
        ],
        after=after,
    )(order, pixels, start_low, small_low)


def add_kernel(plan, *refs):
    ins, outs = refs[: len(refs) - len(plan)], refs[len(refs) - len(plan) :]
    for segments, out in zip(plan, outs):
        at = 0
        for terms in segments:
            total = None
            for source, block in terms:
                value = (ins[source][...] if block is None else ins[source][block]).astype(F32)
                total = value if total is None else total + value
            out[:, at : at + total.shape[1]] = total.astype(out.dtype)
            at += total.shape[1]


def add(arrays, plan, types, after=(), us=0):
    rows = arrays[0].shape[-2]
    widths = [sum(arrays[terms[0][0]].shape[-1] for terms in segments) for segments in plan]
    return launch(
        functools.partial(add_kernel, plan),
        us,
        in_specs=[ROW] * len(arrays),
        out_specs=[ROW] * len(plan),
        out_shape=[shape((rows, width), kind) for width, kind in zip(widths, types)],
        after=after,
    )(*arrays)


def copy_kernel(source, out):
    out[...] = source[...]


def copied(array, after):
    return launch(
        copy_kernel, 1, in_specs=[ROW], out_specs=ROW, out_shape=shape(array.shape, array.dtype), after=after
    )(array)


def pair_kernel(first, second, out):
    out[...] = (first[...].astype(F32) + second[...].astype(F32)).astype(LOW)


def pair_sums(first, second, after=()):
    return launch(
        pair_kernel, 0, in_specs=[ROW] * 2, out_specs=ROW, out_shape=shape(first.shape, LOW), after=after
    )(first, second)


def share_kernel(counts, half, *refs):
    terms, (keep, send, spare) = list(refs[:-3]), refs[-3:]
    at = 0
    for count, blocks in counts:
        own, *others = [terms.pop(0) for _ in range(count)]
        total = own[0].astype(F32)
        for chip in range(1, blocks):
            total = total + own[chip].astype(F32)
        for other in others:
            total = total + other[...].astype(F32)
        spare[:, at : at + total.shape[1]] = total
        at += total.shape[1]
    rows = keep.shape[0]
    kept = half[0]
    keep[...] = spare[pl.ds(pl.multiple_of(kept * rows, 8), rows)]
    send[...] = spare[pl.ds(pl.multiple_of((1 - kept) * rows, 8), rows)].astype(LOW)


def share_halves(half, parts, after=()):
    rows = parts[0][1].shape[1]
    columns = sum(part[1].shape[2] for part in parts)
    terms = [term for part in parts for term in part[1:]]
    return launch(
        functools.partial(share_kernel, [(len(part) - 1, part[0]) for part in parts]),
        0,
        in_specs=[NUMBERS] + [ROW] * len(terms),
        out_specs=[ROW] * 2,
        out_shape=[shape((rows // 2, columns), F32), shape((rows // 2, columns), LOW)],
        scratch_shapes=[pltpu.VMEM((rows, columns), F32)],
        after=after,
    )(half, *terms)


def adam_update(master, first, second, grad, decay):
    first_new = FIRST_DECAY * first + (1.0 - FIRST_DECAY) * grad
    second_new = SECOND_DECAY * second + (1.0 - SECOND_DECAY) * grad * grad
    first_hat = first_new / (1.0 - FIRST_DECAY**STEP)
    second_hat = second_new / (1.0 - SECOND_DECAY**STEP)
    master_new = master - LEARN_RATE * (
        first_hat / (jnp.sqrt(second_hat) + ADAM_EPSILON) + WEIGHT_DECAY * decay * master
    )
    return (master_new, first_new, second_new)


def targets_of(teacher, masked, counts, after, twin, chips):
    layers, images = lax.axis_size("layer"), masked.shape[0]
    masks = jnp.concatenate([masked, counts[:, None]], axis=1)
    if layers != 4:
        masks = lax.all_gather(masks, "layer", axis=0, tiled=False)
        picked = [teacher_rows(teacher, masks[block], block) for block in range(layers)]
        total = lax.psum_scatter(jnp.stack(picked), "layer", scatter_dimension=0, tiled=False)
        return total, None, None, picked[0]
    at = lax.axis_index("layer")
    near, second, third = [swap(masks, "layer", bit) for bit in (1, 2, 3)]
    own_rows = teacher_rows(teacher, masks, at, after)
    far_rows = teacher_rows(teacher, third, at ^ 3, [own_rows, near, second])
    far = swap(far_rows, "layer", 1)
    second_rows = teacher_rows(teacher, second, at ^ 2, [far_rows, *twin, *chips])

    def near_sum(after):
        rows = teacher_rows(teacher, near, at ^ 1, after)
        return rows, swap(rows, "layer", 1)

    far_sum = lambda after: far_sums(second_rows, far, after)
    return own_rows, near_sum, far_sum, second_rows


def body(
    pixels,
    teacher,
    masked_at,
    mask_count,
    wide_master,
    wide_first,
    wide_second,
    tall_master,
    tall_first,
    tall_second,
):
    owners, layers = lax.axis_size("dp"), lax.axis_size("layer")
    counts, masked = mask_count[0], masked_at[0][:, None, :]
    images = counts.shape[0]
    order = blocks_of(lax.axis_index("dp")) if owners == 8 else jnp.zeros((1,), jnp.int32)
    by_chip = blocks_by_chip(lax.axis_index("dp")) if owners == 8 else order
    tall_low = tall_master.T.astype(LOW)
    wide_embed = part(
        [(wide_master, 0, D), (tall_low, FF, P_SIZE + VECS, TAIL), (wide_master, D, 3 * D)]
    )
    pieces_in = gather_part(wide_embed)
    own_rows, near_sum, far_sum, second_rows = targets_of(
        teacher[0, 0], masked_at[0], counts, [wide_embed], arrived(pieces_in, 1), arrived(pieces_in, 2)
    )
    wide_up = part([(wide_master, 4 * D, D + FF)], [own_rows] + arrived(pieces_in, 3))
    pieces_up = gather_part(wide_up)

    hat_nat, inv_nat, in_nat, position, vectors, hat_tab, inv_tab, in_tab = embed(
        order, counts, pixels[0], masked, pieces_in, after=[wide_up, second_rows]
    )
    targets, waits = [own_rows], arrived(pieces_up, 2)
    if near_sum:
        near_rows, near = near_sum([in_tab])
        far_a, far_b = far_sum([near_rows])
        waits += [far_a]
        far_a = swap(far_a, "layer", 2)
        targets += [near, far_a]
    kv, queries, heads, qkv_w = attention(
        order, counts, in_nat, masked, in_tab, vectors, pieces_in, after=waits
    )
    heads = heads.reshape(images * MOST, D)
    arrivals = targets[2:]
    if near_sum:
        targets.append(swap(far_b, "layer", 2))
    wide_down = part([(tall_low, 0, FF), (wide_master, 5 * D + FF, D)], [heads] + arrived(pieces_up, 4))
    pieces_down = gather_part(wide_down)
    attn, hidden, stats_mid, in_mid, out_up_w = mid(
        order, counts, masked, heads, position, vectors, pieces_up, after=[wide_down] + arrivals
    )
    active_a, slope_a = up(0, FF // 2, in_mid, vectors, out_up_w)
    active_b, slope_b = up(
        FF // 2, FF // 2, in_mid, vectors, out_up_w, after=[active_a] + arrived(pieces_down, 2)
    )
    active, slope = (active_a, active_b), (slope_a, slope_b)
    branch, stats_out, in_out, work, down_head_w = head(order, active, hidden, vectors, pieces_down)
    *down_g, loss, head_sums, grad, grad_low, down_sums = down(
        order, counts, work, stats_out, hidden, branch, active, vectors, in_out, targets, down_head_w
    )
    down_p = Part(down_g)
    *up_g, pre_low, up_bias = pre(order, grad_low, slope, in_mid, down_head_w)
    up_p = Part(up_g)
    down_s, up_s = Owned([down_p], False), Owned([up_p], False)
    heads_grad, hidden_tab, out_sums, attn_low = out_back(
        counts, masked, pre_low, grad, stats_mid, hidden, attn, vectors, out_up_w,
        after=down_p.sums([pre_low]),
    )
    kv_low, table, qkv_sums = attention_back(
        counts, queries, kv, heads_grad.reshape(images, MOST, D), masked,
        after=down_p.sums_out([heads_grad]) + up_p.sums([heads_grad]),
    )
    flat = lambda value: value.reshape(images * NAT, -1)
    qkv_g = qkv_back(
        order, flat(in_nat), flat(kv_low), in_tab, table, heads, attn_low,
        after=down_s.shares([table]) + up_p.sums_out([table]),
    )
    qkv_p = Part(qkv_g)
    start_low, small_low = start_back(
        counts, masked, flat(kv_low), table, hidden_tab, flat(hat_nat), flat(inv_nat),
        hat_tab, inv_tab, vectors, head_sums, down_sums, up_bias, out_sums, qkv_sums, qkv_w,
        after=up_s.shares([qkv_g[0]]),
    )
    embed_g = embed_back(
        by_chip, pixels[0], start_low, small_low, after=qkv_p.sums([start_low]) + down_s.pairs([start_low])
    )
    embed_p = Direct(embed_g)
    last_s = Owned([qkv_p, embed_p], True)
    ready = qkv_p.sums_out([embed_g[0]])
    ready = embed_p.sums(ready)
    ready = up_s.pairs(ready)
    ready = down_s.sum_all(ready)
    ready = last_s.shares(ready)
    ready = up_s.sum_all(ready)
    last_s.pairs(ready)
    down_s, up_s, last_s = down_s.total(), up_s.total(), last_s.total()
    qkv_s, embed_s = last_s[:, : 4 * D], last_s[:, 4 * D :]
    wide_share = jnp.concatenate([embed_s[:, :D], qkv_s, up_s, down_s[:, FF:]], axis=1)
    tall_share = jnp.concatenate([down_s[:, :FF], embed_s[:, D : D + P_SIZE + VECS]], axis=1)
    squares = (jnp.sum(wide_share * wide_share) + jnp.sum(tall_share * tall_share)) / layers
    count = jnp.sum(mask_count.astype(F32))
    loss_sum, mask_total, squares = gathered_sum(jnp.stack([loss[0, 0], count, squares]), ("layer", "dp"))
    per_mask = 1.0 / mask_total
    grad_norm = jnp.sqrt(squares) * per_mask
    factor = CLIP_NORM / jnp.maximum(grad_norm, CLIP_NORM) * per_mask
    wide_new, wide_first_new, wide_second_new = adam_update(
        wide_master, wide_first, wide_second, factor * wide_share, 1.0
    )
    tall_decay = (lax.broadcasted_iota(jnp.int32, (tall_master.shape[0], 1), 0) < FF).astype(F32)
    tall_grad = factor * tall_share.T
    tall_new, tall_first_new, tall_second_new = adam_update(
        tall_master, tall_first, tall_second, tall_grad, tall_decay
    )
    return (
        loss_sum,
        mask_total,
        grad_norm,
        wide_new,
        wide_first_new,
        wide_second_new,
        wide_new.astype(LOW),
        tall_new,
        tall_first_new,
        tall_second_new,
        tall_new.astype(LOW),
        tall_grad[FF + P_SIZE + 2],
    )


def solution(mesh):
    in_specs = (
        P("dp", "layer", None, None),
        P("layer", "dp", None, None, None),
        P("dp", "layer", None),
        P("dp", "layer"),
        P("dp", None),
        P("dp", None),
        P("dp", None),
        P(None, "dp"),
        P(None, "dp"),
        P(None, "dp"),
    )
    out_specs = (
        P(),
        P(),
        P(),
        P("dp", None),
        P("dp", None),
        P("dp", None),
        P("dp", None),
        P(None, "dp"),
        P(None, "dp"),
        P(None, "dp"),
        P(None, "dp"),
        P("dp"),
    )
    return jax.shard_map(body, mesh=mesh, in_specs=in_specs, out_specs=out_specs, check_vma=False)
```

```python
import functools
import math

import jax
import jax.numpy as jnp
from jax import lax
from jax.experimental import pallas as pl
from jax.experimental.pallas import tpu as pltpu
from jax.sharding import PartitionSpec as P

D = 768
HEADS = 12
HD = 64
FF = 3072
PIX = 768
P_SIZE = 196
STEP = 10
VECS = 19
MOST = 144
TAIL = 256

HUBER_BETA = 2.0
CLIP_NORM = 0.05
LEARN_RATE = 0.08
FIRST_DECAY = 0.9
SECOND_DECAY = 0.999
WEIGHT_DECAY = 0.05
ADAM_EPSILON = 1e-08
NORM_EPSILON = 1e-06
INSTANCE_EPSILON = 1e-05
LOW = jnp.bfloat16
F32 = jnp.float32


def flip(size, bit):
    return [(i, i ^ bit) for i in range(size)]


def swap(value, axis, bit):
    return lax.ppermute(value, axis, flip(lax.axis_size(axis), bit))


def over_link(value):
    return lax.ppermute(value, "dp", [(i, i ^ (4 if i & 1 else 2)) for i in range(8)])


def over_other(value):
    return lax.ppermute(value, "dp", [(i, i ^ (2 if i & 1 else 4)) for i in range(8)])


def blocks_of(me):
    link = jnp.where(me & 1 == 1, 4, 2)
    other = 6 - link
    return jnp.stack([me, me ^ 1, me ^ link, me ^ link ^ 1, me ^ 6, me ^ other ^ 1, me ^ other, me ^ 7])


def gather_part(shard, after=None):
    if lax.axis_size("dp") != 8:
        return [lax.all_gather(shard, "dp", axis=0, tiled=True)]
    twin = swap(shard, "dp", 1)
    first, second = over_link(shard), over_link(twin)
    diagonal = over_other(first if after is None else copied(first, after))
    return [shard, twin, first, second, diagonal] + [swap(piece, "dp", 1) for piece in (first, second, diagonal)]


def arrived(pieces, *indices):
    return [pieces[index] for index in indices] if len(pieces) > 1 else []


class Steps:
    def __init__(self):
        self.made = {}
        self.plain = lax.axis_size("dp") != 8 or lax.axis_size("layer") != 4

    def step(self, name, make):
        if self.plain:
            return []
        if name not in self.made:
            self.made[name] = list(make())
        return self.made[name]


class Part(Steps):
    def __init__(self, grads):
        super().__init__()
        self.grads = grads

    def core(self):
        return self.step("core", lambda: [swap(self.grads[2], "dp", 1)])

    def sums(self, after=()):
        def make():
            plan = [[[(0, block), (1, block)]] for block in range(3)]
            return add([self.grads[1], *self.core()], plan, [F32, LOW, LOW], after)

        return self.step("sums", make)

    def crossed(self):
        def make():
            _, second, diagonal = self.sums()
            return [over_other(diagonal), over_link(second)]

        return self.step("crossed", make)


    def sums_out(self, after=()):
        def make():
            diagonal, second = self.crossed()
            arrays = [self.sums()[0], diagonal, self.grads[0], second]
            return add(arrays, [[[(0, None), (1, None)]], [[(2, 1), (3, None)]]], [LOW, LOW], after)

        return self.step("sums_out", make)

    def last(self):
        def make():
            ahead, twin = self.sums_out()
            return [over_link(ahead), swap(twin, "dp", 1)]

        return self.step("last", make)

    def terms(self):
        return [1, self.grads[0], *self.last()]


def blocks_by_chip(me):
    chips, core = 2 * jnp.arange(4), me & 1
    return jnp.concatenate([chips + core, chips + 1 - core])


class Direct(Steps):
    def __init__(self, grads):
        super().__init__()
        self.grads = grads

    def core(self):
        return self.step("core", lambda: [swap(self.grads[1], "dp", 1)])

    def sums(self, after=()):
        return self.step("sums", lambda: [pair_sums(self.grads[0], *self.core(), after)])

    def last(self):
        groups = [[0, 2, 4, 6], [1, 3, 5, 7]]
        spread = functools.partial(lax.all_to_all, axis_name="dp", split_axis=0, concat_axis=0)
        return self.step("last", lambda: [spread(*self.sums(), axis_index_groups=groups, tiled=True)])

    def terms(self):
        return [4, *self.last()]


class Owned(Steps):
    def __init__(self, parts, by_halves):
        super().__init__()
        self.parts, self.by_halves = parts, by_halves
        self.place = lax.axis_index("layer")

    def shares(self, after=()):
        def make():
            if self.by_halves:
                return share_halves((self.place & 1)[None], [part.terms() for part in self.parts], after)
            terms = self.parts[0].terms()[1:]
            plan = [[[(0, 0), (1, None), (2, None)]]] * 2
            return add(terms, plan, [F32, LOW], after)

        return self.step("shares", make)

    def near(self):
        def make():
            sent = self.shares()[1]
            if self.by_halves:
                return [swap(sent, "layer", 1)]
            return [lax.ppermute(sent, "layer", [(0, 1), (3, 2)])]

        return self.step("near", make)

    def pairs(self, after=()):
        plan = [[[(0, None), (1, None)]]]
        return self.step("pairs", lambda: add([self.shares()[0], *self.near()], plan, [LOW], after))

    def far(self):
        def make():
            if self.by_halves:
                return [swap(*self.pairs(), "layer", 2)]
            return [lax.ppermute(*self.pairs(), "layer", [(1, 2), (2, 1)])]

        return self.step("far", make)

    def sum_all(self, after=()):
        plan = [[[(0, None), (1, None)]]]
        return self.step("all", lambda: add([*self.pairs(), *self.far()], plan, [LOW], after))

    def back(self):
        def make():
            if self.by_halves:
                return [swap(*self.sum_all(), "layer", 1)]
            return [lax.ppermute(*self.sum_all(), "layer", [(1, 0), (2, 3)])]

        return self.step("back", make)

    def scattered(self):
        grads = [part.grads[0].reshape(D, -1) for part in self.parts]
        shares = [lax.psum_scatter(grad, "dp", scatter_dimension=0, tiled=True) for grad in grads]
        return jnp.concatenate(shares, axis=1)

    def squared(self):
        if self.plain:
            return [self.total()]
        return [*self.sum_all(), *self.back()] if self.by_halves else [self.total()]

    def total(self):
        if self.plain:
            if "total" not in self.made:
                self.made["total"] = lax.psum(self.scattered(), "layer").astype(F32)
            return self.made["total"]
        (mine,), (other,) = self.sum_all(), self.back()
        if not self.by_halves:
            return jnp.where((self.place == 1) | (self.place == 2), mine, other).astype(F32)
        even = self.place & 1 == 0
        halves = [jnp.where(even, mine, other), jnp.where(even, other, mine)]
        return jnp.concatenate(halves, axis=0).astype(F32)


NAT = 208
TILE = 256
CHUNK = 48
SPARE_VMEM = 6 * 2**20
COST_TEACHER = 1
HEAVY = 2.5e9
ROW = pl.BlockSpec(memory_space=pltpu.VMEM)
FAR = pl.BlockSpec(memory_space=pl.ANY)
NUMBERS = pl.BlockSpec(memory_space=pltpu.SMEM)


def late(dims, dtype):
    return pltpu.HBM(dims, dtype)


def shape(dims, dtype):
    return jax.ShapeDtypeStruct(dims, dtype)


def launch(kernel, us, in_specs, out_specs, out_shape, scratch_shapes=(), grid=(), prefetch=0, after=()):
    def call(*args):
        count = len(args)

        def body(*refs):
            kernel(*refs[:count], *refs[count + len(after) :])

        held = sum(
            math.prod(ref.shape) * jnp.dtype(ref.dtype).itemsize
            for ref in scratch_shapes
            if jnp.issubdtype(ref.dtype, jnp.floating)
        )
        spec = pltpu.PrefetchScalarGridSpec(
            num_scalar_prefetch=prefetch,
            grid=grid,
            in_specs=list(in_specs) + [FAR] * len(after),
            out_specs=out_specs,
            scratch_shapes=list(scratch_shapes),
        )
        return pl.pallas_call(
            body,
            grid_spec=spec,
            out_shape=out_shape,
            compiler_params=pltpu.CompilerParams(vmem_limit_bytes=held + SPARE_VMEM),
            cost_estimate=pl.CostEstimate(flops=int(us * HEAVY), bytes_accessed=1 << 20 if us else 1, transcendentals=0),
        )(*args, *after)

    return call


def dot(left, right):
    return jnp.dot(left, right, preferred_element_type=F32)


def dot_t(left, right):
    return lax.dot_general(left, right, (((1,), (1,)), ((), ())), preferred_element_type=F32)


def t_dot(left, right):
    return lax.dot_general(left, right, (((0,), (0,)), ((), ())), preferred_element_type=F32)


def fetch(order, pieces, weight, sems, columns=None):
    rows = pieces[0].shape[0]
    copies = []
    for index, piece in enumerate(pieces):
        source = piece if columns is None else piece.at[:, columns]
        at = pl.multiple_of(order[index] * rows, 16 if rows % 16 == 0 else 8)
        copies.append(pltpu.make_async_copy(source, weight.at[pl.ds(at, rows)], sems.at[index]))
    for copy in copies:
        copy.start()
    return copies


def wait_all(copies):
    for copy in copies:
        copy.wait()


def one_hot(masked, count, rows):
    patch = lax.broadcasted_iota(jnp.int32, (rows, MOST), 0)
    slot = lax.broadcasted_iota(jnp.int32, (rows, MOST), 1)
    return jnp.where((masked[:, :MOST] == patch) & (slot < count), 1.0, 0.0)


def normed_with(values):
    mean = jnp.mean(values, axis=-1, keepdims=True)
    centered = values - mean
    inv_std = lax.rsqrt(jnp.mean(centered * centered, axis=-1, keepdims=True) + NORM_EPSILON)
    lane = lax.broadcasted_iota(jnp.int32, (1, 128), 1)
    return centered * inv_std, jnp.where(lane == 0, mean, inv_std)


def normed(values):
    centered = values - jnp.mean(values, axis=-1, keepdims=True)
    inv_std = lax.rsqrt(jnp.mean(centered * centered, axis=-1, keepdims=True) + NORM_EPSILON)
    return centered * inv_std, inv_std


def norm_in(grad_in, hat, inv_std, gain):
    scaled = grad_in * gain
    return inv_std * (
        scaled
        - jnp.mean(scaled, axis=-1, keepdims=True)
        - hat * jnp.mean(scaled * hat, axis=-1, keepdims=True)
    )


def wide(column):
    return jnp.broadcast_to(column, (column.shape[0], 128))


def folded(values):
    return jnp.sum(values.reshape(-1, 8, values.shape[-1]), axis=0)


def total_row(values):
    return jnp.sum(values, axis=0, keepdims=True)


def split_store(outs, columns, grad):
    rows = outs[0].shape[1]
    low = grad.astype(LOW)
    at = 0
    for out in outs:
        for index in range(out.shape[0]):
            out[index, :, columns] = low[at : at + rows]
            at += rows


def split_shapes(blocks, columns, counts=(2, 3, 3)):
    if blocks == 1:
        counts = (1,)
    return [shape((count, D // blocks, columns), LOW) for count in counts]


def teacher_kernel(counts, teacher, masked, out):
    for index in range(teacher.shape[0]):
        pick = one_hot(masked[index], counts[index], P_SIZE).astype(LOW)
        rows = slice(index * MOST, (index + 1) * MOST)
        for at in range(0, D, TILE):
            low = teacher[index, :, at : at + TILE]
            values = low.astype(F32)
            mean = jnp.sum(values, axis=0, keepdims=True) * (1.0 / P_SIZE)
            centered = values - mean
            square = jnp.sum(centered * centered, axis=0, keepdims=True) * (1.0 / P_SIZE)
            inv = lax.rsqrt(square + INSTANCE_EPSILON)
            out[rows, at : at + TILE] = ((t_dot(pick, low) - mean) * inv).astype(LOW)


def teacher_rows(teacher, masks, block, after=()):
    images = masks.shape[0]
    return launch(
        teacher_kernel,
        COST_TEACHER,
        in_specs=[NUMBERS, ROW, ROW],
        out_specs=ROW,
        out_shape=shape((images * MOST, D), LOW),
        after=after,
    )(masks[:, P_SIZE], lax.dynamic_slice_in_dim(teacher, block * images, images), masks[:, None, :P_SIZE])


def far_kernel(mine, other, first, second):
    total = (mine[...].astype(F32) + other[...].astype(F32)).astype(LOW)
    half = first.shape[1]
    first[...] = total[:, :half]
    second[...] = total[:, half:]


def far_sums(mine, other, after=()):
    rows = mine.shape[0]
    return launch(
        far_kernel,
        1,
        in_specs=[ROW] * 2,
        out_specs=[ROW] * 2,
        out_shape=[shape((rows, D // 2), LOW)] * 2,
        after=after,
    )(mine, other)


def part_kernel(spans, *refs):
    ins, out = refs[: len(spans)], refs[-1]
    at = 0
    for (source, start, size, *room), ref in zip(spans, ins):
        out[:, at : at + size] = ref[:, start : start + size].astype(LOW)
        at += size
        if room:
            out[:, at : at + room[0] - size] = jnp.zeros((out.shape[0], room[0] - size), LOW)
            at += room[0] - size


def part(spans, after=()):
    rows = spans[0][0].shape[0]
    return launch(
        functools.partial(part_kernel, spans),
        0.2,
        in_specs=[ROW] * len(spans),
        out_specs=ROW,
        out_shape=shape((rows, sum(span[-1] for span in spans)), LOW),
        after=after,
    )(*[span[0] for span in spans])


def embed_kernel(owners, order, counts, pixels, masked, *refs):
    pieces, refs = refs[:owners], refs[owners:]
    hat, inv, rows_in, position, vectors, hat_tab, inv_tab, tab_in, weight, sems = refs
    step = pl.program_id(0)

    @pl.when(step == 0)
    def _():
        wait_all(fetch(order, pieces, weight, sems, pl.ds(0, D + TAIL)))
        small = weight[:, D:].astype(F32).T
        vectors[...] = small[P_SIZE : P_SIZE + vectors.shape[0]]
        rows = small[:P_SIZE]
        zeros = jnp.zeros((NAT - P_SIZE, D), F32)
        position[...] = jnp.concatenate([rows, zeros], axis=0).astype(LOW)
        table, table_inv = normed(rows + small[P_SIZE + 14 : P_SIZE + 15])
        hat_tab[...] = jnp.concatenate([table, zeros], axis=0)
        inv_tab[...] = jnp.concatenate([wide(table_inv), zeros[:, :128]], axis=0)
        table = table * small[P_SIZE : P_SIZE + 1] + small[P_SIZE + 1 : P_SIZE + 2]
        tab_in[...] = jnp.concatenate([table, zeros], axis=0).astype(LOW)

    flag = jnp.sum(one_hot(masked[0], counts[step], P_SIZE), axis=1, keepdims=True)
    embedded = dot(pixels[0], weight[:, :D]) + vectors[13:14]
    start = flag * vectors[14:15] + (1.0 - flag) * embedded + position[...].astype(F32)[:P_SIZE]
    value, value_inv = normed(start)
    zeros = jnp.zeros((NAT - P_SIZE, D), F32)
    hat[0] = jnp.concatenate([value, zeros], axis=0)
    inv[0] = jnp.concatenate([wide(value_inv), zeros[:, :128]], axis=0)
    value = value * vectors[0:1] + vectors[1:2]
    rows_in[0] = jnp.concatenate([value, zeros], axis=0).astype(LOW)


def embed(order, counts, pixels, masked, pieces, after=()):
    images, owners = pixels.shape[0], len(pieces)
    whole = lambda *dims: pl.BlockSpec(dims, lambda i, order, counts: (0,) * len(dims))
    image = lambda *dims: pl.BlockSpec((1, *dims), lambda i, order, counts: (i,) + (0,) * len(dims))
    return launch(
        functools.partial(embed_kernel, owners),
        1,
        prefetch=2,
        grid=(images,),
        in_specs=[image(P_SIZE, PIX), image(1, P_SIZE)] + [FAR] * owners,
        out_specs=[
            image(NAT, D),
            image(NAT, 128),
            image(NAT, D),
            whole(NAT, D),
            whole(24, D),
            whole(NAT, D),
            whole(NAT, 128),
            whole(NAT, D),
        ],
        scratch_shapes=[pltpu.VMEM((D, D + TAIL), LOW), pltpu.SemaphoreType.DMA((owners,))],
        out_shape=[
            late((images, NAT, D), F32),
            late((images, NAT, 128), F32),
            shape((images, NAT, D), LOW),
            shape((NAT, D), LOW),
            shape((24, D), F32),
            late((NAT, D), F32),
            late((NAT, 128), F32),
            shape((NAT, D), LOW),
        ],
        after=after,
    )(order, counts, pixels, masked, *pieces)


def halves(pair):
    lane = lax.broadcasted_iota(jnp.int32, (1, 128), 1)
    first = jnp.where(lane < HD, 1.0, 0.0).astype(LOW)
    return jnp.concatenate([pair * first, pair * (1.0 - first.astype(F32)).astype(LOW)], axis=0)


def merged(both):
    lane = lax.broadcasted_iota(jnp.int32, (MOST, 128), 1)
    return jnp.where(lane < HD, both[:MOST], both[MOST:])


def attention_kernel(owners, order, counts, rows_in, masked, tab_in, vectors, *refs):
    pieces, refs = refs[:owners], refs[owners:]
    kv, queries, heads, weight, table, sems = refs
    step = pl.program_id(0)

    @pl.when(step == 0)
    def _():
        wait_all(fetch(order, pieces, weight, sems, pl.ds(D + TAIL, 3 * D)))
        table[...] = (dot(tab_in[...], weight[:, :D]) + vectors[2:3]).astype(LOW)

    kv[0, :, :D] = dot(rows_in[0], weight[:, D : 2 * D]).astype(LOW)
    kv[0, :, D:] = (dot(rows_in[0], weight[:, 2 * D :]) + vectors[3:4]).astype(LOW)
    pick = one_hot(masked[0], counts[step], NAT).astype(LOW)
    queries[0] = t_dot(pick, table[...]).astype(LOW)
    key_index = lax.broadcasted_iota(jnp.int32, (1, NAT), 1)
    for at in range(0, D, 128):
        pair = halves(queries[0, :, at : at + 128]) * jnp.asarray(1.0 / math.sqrt(HD), LOW)
        scores = dot_t(pair, kv[0, :, at : at + 128])
        scores = jnp.where(key_index < P_SIZE, scores, -1e30)
        shifted = jnp.exp(scores - jnp.max(scores, axis=1, keepdims=True))
        probs = (shifted * (1.0 / jnp.sum(shifted, axis=1, keepdims=True))).astype(LOW)
        heads[0, :, at : at + 128] = merged(dot(probs, kv[0, :, D + at : D + at + 128])).astype(LOW)


def attention(order, counts, rows_in, masked, tab_in, vectors, pieces, after=()):
    images, owners = rows_in.shape[0], len(pieces)
    whole = lambda *dims: pl.BlockSpec(dims, lambda i, order, counts: (0,) * len(dims))
    image = lambda *dims: pl.BlockSpec((1, *dims), lambda i, order, counts: (i,) + (0,) * len(dims))
    return launch(
        functools.partial(attention_kernel, owners),
        12,
        prefetch=2,
        grid=(images,),
        in_specs=[image(NAT, D), image(1, P_SIZE), whole(NAT, D), whole(24, D)] + [FAR] * owners,
        out_specs=[image(NAT, 2 * D), image(MOST, D), image(MOST, D), whole(D, 3 * D)],
        scratch_shapes=[
            pltpu.VMEM((NAT, D), LOW),
            pltpu.SemaphoreType.DMA((owners,)),
        ],
        out_shape=[late((images, NAT, 2 * D), LOW), late((images, MOST, D), LOW), shape((images, MOST, D), LOW), late((D, 3 * D), LOW)],
        after=after,
    )(order, counts, rows_in, masked, tab_in, vectors, *pieces)


def chunks(count, body):
    lax.fori_loop(0, count, lambda k, _: (body(k), 0)[1], 0, unroll=3)


def at_chunk(k, rows=CHUNK):
    return pl.ds(pl.multiple_of(k * rows, 16), rows)


def gelu_parts(value):
    size = jnp.abs(value) * math.sqrt(0.5)
    t = 1.0 / (1.0 + 0.3275911 * size)
    bell = jnp.exp(-size * size)
    poly = t * (0.254829592 + t * (-0.284496736 + t * (1.421413741 + t * (-1.453152027 + t * 1.061405429))))
    below = 0.5 * poly * bell
    share = jnp.where(value < 0, below, 1.0 - below)
    return value * share, share + value * bell * (1.0 / math.sqrt(2.0 * math.pi))


def mid_kernel(owners, images, order, counts, masked, heads, position, vectors, *refs):
    pieces, refs = refs[:owners], refs[owners:]
    attn, hidden, stats, rows_in, weight, sems, up_sems = refs
    copies = fetch(order, pieces, weight.at[:, pl.ds(0, D)], sems, pl.ds(0, D))
    up_copies = fetch(order, pieces, weight.at[:, pl.ds(D, FF)], up_sems, pl.ds(D, FF))
    for index in range(images):
        pick = one_hot(masked[index], counts[index], NAT).astype(LOW)
        hidden[index * MOST : (index + 1) * MOST] = t_dot(pick, position[...]) + vectors[14:15]
    wait_all(copies)
    for at in range(0, D, TILE):
        attn[:, at : at + TILE] = dot(heads[...], weight[:, at : at + TILE])

    def first(k):
        rows = at_chunk(k)
        branch = attn[rows] + vectors[4:5]
        attn[rows] = branch
        value = hidden[rows] + vectors[5:6] * branch
        hidden[rows] = value
        value, stats[rows] = normed_with(value)
        rows_in[rows] = (value * vectors[6:7] + vectors[7:8]).astype(LOW)

    chunks(hidden.shape[0] // CHUNK, first)
    wait_all(up_copies)


def mid(order, counts, masked, heads, position, vectors, pieces, after=()):
    rows, owners = heads.shape[0], len(pieces)
    return launch(
        functools.partial(mid_kernel, owners, masked.shape[0]),
        6,
        in_specs=[NUMBERS, NUMBERS] + [ROW] * 4 + [FAR] * owners,
        out_specs=[ROW] * 5,
        out_shape=[
            shape((rows, D), F32),
            shape((rows, D), F32),
            shape((rows, 128), F32),
            shape((rows, D), LOW),
            shape((D, D + FF), LOW),
        ],
        scratch_shapes=[pltpu.SemaphoreType.DMA((owners,))] * 2,
        after=after,
    )(order, counts, masked, heads, position, vectors, *pieces)


def up_kernel(first, rows_in, vectors, weight, active, slope, pre_a, pre_b):
    def product(tile, into):
        into[...] = dot(rows_in[...], weight[:, pl.ds(pl.multiple_of(D + first + tile * TILE, TILE), TILE)])

    def finish(tile, source):
        columns = pl.ds(pl.multiple_of(tile * TILE, TILE), TILE)
        part = D // TILE
        row = 15 + first // D + tile // part
        bias = vectors[pl.ds(row, 1), pl.ds(pl.multiple_of((tile % part) * TILE, TILE), TILE)]
        for start in range(0, source.shape[0], 48):
            value, down = gelu_parts(source[start : start + 48] + bias)
            active[start : start + 48, columns] = value.astype(LOW)
            slope[start : start + 48, columns] = down.astype(LOW)

    tiles = active.shape[1] // TILE
    product(0, pre_a)

    def pair(k):
        product(2 * k + 1, pre_b)
        finish(2 * k, pre_a)
        product(jnp.minimum(2 * k + 2, tiles - 1), pre_a)
        finish(2 * k + 1, pre_b)

    chunks(tiles // 2, pair)


def up(first, columns, rows_in, vectors, weight, after=()):
    rows = rows_in.shape[0]
    return launch(
        functools.partial(up_kernel, first),
        7,
        in_specs=[ROW] * 3,
        out_specs=[ROW] * 2,
        out_shape=[shape((rows, columns), LOW)] * 2,
        scratch_shapes=[
            pltpu.VMEM((rows, TILE), F32),
            pltpu.VMEM((rows, TILE), F32),
        ],
        after=after,
    )(rows_in, vectors, weight)


def place(order, source, turned, scratch):
    blocks = order.shape[0]
    if blocks == 1:
        turned[...] = source.T
        return
    rows = D // blocks
    scratch[...] = source.T
    for index in range(blocks):
        at = pl.multiple_of(order[index] * rows, 16 if rows % 16 == 0 else 8)
        turned[index * rows : (index + 1) * rows] = scratch[pl.ds(at, rows)]


def head_kernel(owners, order, active_a, active_b, hidden, vectors, *refs):
    pieces, refs = refs[:owners], refs[owners:]
    branch, stats, rows_in, work, weight, sems, head_sems = refs
    copies = fetch(order, pieces, weight.at[:, pl.ds(0, FF)], sems, pl.ds(0, FF))
    head_copies = fetch(order, pieces, weight.at[:, pl.ds(FF, D)], head_sems, pl.ds(FF, D))
    wait_all(copies)
    half = active_a.shape[1]
    for at in range(0, D, TILE):
        rows = slice(at, at + TILE)
        value = dot_t(active_a[...], weight[rows, :half])
        branch[:, rows] = value + dot_t(active_b[...], weight[rows, half:FF])

    def first(k):
        rows = at_chunk(k)
        value = branch[rows] + vectors[8:9]
        branch[rows] = value
        value, stats[rows] = normed_with(hidden[rows] + vectors[9:10] * value)
        rows_in[rows] = (value * vectors[10:11] + vectors[11:12]).astype(LOW)

    chunks(hidden.shape[0] // CHUNK, first)
    wait_all(head_copies)
    for at in range(0, D, TILE):
        work[:, at : at + TILE] = dot(rows_in[...], weight[:, FF + at : FF + at + TILE])


def head(order, active, hidden, vectors, pieces, after=()):
    rows, owners = hidden.shape[0], len(pieces)
    return launch(
        functools.partial(head_kernel, owners),
        10,
        in_specs=[NUMBERS] + [ROW] * 4 + [FAR] * owners,
        out_specs=[ROW] * 5,
        out_shape=[
            shape((rows, D), F32),
            shape((rows, 128), F32),
            shape((rows, D), LOW),
            shape((rows, D), F32),
            shape((D, FF + D), LOW),
        ],
        scratch_shapes=[pltpu.SemaphoreType.DMA((owners,))] * 2,
        after=after,
    )(order, *active, hidden, vectors, *pieces)


def down_kernel(parts, order, counts, work, stats, hidden, branch, active_a, active_b, vectors, rows_in, weight, *refs):
    targets, refs = refs[:parts], refs[parts:]
    outs = 3 if order.shape[0] > 1 else 1
    grads = refs[:outs]
    loss, head_sums, grad, grad_low, sums, error_low, turned, spare = refs[outs:]
    head_sums[...] = jnp.zeros_like(head_sums)
    sums[...] = jnp.zeros_like(sums)
    steps = grad.shape[0] // CHUNK

    def errors(k):
        rows = at_chunk(k)
        target = targets[0][rows].astype(F32)
        if len(targets) > 1:
            near, first, second = [other[rows].astype(F32) for other in targets[1:]]
            target = target + near + jnp.concatenate([first, second], axis=1)
        error = work[rows] + vectors[12:13] - target * (1.0 / lax.axis_size("layer"))
        size = jnp.abs(error)
        entry = jnp.where(size < HUBER_BETA, error * error * (0.5 / HUBER_BETA), size - 0.5 * HUBER_BETA)
        per_image = MOST // CHUNK
        row = lax.broadcasted_iota(jnp.int32, (CHUNK, 1), 0) + lax.rem(k, per_image) * CHUNK
        flag = row < counts[k // per_image]
        head_sums[0] += folded(jnp.where(flag, entry, 0.0))
        value = jnp.where(flag, jnp.clip(error * (1.0 / HUBER_BETA), -1.0, 1.0), 0.0)
        head_sums[1] += folded(value)
        error_low[rows] = value.astype(LOW)

    chunks(steps, errors)
    loss[0, 0] = jnp.sum(head_sums[0])
    for at in range(0, D, TILE):
        grad[:, at : at + TILE] = dot_t(error_low[...], weight[at : at + TILE, FF:])

    def back(k):
        rows = at_chunk(k)
        grad_in, branch_rows = grad[rows], branch[rows]
        block = hidden[rows] + vectors[9:10] * branch_rows
        value = (block - stats[rows, :1]) * stats[rows, 1:2]
        sums[0] += folded(grad_in * value)
        sums[1] += folded(grad_in)
        value = norm_in(grad_in, value, stats[rows, 1:2], vectors[10:11])
        grad[rows] = value
        sums[2] += folded(value * branch_rows)
        value = value * vectors[9:10]
        sums[3] += folded(value)
        grad_low[rows] = value.astype(LOW)

    chunks(steps, back)
    place(order, grad_low[...], turned, spare)
    half = active_a.shape[1]
    for at in range(0, FF, TILE):
        source = active_a[:, at : at + TILE] if at < half else active_b[:, at - half : at - half + TILE]
        split_store(grads, slice(at, at + TILE), dot(turned[...], source))
    place(order, rows_in[...], turned, spare)
    for at in range(0, D, TILE):
        columns = slice(FF + at, FF + at + TILE)
        split_store(grads, columns, dot(turned[...], error_low[:, at : at + TILE]))


def down(order, counts, work, stats, hidden, branch, active, vectors, rows_in, targets, weight, after=()):
    rows = hidden.shape[0]
    grads = split_shapes(order.shape[0], FF + D)
    return launch(
        functools.partial(down_kernel, len(targets)),
        15,
        in_specs=[NUMBERS, NUMBERS] + [ROW] * (9 + len(targets)),
        out_specs=[ROW] * len(grads) + [NUMBERS] + [ROW] * 4,
        out_shape=grads
        + [
            shape((1, 1), F32),
            shape((2, 8, D), F32),
            shape((rows, D), F32),
            shape((rows, D), LOW),
            shape((4, 8, D), F32),
        ],
        scratch_shapes=[
            pltpu.VMEM((rows, D), LOW),
            pltpu.VMEM((D, rows), LOW),
            pltpu.VMEM((D, rows), LOW),
        ],
        after=after,
    )(order, counts, work, stats, hidden, branch, *active, vectors, rows_in, weight, *targets)


def pre_kernel(order, grad_low, slope_a, slope_b, rows_in, weight, *refs):
    outs = 3 if order.shape[0] > 1 else 1
    grads = refs[:outs]
    pre_low, bias, turned, spare = refs[outs:]
    place(order, rows_in[...], turned, spare)

    half = slope_a.shape[1]
    for at in range(0, FF, TILE):
        columns = slice(at, at + TILE)
        slope, start = (slope_a, at) if at < half else (slope_b, at - half)
        value = dot(grad_low[...], weight[:, columns]) * slope[:, start : start + TILE].astype(F32)
        bias[:, columns] = folded(value)
        pre_low[:, columns] = value.astype(LOW)
        split_store(grads, columns, dot(turned[...], pre_low[:, columns]))


def pre(order, grad_low, slope, rows_in, weight, after=()):
    rows = grad_low.shape[0]
    grads = split_shapes(order.shape[0], FF)
    return launch(
        pre_kernel,
        12,
        in_specs=[NUMBERS] + [ROW] * 5,
        out_specs=[ROW] * (len(grads) + 2),
        out_shape=grads + [shape((rows, FF), LOW), shape((8, FF), F32)],
        scratch_shapes=[
            pltpu.VMEM((D, rows), LOW),
            pltpu.VMEM((D, rows), LOW),
        ],
        after=after,
    )(order, grad_low, *slope, rows_in, weight)


def out_kernel(images, counts, masked, pre_low, grad, stats, hidden, attn, vectors, weight, *refs):
    heads_grad, table, sums, attn_low, work, high, rest = refs
    for at in range(0, D, TILE):
        work[:, at : at + TILE] = dot_t(pre_low[...], weight[at : at + TILE, D:])
    sums[...] = jnp.zeros_like(sums)

    def back(k):
        rows = at_chunk(k)
        grad_in = work[rows]
        value = (hidden[rows] - stats[rows, :1]) * stats[rows, 1:2]
        sums[0] += folded(grad_in * value)
        sums[1] += folded(grad_in)
        value = grad[rows] + norm_in(grad_in, value, stats[rows, 1:2], vectors[6:7])
        low = value.astype(LOW)
        high[rows] = low
        rest[rows] = (value - low.astype(F32)).astype(LOW)
        sums[2] += folded(value * attn[rows])
        value = value * vectors[5:6]
        sums[3] += folded(value)
        attn_low[rows] = value.astype(LOW)

    chunks(work.shape[0] // CHUNK, back)
    for at in range(0, D, TILE):
        heads_grad[:, at : at + TILE] = dot_t(attn_low[...], weight[at : at + TILE, :D]).astype(LOW)
    for index in range(images):
        pick = one_hot(masked[index], counts[index], NAT).astype(LOW)
        rows = slice(index * MOST, (index + 1) * MOST)
        value = dot(pick, high[rows]) + dot(pick, rest[rows])
        table[...] = value if index == 0 else table[...] + value


def out_back(counts, masked, pre_low, grad, stats, hidden, attn, vectors, weight, after=()):
    rows = grad.shape[0]
    return launch(
        functools.partial(out_kernel, masked.shape[0]),
        14,
        in_specs=[NUMBERS] + [ROW] * 8,
        out_specs=[ROW] * 4,
        out_shape=[shape((rows, D), LOW), shape((NAT, D), F32), shape((4, 8, D), F32), shape((rows, D), LOW)],
        scratch_shapes=[
            pltpu.VMEM((rows, D), F32),
            pltpu.VMEM((rows, D), LOW),
            pltpu.VMEM((rows, D), LOW),
        ],
        after=after,
    )(counts, masked, pre_low, grad, stats, hidden, attn, vectors, weight)


def attention_back_kernel(counts, queries, kv, heads_grad, masked, kv_low, table, sums, query_low):
    step = pl.program_id(0)

    @pl.when(step == 0)
    def _():
        table[...] = jnp.zeros_like(table)
        sums[...] = jnp.zeros_like(sums)

    scale = 1.0 / math.sqrt(HD)
    key_index = lax.broadcasted_iota(jnp.int32, (NAT, 1), 0)
    for at in range(0, D, 128):
        lanes = slice(at, at + 128)
        high = slice(D + at, D + at + 128)
        pair = halves(queries[0, :, lanes]) * jnp.asarray(scale, LOW)
        grad = halves(heads_grad[0, :, lanes])
        keys, values = kv[0, :, lanes], kv[0, :, high]
        scores = jnp.where(key_index < P_SIZE, dot_t(keys, pair), -1e30)
        shifted = jnp.exp(scores - jnp.max(scores, axis=0, keepdims=True))
        probs = shifted * (1.0 / jnp.sum(shifted, axis=0, keepdims=True))
        prob_grad = dot_t(values, grad)
        value_grad = dot(probs.astype(LOW), grad).astype(LOW)
        kv_low[0, :, high] = value_grad
        sums[1, :, lanes] += folded(value_grad.astype(F32))
        inner = jnp.sum(probs * prob_grad, axis=0, keepdims=True)
        score_grad = (probs * (prob_grad - inner)).astype(LOW)
        kv_low[0, :, lanes] = dot(score_grad, pair).astype(LOW)
        query_grad = merged(t_dot(score_grad, keys) * scale).astype(LOW)
        query_low[:, lanes] = query_grad
        sums[0, :, lanes] += folded(query_grad.astype(F32))
    pick = one_hot(masked[0], counts[step], NAT).astype(LOW)
    table[...] += dot(pick, query_low[...])


def attention_back(counts, queries, kv, heads_grad, masked, after=()):
    images = kv.shape[0]
    whole = lambda *dims: pl.BlockSpec(dims, lambda i, counts: (0,) * len(dims))
    image = lambda *dims: pl.BlockSpec((1, *dims), lambda i, counts: (i,) + (0,) * len(dims))
    return launch(
        attention_back_kernel,
        15,
        prefetch=1,
        grid=(images,),
        in_specs=[image(MOST, D), image(NAT, 2 * D), image(MOST, D), image(1, P_SIZE)],
        out_specs=[image(NAT, 2 * D), whole(NAT, D), whole(2, 8, D)],
        scratch_shapes=[pltpu.VMEM((MOST, D), LOW)],
        out_shape=[shape((images, NAT, 2 * D), LOW), shape((NAT, D), F32), shape((2, 8, D), F32)],
        after=after,
    )(counts, queries, kv, heads_grad, masked)


def high_rest(value):
    high = value.astype(LOW)
    return jnp.concatenate([high, (value - high.astype(F32)).astype(LOW)], axis=0)


def qkv_kernel(blocks, order, rows_in, kv_low, tab_in, table, heads, attn_low, *refs):
    outs = 3 if blocks > 1 else 1
    grads = refs[:outs]
    turned, spare, tab_turned, tab_spare, heads_turned, heads_spare = refs[outs:]
    place(order, heads[...], heads_turned, heads_spare)
    for at in range(0, D, TILE):
        columns = slice(3 * D + at, 3 * D + at + TILE)
        split_store(grads, columns, dot(heads_turned[...], attn_low[:, at : at + TILE]))
    place(order, tab_in[...], tab_turned, tab_spare)
    both = high_rest(table[...])
    twice = jnp.concatenate([tab_turned[...], tab_turned[...]], axis=1)
    for at in range(0, D, TILE):
        split_store(grads, slice(at, at + TILE), dot(twice, both[:, at : at + TILE]))
    place(order, rows_in[...], turned, spare)

    for at in range(0, 2 * D, TILE):
        split_store(grads, slice(D + at, D + at + TILE), dot(turned[...], kv_low[:, at : at + TILE]))


def qkv_back(order, rows_in, kv_low, tab_in, table, heads, attn_low, after=()):
    blocks, rows = order.shape[0], rows_in.shape[0]
    grads = split_shapes(blocks, 4 * D)
    return launch(
        functools.partial(qkv_kernel, blocks),
        7,
        in_specs=[NUMBERS] + [ROW] * 6,
        out_specs=[ROW] * len(grads),
        out_shape=grads,
        scratch_shapes=[
            pltpu.VMEM((D, rows), LOW),
            pltpu.VMEM((D, rows), LOW),
            pltpu.VMEM((D, NAT), LOW),
            pltpu.VMEM((D, NAT), LOW),
            pltpu.VMEM((D, heads.shape[0]), LOW),
            pltpu.VMEM((D, heads.shape[0]), LOW),
        ],
        after=after,
    )(order, rows_in, kv_low, tab_in, table, heads, attn_low)


def start_kernel(images, counts, masked, kv_low, table, hidden_tab, hat, inv, hat_tab, inv_tab, vectors, head_sums, down_sums, up_bias, out_sums, qkv_sums, weight, *refs):
    start_low, small_low, work, small, sums = refs
    for at in range(0, D, TILE):
        work[:, at : at + TILE] = dot_t(kv_low[...], weight[at : at + TILE, D:])
    both = high_rest(table[...])
    tab_in = dot_t(both, weight[:, :D])
    tab_in = tab_in[:NAT] + tab_in[NAT:]
    gain = vectors[0:1]
    sums[...] = jnp.zeros_like(sums)
    sums[0] += folded(tab_in * hat_tab[...])
    sums[1] += folded(tab_in)
    tab_grad = norm_in(tab_in, hat_tab[...], inv_tab[:, :1], gain) + hidden_tab[...]
    sums[2] += folded(tab_grad)
    small[:NAT] = tab_grad
    half = NAT // 2
    for index in range(images):
        flags = jnp.sum(one_hot(masked[index], counts[index], NAT), axis=1, keepdims=True)
        for part in range(2):
            rows = slice(index * NAT + part * half, index * NAT + (part + 1) * half)
            flag = flags[part * half : (part + 1) * half]
            grad_in, value = work[rows], hat[rows]
            sums[0] += folded(grad_in * value)
            sums[1] += folded(grad_in)
            value = norm_in(grad_in, value, inv[rows, :1], gain)
            small[part * half : (part + 1) * half] += value
            sums[2] += folded(value * flag)
            value = value * (1.0 - flag)
            sums[3] += folded(value)
            start_low[rows] = value.astype(LOW)
    line = [
        total_row(sums[0]),
        total_row(sums[1]),
        total_row(qkv_sums[0]),
        total_row(qkv_sums[1]),
        total_row(out_sums[3]),
        total_row(out_sums[2]),
        total_row(out_sums[0]),
        total_row(out_sums[1]),
        total_row(down_sums[3]),
        total_row(down_sums[2]),
        total_row(down_sums[0]),
        total_row(down_sums[1]),
        total_row(head_sums[1]),
        total_row(sums[3]),
        total_row(sums[2]),
    ]
    line += [total_row(up_bias[:, at : at + D]) for at in range(0, FF, D)]
    for index, value in enumerate(line):
        small[P_SIZE + index : P_SIZE + index + 1] = value
    small[P_SIZE + len(line) :] = jnp.zeros((TAIL - P_SIZE - len(line), D), F32)
    small_low[...] = small[...].T


def start_back(counts, masked, kv_low, table, hidden_tab, hat, inv, hat_tab, inv_tab, vectors, head_sums, down_sums, up_bias, out_sums, qkv_sums, weight, after=()):
    rows, images = kv_low.shape[0], masked.shape[0]
    return launch(
        functools.partial(start_kernel, images),
        8,
        in_specs=[NUMBERS] + [ROW] * 15,
        out_specs=[ROW] * 2,
        out_shape=[shape((rows, D), LOW), shape((D, TAIL), F32)],
        scratch_shapes=[
            pltpu.VMEM((rows, D), F32),
            pltpu.VMEM((TAIL, D), F32),
            pltpu.VMEM((4, 8, D), F32),
        ],
        after=after,
    )(counts, masked, kv_low, table, hidden_tab, hat, inv, hat_tab, inv_tab, vectors, head_sums, down_sums, up_bias, out_sums, qkv_sums, weight)


def embed_back_kernel(images, blocks, order, pixels, start_low, small_low, *refs):
    outs = 2 if blocks > 1 else 1
    grads = refs[:outs]
    turned, spare, pixel_rows = refs[outs:]
    for index in range(images):
        zeros = jnp.zeros((NAT - P_SIZE, PIX), F32)
        padded = jnp.concatenate([pixels[index].astype(F32), zeros], axis=0)
        pixel_rows[index * NAT : (index + 1) * NAT] = padded.astype(LOW)
    place(order, pixel_rows[...], turned, spare)
    rows = D // order.shape[0]
    block = 0
    for out in grads:
        for index in range(out.shape[0]):
            at = pl.multiple_of(order[block] * rows, 16 if rows % 16 == 0 else 8)
            out[index, :, D:] = small_low[pl.ds(at, rows)].astype(LOW)
            block += 1
    for at in range(0, D, TILE):
        split_store(grads, slice(at, at + TILE), dot(turned[...], start_low[:, at : at + TILE]))


def embed_back(order, pixels, start_low, small_low, after=()):
    rows, blocks = start_low.shape[0], order.shape[0]
    grads = split_shapes(blocks, D + TAIL, (4, 4))
    return launch(
        functools.partial(embed_back_kernel, pixels.shape[0], blocks),
        0.1,
        in_specs=[NUMBERS] + [ROW] * 3,
        out_specs=[ROW] * len(grads),
        out_shape=grads,
        scratch_shapes=[
            pltpu.VMEM((D, rows), LOW),
            pltpu.VMEM((D, rows), LOW),
            pltpu.VMEM((rows, D), LOW),
        ],
        after=after,
    )(order, pixels, start_low, small_low)


def add_kernel(plan, *refs):
    ins, outs = refs[: len(refs) - len(plan)], refs[len(refs) - len(plan) :]
    for segments, out in zip(plan, outs):
        at = 0
        for terms in segments:
            total = None
            for source, block in terms:
                value = (ins[source][...] if block is None else ins[source][block]).astype(F32)
                total = value if total is None else total + value
            out[:, at : at + total.shape[1]] = total.astype(out.dtype)
            at += total.shape[1]


def add(arrays, plan, types, after=(), us=0):
    rows = arrays[0].shape[-2]
    widths = [sum(arrays[terms[0][0]].shape[-1] for terms in segments) for segments in plan]
    return launch(
        functools.partial(add_kernel, plan),
        us,
        in_specs=[ROW] * len(arrays),
        out_specs=[ROW] * len(plan),
        out_shape=[shape((rows, width), kind) for width, kind in zip(widths, types)],
        after=after,
    )(*arrays)


def copy_kernel(source, out):
    out[...] = source[...]


def copied(array, after):
    return launch(
        copy_kernel, 1, in_specs=[ROW], out_specs=ROW, out_shape=shape(array.shape, array.dtype), after=after
    )(array)


def pair_kernel(first, second, out):
    out[...] = (first[...].astype(F32) + second[...].astype(F32)).astype(LOW)


def pair_sums(first, second, after=()):
    return launch(
        pair_kernel, 0, in_specs=[ROW] * 2, out_specs=ROW, out_shape=shape(first.shape, LOW), after=after
    )(first, second)


def share_kernel(counts, half, *refs):
    terms, (keep, send, spare) = list(refs[:-3]), refs[-3:]
    at = 0
    for count, blocks in counts:
        own, *others = [terms.pop(0) for _ in range(count)]
        total = own[0].astype(F32)
        for chip in range(1, blocks):
            total = total + own[chip].astype(F32)
        for other in others:
            total = total + other[...].astype(F32)
        spare[:, at : at + total.shape[1]] = total
        at += total.shape[1]
    rows = keep.shape[0]
    kept = half[0]
    keep[...] = spare[pl.ds(pl.multiple_of(kept * rows, 8), rows)]
    send[...] = spare[pl.ds(pl.multiple_of((1 - kept) * rows, 8), rows)].astype(LOW)


def share_halves(half, parts, after=()):
    rows = parts[0][1].shape[1]
    columns = sum(part[1].shape[2] for part in parts)
    terms = [term for part in parts for term in part[1:]]
    return launch(
        functools.partial(share_kernel, [(len(part) - 1, part[0]) for part in parts]),
        0,
        in_specs=[NUMBERS] + [ROW] * len(terms),
        out_specs=[ROW] * 2,
        out_shape=[shape((rows // 2, columns), F32), shape((rows // 2, columns), LOW)],
        scratch_shapes=[pltpu.VMEM((rows, columns), F32)],
        after=after,
    )(half, *terms)


def sum_squares(parts):
    squares = jnp.zeros((1, 1), F32)
    for part in parts:
        value = part[...].astype(F32)
        squares = squares + jnp.sum(jnp.sum(value * value, axis=0, keepdims=True), axis=1, keepdims=True)
    return squares


def open_kernel(loss, counts, *refs):
    parts, out = refs[:-1], refs[-1]
    count = counts[0]
    for index in range(1, counts.shape[0]):
        count = count + counts[index]
    lane = lax.broadcasted_iota(jnp.int32, out.shape, 1)
    last = jnp.where(lane == 1, count.astype(F32), jnp.broadcast_to(sum_squares(parts), out.shape))
    out[...] = jnp.where(lane == 0, loss[0, 0], last)


def close_kernel(early, *refs):
    parts, out = refs[:-1], refs[-1]
    lane = lax.broadcasted_iota(jnp.int32, early.shape, 1)
    row = early[...] + jnp.where(lane == 2, jnp.broadcast_to(sum_squares(parts), early.shape), 0.0)
    out[...] = jnp.broadcast_to(row, out.shape)


def close(loss, counts, parts, last, size):
    early = launch(
        open_kernel,
        0,
        in_specs=[NUMBERS, NUMBERS] + [ROW] * len(parts),
        out_specs=ROW,
        out_shape=shape((1, 128), F32),
    )(loss, counts, *parts)
    return launch(
        close_kernel,
        0,
        in_specs=[ROW] * (1 + len(last)),
        out_specs=ROW,
        out_shape=shape((size, 128), F32),
    )(early, *last)


def factor_kernel(copies, rows, out):
    total = jnp.sum(rows[...], axis=0, keepdims=True)
    loss, masks, squares = total[:, :1], total[:, 1:2], total[:, 2:3] * (1.0 / copies)
    per_mask = 1.0 / masks
    norm = jnp.sqrt(squares) * per_mask
    factor = CLIP_NORM / jnp.maximum(norm, CLIP_NORM) * per_mask
    lane = lax.broadcasted_iota(jnp.int32, (1, 128), 1)
    out[...] = jnp.where(lane == 0, loss, jnp.where(lane == 1, masks, jnp.where(lane == 2, norm, factor)))


def factors(rows, copies):
    return launch(
        functools.partial(factor_kernel, copies),
        1,
        in_specs=[ROW],
        out_specs=ROW,
        out_shape=shape((1, 128), F32),
    )(rows)


def adam_update(master, first, second, grad, decay):
    first_new = FIRST_DECAY * first + (1.0 - FIRST_DECAY) * grad
    second_new = SECOND_DECAY * second + (1.0 - SECOND_DECAY) * grad * grad
    first_hat = first_new / (1.0 - FIRST_DECAY**STEP)
    second_hat = second_new / (1.0 - SECOND_DECAY**STEP)
    master_new = master - LEARN_RATE * (
        first_hat / (jnp.sqrt(second_hat) + ADAM_EPSILON) + WEIGHT_DECAY * decay * master
    )
    return (master_new, first_new, second_new)


def targets_of(teacher, masked, counts, after, twin, chips):
    layers, images = lax.axis_size("layer"), masked.shape[0]
    masks = jnp.concatenate([masked, counts[:, None]], axis=1)
    if layers != 4:
        masks = lax.all_gather(masks, "layer", axis=0, tiled=False)
        picked = [teacher_rows(teacher, masks[block], block) for block in range(layers)]
        total = lax.psum_scatter(jnp.stack(picked), "layer", scatter_dimension=0, tiled=False)
        return total, None, None, picked[0]
    at = lax.axis_index("layer")
    near, second, third = [swap(masks, "layer", bit) for bit in (1, 2, 3)]
    own_rows = teacher_rows(teacher, masks, at, after)
    far_rows = teacher_rows(teacher, third, at ^ 3, [own_rows, near, second])
    far = swap(far_rows, "layer", 1)
    second_rows = teacher_rows(teacher, second, at ^ 2, [far_rows, *twin, *chips])

    def near_sum(after):
        rows = teacher_rows(teacher, near, at ^ 1, after)
        return rows, swap(rows, "layer", 1)

    far_sum = lambda after: far_sums(second_rows, far, after)
    return own_rows, near_sum, far_sum, second_rows


def body(
    pixels,
    teacher,
    masked_at,
    mask_count,
    wide_master,
    wide_first,
    wide_second,
    tall_master,
    tall_first,
    tall_second,
):
    owners, layers = lax.axis_size("dp"), lax.axis_size("layer")
    counts, masked = mask_count[0], masked_at[0][:, None, :]
    images = counts.shape[0]
    order = blocks_of(lax.axis_index("dp")) if owners == 8 else jnp.zeros((1,), jnp.int32)
    by_chip = blocks_by_chip(lax.axis_index("dp")) if owners == 8 else order
    tall_low = tall_master.T.astype(LOW)
    wide_embed = part(
        [(wide_master, 0, D), (tall_low, FF, P_SIZE + VECS, TAIL), (wide_master, D, 3 * D)]
    )
    pieces_in = gather_part(wide_embed)
    own_rows, near_sum, far_sum, second_rows = targets_of(
        teacher[0, 0], masked_at[0], counts, [wide_embed], arrived(pieces_in, 1), arrived(pieces_in, 2)
    )
    wide_up = part([(wide_master, 4 * D, D + FF)], [own_rows] + arrived(pieces_in, 3))
    pieces_up = gather_part(wide_up)

    hat_nat, inv_nat, in_nat, position, vectors, hat_tab, inv_tab, in_tab = embed(
        order, counts, pixels[0], masked, pieces_in, after=[wide_up, second_rows]
    )
    targets, waits = [own_rows], arrived(pieces_up, 2)
    if near_sum:
        near_rows, near = near_sum([in_tab])
        far_a, far_b = far_sum([near_rows])
        waits += [far_a]
        far_a = swap(far_a, "layer", 2)
        targets += [near, far_a]
    kv, queries, heads, qkv_w = attention(
        order, counts, in_nat, masked, in_tab, vectors, pieces_in, after=waits
    )
    heads = heads.reshape(images * MOST, D)
    arrivals = targets[2:]
    if near_sum:
        targets.append(swap(far_b, "layer", 2))
    wide_down = part([(tall_low, 0, FF), (wide_master, 5 * D + FF, D)], [heads] + arrived(pieces_up, 4))
    pieces_down = gather_part(wide_down)
    attn, hidden, stats_mid, in_mid, out_up_w = mid(
        order, counts, masked, heads, position, vectors, pieces_up, after=[wide_down] + arrivals
    )
    active_a, slope_a = up(0, FF // 2, in_mid, vectors, out_up_w)
    active_b, slope_b = up(
        FF // 2, FF // 2, in_mid, vectors, out_up_w, after=[active_a] + arrived(pieces_down, 2)
    )
    active, slope = (active_a, active_b), (slope_a, slope_b)
    branch, stats_out, in_out, work, down_head_w = head(order, active, hidden, vectors, pieces_down)
    *down_g, loss, head_sums, grad, grad_low, down_sums = down(
        order, counts, work, stats_out, hidden, branch, active, vectors, in_out, targets, down_head_w
    )
    down_p = Part(down_g)
    *up_g, pre_low, up_bias = pre(order, grad_low, slope, in_mid, down_head_w)
    up_p = Part(up_g)
    down_s, up_s = Owned([down_p], False), Owned([up_p], False)
    heads_grad, hidden_tab, out_sums, attn_low = out_back(
        counts, masked, pre_low, grad, stats_mid, hidden, attn, vectors, out_up_w,
        after=down_p.sums([pre_low]),
    )
    kv_low, table, qkv_sums = attention_back(
        counts, queries, kv, heads_grad.reshape(images, MOST, D), masked,
        after=down_p.sums_out([heads_grad]) + up_p.sums([heads_grad]),
    )
    flat = lambda value: value.reshape(images * NAT, -1)
    qkv_g = qkv_back(
        order, flat(in_nat), flat(kv_low), in_tab, table, heads, attn_low,
        after=down_s.shares([table]) + up_p.sums_out([table]),
    )
    qkv_p = Part(qkv_g)
    start_low, small_low = start_back(
        counts, masked, flat(kv_low), table, hidden_tab, flat(hat_nat), flat(inv_nat),
        hat_tab, inv_tab, vectors, head_sums, down_sums, up_bias, out_sums, qkv_sums, qkv_w,
        after=up_s.shares([qkv_g[0]]),
    )
    embed_g = embed_back(
        by_chip, pixels[0], start_low, small_low, after=qkv_p.sums([start_low]) + down_s.pairs([start_low])
    )
    embed_p = Direct(embed_g)
    last_s = Owned([qkv_p, embed_p], True)
    ready = qkv_p.sums_out([embed_g[0]])
    ready = embed_p.sums(ready)
    ready = up_s.pairs(ready)
    ready = down_s.sum_all(ready)
    ready = last_s.shares(ready)
    ready = up_s.sum_all(ready)
    last_s.pairs(ready)
    squared = [array for one in (down_s, up_s, last_s) for array in one.squared()]
    down_s, up_s, last_s = down_s.total(), up_s.total(), last_s.total()
    qkv_s, embed_s = last_s[:, : 4 * D], last_s[:, 4 * D :]
    wide_share = jnp.concatenate([embed_s[:, :D], qkv_s, up_s, down_s[:, FF:]], axis=1)
    tall_share = jnp.concatenate([down_s[:, :FF], embed_s[:, D : D + P_SIZE + VECS]], axis=1)
    axes = ("layer", "dp")
    rows = close(loss, counts, squared[:-1], squared[-1:], lax.axis_size(axes))
    rows = lax.all_to_all(rows, axes, split_axis=0, concat_axis=0, tiled=True)
    loss_sum, mask_total, grad_norm, factor = factors(rows, layers)[0, :4]
    wide_new, wide_first_new, wide_second_new = adam_update(
        wide_master, wide_first, wide_second, factor * wide_share, 1.0
    )
    tall_decay = (lax.broadcasted_iota(jnp.int32, (tall_master.shape[0], 1), 0) < FF).astype(F32)
    tall_grad = factor * tall_share.T
    tall_new, tall_first_new, tall_second_new = adam_update(
        tall_master, tall_first, tall_second, tall_grad, tall_decay
    )
    return (
        loss_sum,
        mask_total,
        grad_norm,
        wide_new,
        wide_first_new,
        wide_second_new,
        wide_new.astype(LOW),
        tall_new,
        tall_first_new,
        tall_second_new,
        tall_new.astype(LOW),
        tall_grad[FF + P_SIZE + 2],
    )


def solution(mesh):
    in_specs = (
        P("dp", "layer", None, None),
        P("layer", "dp", None, None, None),
        P("dp", "layer", None),
        P("dp", "layer"),
        P("dp", None),
        P("dp", None),
        P("dp", None),
        P(None, "dp"),
        P(None, "dp"),
        P(None, "dp"),
    )
    out_specs = (
        P(),
        P(),
        P(),
        P("dp", None),
        P("dp", None),
        P("dp", None),
        P("dp", None),
        P(None, "dp"),
        P(None, "dp"),
        P(None, "dp"),
        P(None, "dp"),
        P("dp"),
    )
    return jax.shard_map(body, mesh=mesh, in_specs=in_specs, out_specs=out_specs, check_vma=False)
```
